32 devices in a mesh: fsdp: 8 (over y, x, core), ctx: 4 (over z).
Axes of the slice: x: 2, y: 2, z: 4, core: 2. Of those that a mesh axis runs over, the one named last changes fastest.
Arguments:
- tokens: bfloat16 [8, 512, 2048], P('fsdp', 'ctx'), may hold values from -6 to 6
- doc_starts: int32 [8, 4], P('fsdp'), may hold values from 0 to 511, as said below
- expert_ids: int32 [8, 512, 8], P('fsdp', 'ctx'), may hold values from 0 to 63, all different within a row; in each aligned block of 128 rows (0 to 127, 128 to 255, ..., all dimensions but the last counted through in order) at most 24 rows name the same one
- w_query: bfloat16 [2048, 2048], P(('fsdp', 'ctx')), may hold values from -0.125 to 0.125
- w_key: bfloat16 [2048, 2048], P(('fsdp', 'ctx')), may hold values from -0.125 to 0.125
- w_value: bfloat16 [2048, 2048], P(('fsdp', 'ctx')), may hold values from -0.125 to 0.125
- w_attn_out: bfloat16 [2048, 2048], P(('fsdp', 'ctx')), may hold values from -1 to 1
- w_router: bfloat16 [2048, 64], P(('fsdp', 'ctx')), may hold values from -0.0625 to 0.0625
- g_attn: bfloat16 [2048], P(('fsdp', 'ctx')), may hold values from 0.099609375 to 1.8984375
- g_query: bfloat16 [2048], P(('fsdp', 'ctx')), may hold values from 0.099609375 to 1.8984375
- g_key: bfloat16 [2048], P(('fsdp', 'ctx')), may hold values from 0.099609375 to 1.8984375
- g_ffn: bfloat16 [2048], P(('fsdp', 'ctx')), may hold values from 0.099609375 to 1.8984375
- w_in: bfloat16 [128, 2048, 1024], P(('fsdp', 'ctx')), may hold values from -0.125 to 0.125
- w_out: bfloat16 [128, 512, 2048], P(('fsdp', 'ctx')), may hold values from -6 to 6
- cotangent: bfloat16 [8, 512, 2048], P('fsdp', 'ctx'), may hold values from -6 to 6
Outputs:
- output: bfloat16 [8, 512, 2048], P('fsdp', 'ctx')
- input_grad: float32 [8, 512, 2048], P('fsdp', 'ctx')
- grad_query: float32 [2048, 2048], P(('fsdp', 'ctx'))
- grad_key: float32 [2048, 2048], P(('fsdp', 'ctx'))
- grad_value: float32 [2048, 2048], P(('fsdp', 'ctx'))
- grad_attn_out: float32 [2048, 2048], P(('fsdp', 'ctx'))
- grad_router: float32 [2048, 64], P(('fsdp', 'ctx'))
- grad_g_attn: float32 [2048], P(('fsdp', 'ctx'))
- grad_g_query: float32 [2048], P(('fsdp', 'ctx'))
- grad_g_key: float32 [2048], P(('fsdp', 'ctx'))
- grad_g_ffn: float32 [2048], P(('fsdp', 'ctx'))
- grad_w_in: float32 [128, 2048, 1024], P(('fsdp', 'ctx'))
- grad_w_out: float32 [128, 512, 2048], P(('fsdp', 'ctx'))
The draws below stay inside these ranges and needn't reach their ends.
Inputs may be any that keep to these rules, and one draw needn't show every extreme that they name: `doc_starts`: each row rises strictly from 0. `expert_ids`: each row names 8 different experts; within the rows of one device (aligned blocks of 128 positions) no expert is named more than 24 times.
All inputs are finite; a program needn't handle non-finite values.
Results may differ from the reference program's by a relative error of at most 0.03.
Values may be sent and summed in bfloat16 or wider, within the bound.
No kernel may reach another device: no remote copies, remote signals or barrier semaphores. Data moves between devices by JAX's collectives and lax.ppermute only.
A program may use at most 384 MiB of HBM per device.

```python
import math
import jax
import jax.numpy as jnp
import numpy as np
from jax import lax

D = 2048
H = 16
HD = 128
E = 64
TOP = 8
FH = 512
PIECES = 128
TOK_DEV = 128
SEQ = 512
STREAMS = 8
CAP = 24
N_CTX = 4


def draw_doc_starts(key, part):
    key_long, key_early, key_end, key_late, key_pick = jax.random.split(key, 5)
    long_start = jax.random.randint(key_long, (STREAMS,), 2, TOK_DEV)
    early_start = jax.random.randint(key_early, (STREAMS,), 1, long_start)
    long_end = jax.random.randint(key_end, (STREAMS,), SEQ - TOK_DEV + 1, SEQ - 1)
    late_start = jax.random.randint(key_late, (STREAMS,), long_end + 1, SEQ)
    pick_form = jax.random.randint(key_pick, (STREAMS,), 0, 2)
    zero_column = jnp.zeros((STREAMS,), jnp.int32)
    first_form = jnp.stack([zero_column, long_start, long_end, late_start], axis=1)
    second_form = jnp.stack([zero_column, early_start, long_start, long_end], axis=1)
    return jnp.where(pick_form[:, None] == 0, first_form, second_form).astype(jnp.int32)


def levels(key, shape, shards, low, top_value):
    loudness = 1.0
    for position, parts in shards:
        heights = jax.random.uniform(jax.random.fold_in(jax.random.fold_in(key, 6), position), (parts,), jnp.float32, low / len(shards), top_value / len(shards))
        loudness = loudness * jnp.repeat(jnp.exp(heights), shape[position] // parts).reshape((-1,) + (1,) * (len(shape) - 1 - position))
    return loudness


def assign_block(own_key, own, number, rows, count, top, reach, skew):
    ranking = jax.random.permutation(own_key, count)
    crowded, ordinary = shares(count, rows * top, reach, skew, True), shares(count, rows * top, reach, skew, False)
    places = jnp.arange(count)

    def named(sizes, rotation):
        used = int((sizes > 0).sum())
        fixed = max(1, used // 4)
        shifted = fixed + (places - fixed + rotation * (used - fixed)) % max(1, count - fixed)
        return jnp.zeros((count,), jnp.int32).at[ranking[jnp.where(places < fixed, places, shifted)]].set(jnp.asarray(sizes, jnp.int32))

    sizes = jnp.where(number % 4 == 0, named(crowded, number // 4), named(ordinary, number - number // 4 - 1))
    mixed = jax.random.permutation(jax.random.fold_in(own, 3), count)
    source_of, taker = mixed[0:count // 2 * 2:2], mixed[1:count // 2 * 2:2]
    room = jnp.minimum(sizes[source_of] - 1, reach - sizes[taker]) // 2
    room = jnp.where((source_of == ranking[0]) | (taker == ranking[0]) | (sizes[taker] == 0), 0, jnp.maximum(room, 0))
    shifted = jax.random.randint(jax.random.fold_in(own, 4), (count // 2,), 0, 1 << 20) % (room + 1)
    sizes = sizes.at[source_of].add(-shifted).at[taker].add(shifted)
    members = jnp.searchsorted(jnp.cumsum(sizes), jnp.arange(rows * top), side="right").astype(jnp.int32)
    listing = members.reshape(top, rows).T
    listing = listing[jax.random.permutation(jax.random.fold_in(own, 1), rows)]
    rotation = jax.random.randint(jax.random.fold_in(own, 2), (rows, 1), 0, top)
    return jnp.take_along_axis(listing, (jnp.arange(top)[None, :] + rotation) % top, axis=1)


def shares(count, total, reach, lean, full):
    portions = [(1 << 20) // math.isqrt(rank ** lean) + 1 for rank in range(1, count + 1)]
    largest = reach if full else min(reach, max(-(-total // count), total * portions[0] // sum(portions)))
    least = 1 if total - largest >= count - 1 else 0
    holding, surplus = [largest] + [least] * (count - 1), total - largest - least * (count - 1)
    while surplus > 0:
        movable = [i for i in range(1, count) if holding[i] < largest] or [i for i in range(1, count) if holding[i] < reach]
        whole, remaining = sum([portions[i] for i in movable]), surplus
        for i in movable:
            addition = min(reach - holding[i], max(1, remaining * portions[i] // whole), surplus)
            holding[i] = holding[i] + addition
            surplus = surplus - addition
    return np.array(holding)


def normal_values(key, dims, width, limit, shards=(), held_as=jnp.bfloat16):
    drawn = jax.random.normal(key, dims, jnp.float32) * width
    if len(shards) > 0:
        drawn = levels(key, dims, shards, -0.22, 0.18) * drawn
    return jnp.clip(drawn, min=-limit, max=limit).astype(held_as)


def setup_inputs(seed: int = 0) -> dict:
    keys = jax.random.split(jax.random.key(seed), 16)
    tokens = normal_values(keys[0], (STREAMS, SEQ, D), 1.0, 6.0, ((0, 8), (1, 4)))
    doc_starts = draw_doc_starts(jax.random.fold_in(keys[15], 71), 0)
    expert_ids_keys = jax.random.split(jax.random.fold_in(keys[2], 1), STREAMS * SEQ // TOK_DEV)
    expert_ids_turns = jax.random.permutation(jax.random.fold_in(keys[2], 3), STREAMS * SEQ // TOK_DEV)
    expert_ids = jax.vmap(lambda own, number: assign_block(jax.random.fold_in(keys[2], 2), own, number, TOK_DEV, E, TOP, CAP, 1))(expert_ids_keys, expert_ids_turns).reshape((STREAMS, SEQ, TOP))
    w_query = normal_values(keys[3], (D, D), D ** -0.5, 0.125, ((0, 32),))
    w_key = normal_values(keys[4], (D, D), D ** -0.5, 0.125, ((0, 32),))
    w_value = normal_values(keys[5], (D, D), D ** -0.5, 0.125, ((0, 32),))
    w_attn_out = normal_values(keys[6], (D, D), (D // 64) ** -0.5, 1.0, ((0, 32),))
    w_router = normal_values(keys[7], (D, E), (4 * D) ** -0.5, 0.0625, ((0, 32),))
    g_attn = jnp.clip(1.0 + 0.18 * jax.random.normal(keys[8], (D,), jnp.float32), 0.099609375, 1.8984375).astype(jnp.bfloat16)
    g_query = jnp.clip(1.0 + 0.18 * jax.random.normal(keys[9], (D,), jnp.float32), 0.099609375, 1.8984375).astype(jnp.bfloat16)
    g_key = jnp.clip(1.0 + 0.18 * jax.random.normal(keys[10], (D,), jnp.float32), 0.099609375, 1.8984375).astype(jnp.bfloat16)
    g_ffn = jnp.clip(1.0 + 0.18 * jax.random.normal(keys[11], (D,), jnp.float32), 0.099609375, 1.8984375).astype(jnp.bfloat16)
    w_in = normal_values(keys[12], (PIECES, D, 2 * FH), D ** -0.5, 0.125, ((0, 32),))
    w_out = normal_values(keys[13], (PIECES, FH, D), 1.0, 6.0, ((0, 32),))
    cotangent = normal_values(keys[14], (STREAMS, SEQ, D), 1.0, 6.0, ((0, 8), (1, 4)))
    return {"tokens": tokens, "doc_starts": doc_starts, "expert_ids": expert_ids, "w_query": w_query, "w_key": w_key, "w_value": w_value, "w_attn_out": w_attn_out, "w_router": w_router, "g_attn": g_attn, "g_query": g_query, "g_key": g_key, "g_ffn": g_ffn, "w_in": w_in, "w_out": w_out, "cotangent": cotangent}


@jax.custom_vjp
def low(v):
    return lax.optimization_barrier(v.astype(jnp.bfloat16)).astype(jnp.float32)

@jax.custom_vjp
def low_back(v):
    return v

def low_keep(v):
    return (low(v), None)

def low_pass(kept, grad):
    return (grad,)

def back_keep(v):
    return (v, None)

def back_low(kept, grad):
    return (low(grad),)
low.defvjp(low_keep, low_pass)
low_back.defvjp(back_keep, back_low)
epsilon = 1e-05
masked_score = -1e+30
rope_base = 10000.0
highest_prec = lax.Precision.HIGHEST

def matmul(left_op, right_op):
    return jnp.dot(left_op, right_op, precision=highest_prec, preferred_element_type=jnp.float32)

def rms_scale(values, gain_vec):
    inv_rms = lax.rsqrt(lax.optimization_barrier(jnp.mean(values * values, axis=-1, keepdims=True)) + epsilon)
    return values * inv_rms * gain_vec

def rotary_tables(positions, head_dim):
    half_dim = head_dim // 2
    frequency = rope_base ** (-(jnp.arange(half_dim, dtype=jnp.float32) * 2.0 / head_dim))
    angles = positions.astype(jnp.float32)[:, None] * frequency[None, :]
    return (jnp.cos(angles), jnp.sin(angles))

def rotate(values, cosine, sine_tab, head_count):
    row_count = values.shape[0]
    shaped = values.reshape(row_count, head_count, -1)
    half_dim = shaped.shape[-1] // 2
    first_half = shaped[..., :half_dim]
    second_half = shaped[..., half_dim:]
    cos_heads = cosine[:, None, :]
    sin_heads = sine_tab[:, None, :]
    turned = jnp.concatenate([first_half * cos_heads - second_half * sin_heads, second_half * cos_heads + first_half * sin_heads], axis=-1)
    return turned.reshape(row_count, -1)

def doc_index(positions, starts):
    return lax.optimization_barrier(jnp.sum((starts[None, :] <= positions[:, None]).astype(jnp.int32), axis=1)) - 1

def dispatch_tables(expert_ids):
    flat_ids = expert_ids.reshape(N_CTX, TOK_DEV * TOP).astype(jnp.int32)
    onehot = (flat_ids[..., None] == jnp.arange(E, dtype=jnp.int32)[None, None, :]).astype(jnp.int32)
    slot_rank = lax.optimization_barrier(jnp.sum(jnp.cumsum(onehot, axis=1) * onehot, axis=-1)) - 1
    block_ids = jnp.arange(N_CTX, dtype=jnp.int32)[:, None]
    slot_pos = (block_ids * CAP + slot_rank).astype(jnp.int32)
    token_ids = (block_ids * TOK_DEV + jnp.arange(TOK_DEV * TOP, dtype=jnp.int32)[None, :] // TOP).astype(jnp.int32)
    slot_table = jnp.zeros((E, N_CTX * CAP), jnp.int32).at[flat_ids, slot_pos].set(token_ids)
    return (slot_table, slot_pos.reshape(SEQ, TOP))

def layer_forward(params, x_rows, starts, expert_ids, slot_table, slot_pos):
    w_query, w_key, w_value, w_attn_out, w_router, g_attn, g_query, g_key, g_ffn, w_in, w_out = params
    positions = jnp.arange(SEQ, dtype=jnp.int32)
    doc_ids = doc_index(positions, starts)
    normed = low(rms_scale(x_rows, g_attn))
    query_raw = low_back(matmul(normed, w_query))
    key_raw = low_back(matmul(normed, w_key))
    value_all = low(low_back(matmul(normed, w_value)))
    cosine, sine_tab = rotary_tables(positions, HD)
    queries = low(rotate(rms_scale(query_raw, g_query), cosine, sine_tab, H))
    keys_all = low(rotate(rms_scale(key_raw, g_key), cosine, sine_tab, H))
    key_heads = keys_all.reshape(SEQ, H, HD)
    value_heads = value_all.reshape(SEQ, H, HD)
    scale_factor = 1.0 / math.sqrt(HD)
    query_block = min(SEQ, 512)

    def attend(block_args):
        query_rows, query_pos = block_args
        query_docs = doc_index(query_pos, starts)
        raw_scores = jnp.einsum('qhd,khd->hqk', query_rows.reshape(-1, H, HD), key_heads, precision=highest_prec) * scale_factor
        allowed = (positions[None, :] <= query_pos[:, None]) & (doc_ids[None, :] == query_docs[:, None])
        scores = jnp.where(allowed[None], low_back(raw_scores), masked_score)
        probs_low = low(jax.nn.softmax(scores, axis=-1))
        mixed_heads = jnp.einsum('hqk,khd->qhd', probs_low, value_heads, precision=highest_prec)
        return mixed_heads.reshape(-1, D)
    block_count = SEQ // query_block
    blocks = lax.map(jax.checkpoint(attend), (queries.reshape(block_count, query_block, D), positions.reshape(block_count, query_block)))
    mixed_all = low(low_back(blocks.reshape(SEQ, D)))
    hidden = x_rows + low_back(matmul(mixed_all, w_attn_out))
    moe_in = low(rms_scale(hidden, g_ffn))
    router_probs = jax.nn.softmax(matmul(moe_in, w_router), axis=-1)
    gate_values = jnp.take_along_axis(router_probs, expert_ids, axis=1)
    gathered = moe_in[slot_table]
    pieces_in = low_back(jnp.stack([gathered, gathered], axis=1)).reshape(2 * E, N_CTX * CAP, D)
    projected = low_back(jnp.einsum('prd,pdf->prf', pieces_in, w_in, precision=highest_prec))
    inner_act = low(jax.nn.silu(projected[..., :FH]) * projected[..., FH:])
    piece_out = low(low_back(jnp.einsum('prf,pfd->prd', inner_act, w_out, precision=highest_prec)))
    combined = lax.optimization_barrier(jnp.sum(piece_out.reshape(E, 2, N_CTX * CAP, D), axis=1))
    slot_values = combined[expert_ids, slot_pos]
    return hidden + lax.optimization_barrier(jnp.sum(gate_values[..., None] * slot_values, axis=1))

def reference(tokens, doc_starts, expert_ids, w_query, w_key, w_value, w_attn_out, w_router, g_attn, g_query, g_key, g_ffn, w_in, w_out, cotangent):
    params = tuple((weight.astype(jnp.float32) for weight in (w_query, w_key, w_value, w_attn_out, w_router, g_attn, g_query, g_key, g_ffn, w_in, w_out)))

    def one_stream(totals, stream_args):
        x_rows, starts, stream_ids, stream_cot = stream_args
        slot_table, slot_pos = dispatch_tables(stream_ids)

        def forward(param_set, inputs):
            return layer_forward(param_set, inputs, starts, stream_ids, slot_table, slot_pos)
        result, pullback = jax.vjp(forward, params, x_rows.astype(jnp.float32))
        param_grads, input_grad = pullback(stream_cot.astype(jnp.float32))
        totals = jax.tree.map(jnp.add, totals, param_grads)
        return (totals, (result.astype(jnp.bfloat16), input_grad))
    zero_grads = tuple((jnp.zeros_like(weight) for weight in params))
    totals, (outputs, input_grads) = lax.scan(one_stream, zero_grads, (tokens, doc_starts, expert_ids, cotangent))
    return (outputs, input_grads, totals[0], totals[1], totals[2], totals[3], totals[4], totals[5], totals[6], totals[7], totals[8], totals[9], totals[10])
```

```python
import math

import jax
import jax.numpy as jnp
from jax import lax
from jax.sharding import PartitionSpec as P

H = 16
HD = 128
E = 64
TOP = 8
FH = 512
CAP = 24

EPS = 1e-05
MASKED = -1e30
ROPE_BASE = 10000.0
HIGHEST = lax.Precision.HIGHEST
F32 = jnp.float32
BF = jnp.bfloat16
ALL = ("fsdp", "ctx")


def pick(stacked, index):
    return lax.dynamic_index_in_dim(stacked, index, 0, keepdims=False)


def add_low(a, b):
    return (a.astype(F32) + b.astype(F32)).astype(BF)


class Links:
    def __init__(self, fsdp_size, ctx_size):
        self.nf = fsdp_size
        self.nc = ctx_size
        self.native = fsdp_size == 8 and ctx_size == 4
        self.f = lax.axis_index("fsdp")
        self.c = lax.axis_index("ctx")

    def swap(self, value, mask):
        return lax.ppermute(value, "fsdp", [(i, i ^ mask) for i in range(self.nf)])

    def shift(self, value, step):
        n = self.nc
        return lax.ppermute(value, "ctx", [(i, (i + step) % n) for i in range(n)])

    def block_of(self, m):
        return self.f ^ m if self.native else jnp.int32(m)

    def gather_ctx(self, value):
        if not self.native:
            return lax.all_gather(value, "ctx", axis=0)
        up = down = value
        below, above = [], []
        last = self.nc - 1
        for k in range(last):
            up = lax.ppermute(up, "ctx", [(i, i + 1) for i in range(k, last)])
            down = lax.ppermute(down, "ctx", [(i + 1, i) for i in range(0, last - k)])
            below.append(up)
            above.append(down)
        line = jnp.stack(below[::-1] + [value] + above)
        return lax.dynamic_slice_in_dim(line, last - self.c, self.nc, 0)

    def sum_ctx(self, value):
        if not self.native:
            return lax.psum(value, "ctx")
        total = value
        for k in range(1, self.nc):
            total = total + self.shift(value, k)
        return total

    def scatter_ctx(self, value):
        if not self.native:
            return lax.psum_scatter(value, "ctx", scatter_dimension=0, tiled=False).astype(F32)
        total = pick(value, self.c).astype(F32)
        for k in range(1, self.nc):
            total = total + self.shift(pick(value, (self.c + k) % self.nc), k).astype(F32)
        return total

    def exchange_ctx(self, value):
        return lax.all_to_all(value, "ctx", split_axis=0, concat_axis=0, tiled=True)

    def gather_fsdp(self, value):
        if not self.native:
            whole = lax.all_gather(value, "fsdp", axis=0)
            return [[whole[m]] for m in range(self.nf)]
        half = value.shape[0] // 2
        from_x = self.swap(value, 2)
        from_y = self.swap(value, 4)
        other = self.swap(value, 1)
        diag_a = self.swap(from_y[:half], 2)
        diag_b = self.swap(from_x[half:], 4)
        other_x = self.swap(from_x, 1)
        other_y = self.swap(from_y, 1)
        other_a = self.swap(diag_a, 1)
        other_b = self.swap(diag_b, 1)

        def cut(rows):
            return [rows[:half], rows[half:]]

        return [
            cut(value),
            cut(other),
            cut(from_x),
            cut(other_x),
            cut(from_y),
            cut(other_y),
            [diag_a, diag_b],
            [other_a, other_b],
        ]

    def gather_fsdp_sorted(self, value):
        blocks = self.gather_fsdp(value)
        if not self.native:
            return jnp.concatenate([b[0] for b in blocks])
        stacked = jnp.concatenate([p for b in blocks for p in b]).reshape((self.nf,) + value.shape)
        return jnp.concatenate([pick(stacked, self.f ^ j) for j in range(self.nf)])

    def scatter_fsdp(self, parts):
        if not self.native:
            whole = jnp.stack(parts)
            return lax.psum_scatter(whole, "fsdp", scatter_dimension=0, tiled=False).astype(F32)
        near = [add_low(parts[m], self.swap(parts[m + 1], 1)) for m in (2, 4, 6)]
        own = parts[0].astype(F32) + self.swap(parts[1], 1).astype(F32)
        to_x, to_y, to_d = near
        half = own.shape[0] // 2
        xa = self.swap(to_x[:half], 2)
        xd = self.swap(to_d[:half], 2)
        yb = self.swap(to_y[half:], 4)
        yd = self.swap(to_d[half:], 4)
        ya = self.swap(add_low(to_y[:half], xd), 4)
        xb = self.swap(add_low(to_x[half:], yd), 2)
        top = own[:half] + xa.astype(F32) + ya.astype(F32)
        bottom = own[half:] + yb.astype(F32) + xb.astype(F32)
        return jnp.concatenate([top, bottom])


def rms_parts(values):
    return lax.rsqrt(jnp.mean(values * values, axis=-1, keepdims=True) + EPS)


def rms_back(values, inv, gain, grad):
    u = grad * gain
    mean = jnp.mean(u * values, axis=-1, keepdims=True)
    return inv * u - values * (inv * inv * inv) * mean, jnp.sum(grad * values * inv, axis=0)


def rotary_tables(positions):
    half = HD // 2
    frequency = ROPE_BASE ** (-(jnp.arange(half, dtype=F32) * 2.0 / HD))
    angles = positions.astype(F32)[:, None] * frequency[None, :]
    return jnp.cos(angles), jnp.sin(angles)


def rotate(values, cosine, sine):
    rows = values.shape[0]
    shaped = values.reshape(rows, -1, HD)
    a, b = shaped[..., : HD // 2], shaped[..., HD // 2 :]
    cos, sin = cosine[:, None, :], sine[:, None, :]
    return jnp.concatenate([a * cos - b * sin, b * cos + a * sin], axis=-1).reshape(rows, -1)


def doc_index(positions, starts):
    return jnp.sum((starts[None, :] <= positions[:, None]).astype(jnp.int32), axis=1) - 1


def dot(a, b):
    return jnp.dot(a, b, preferred_element_type=F32)


def dot_t(a, b):
    return jnp.einsum("td,ed->te", a, b, preferred_element_type=F32)


def t_dot(a, b):
    return jnp.einsum("td,te->de", a, b, preferred_element_type=F32)


def shards(
    tokens,
    doc_starts,
    expert_ids,
    w_query,
    w_key,
    w_value,
    w_attn_out,
    w_router,
    g_attn,
    g_query,
    g_key,
    g_ffn,
    w_in,
    w_out,
    cotangent,
):
    nf, nc = lax.axis_size("fsdp"), lax.axis_size("ctx")
    ndev = nf * nc
    links = Links(nf, nc)
    x_own = tokens[0]
    g_own = cotangent[0]
    tok, dim = x_own.shape
    seq = tok * nc
    width = dim // nc
    heads = H // nc
    own_rows = w_query.shape[0]
    fsdp_rows = own_rows * nc
    starts = doc_starts[0]

    small = jnp.concatenate(
        [
            w_router.reshape(-1),
            g_attn,
            g_query,
            g_key,
            g_ffn,
            expert_ids[0].T.reshape(-1).astype(BF),
        ]
    )
    small_len = small.shape[0]
    small_rows = -(-small_len // (16 * 128)) * 16
    small = jnp.pad(small, (0, small_rows * 128 - small_len)).reshape(1, small_rows, 128)
    small_all = lax.all_to_all(
        jnp.broadcast_to(small, (ndev, small_rows, 128)),
        ALL,
        split_axis=0,
        concat_axis=0,
        tiled=True,
    ).reshape(ndev, -1)
    router_len = own_rows * E
    router = small_all[:, :router_len].reshape(dim, E)
    gains = small_all[:, router_len : router_len + 4 * own_rows].reshape(ndev, 4, own_rows)
    gains = gains.transpose(1, 0, 2).reshape(4, dim).astype(F32)
    gain_attn, gain_query, gain_key, gain_ffn = gains
    ids_all = small_all[:, router_len + 4 * own_rows : small_len].astype(jnp.int32)
    ids_all = ids_all.reshape(nf, nc, TOP, tok)

    qkv_own = jnp.stack([w.reshape(own_rows, nc, width) for w in (w_query, w_key, w_value)], axis=2)
    qkv_own = qkv_own.transpose(1, 0, 2, 3).reshape(nc, own_rows, 3 * width)
    qkv_rows = links.exchange_ctx(qkv_own).reshape(fsdp_rows, 3 * width)
    w_qkv = links.gather_fsdp_sorted(qkv_rows)
    x_all = links.gather_ctx(x_own).reshape(seq, dim)
    w_o = links.gather_fsdp_sorted(links.gather_ctx(w_attn_out).reshape(fsdp_rows, dim))
    g_stream = links.gather_ctx(g_own).reshape(seq, dim)
    g_blocks = links.gather_fsdp(g_stream)

    x_float = x_all.astype(F32)
    normed = (x_float * rms_parts(x_float) * gain_attn).astype(BF)
    raw = dot(normed, w_qkv)
    query_raw, key_raw = raw[:, :width], raw[:, width : 2 * width]
    value = raw[:, 2 * width :].astype(BF)
    sums = jnp.stack([jnp.sum(query_raw * query_raw, -1), jnp.sum(key_raw * key_raw, -1)])
    sums = links.sum_ctx(sums)
    inv_query = lax.rsqrt(sums[0] / dim + EPS)[:, None]
    inv_key = lax.rsqrt(sums[1] / dim + EPS)[:, None]
    positions = jnp.arange(seq, dtype=jnp.int32)
    cosine, sine = rotary_tables(positions)
    gq = pick(gain_query.reshape(nc, width), links.c)
    gk = pick(gain_key.reshape(nc, width), links.c)
    queries = rotate(query_raw * inv_query * gq, cosine, sine).astype(BF).reshape(seq, heads, HD)
    keys = rotate(key_raw * inv_key * gk, cosine, sine).astype(BF).reshape(seq, heads, HD)
    values = value.reshape(seq, heads, HD)
    scale = 1.0 / math.sqrt(HD)
    docs = doc_index(positions, starts)
    allowed = (positions[None, :] <= positions[:, None]) & (docs[None, :] == docs[:, None])
    scores = jnp.einsum("qhd,khd->hqk", queries, keys, preferred_element_type=F32) * scale
    probs = jax.nn.softmax(jnp.where(allowed[None], scores, MASKED), axis=-1)
    probs_low = probs.astype(BF)
    mixed = jnp.einsum("hqk,khd->qhd", probs_low, values, preferred_element_type=F32)
    mixed = mixed.reshape(seq, width).astype(BF)
    mixed_all = links.gather_ctx(mixed).transpose(1, 0, 2).reshape(seq, dim)
    hidden = x_float + dot(mixed_all, w_o)
    inv_ffn = rms_parts(hidden)
    moe_in = (hidden * inv_ffn * gain_ffn).astype(BF)

    x_blocks = links.gather_fsdp(moe_in)
    pieces = w_in.shape[0]
    halves = min(2, pieces)
    experts = pieces // halves
    device = links.f * nc + links.c
    first_expert = device * pieces // 2
    mine = first_expert + jnp.arange(experts, dtype=jnp.int32)
    ids_rel = jnp.stack([pick(ids_all, links.block_of(m)) for m in range(nf)])
    named = jnp.any(ids_rel[:, :, None] == mine[:, None, None], axis=3)
    before = (jnp.arange(tok)[:, None] < jnp.arange(tok)[None, :]).astype(BF)
    rank = jnp.einsum("mcjt,ts->mcjs", named.astype(BF), before, preferred_element_type=F32)
    slots = (
        named[:, :, :, None] & (rank[:, :, :, None] == jnp.arange(CAP, dtype=F32)[:, None])
    ).astype(BF)

    def take_rows(blocks):
        taken = []
        for m in range(nf):
            at = 0
            for piece in blocks[m]:
                n = piece.shape[0] // tok
                taken.append(
                    jnp.einsum(
                        "cjrt,ctd->jcrd",
                        slots[m, at : at + n],
                        piece.reshape(n, tok, dim),
                        preferred_element_type=BF,
                    )
                )
                at += n
        return jnp.concatenate(taken, axis=1).reshape(experts, ndev * CAP, dim)

    def put_rows(rows):
        shaped = rows.reshape(experts, nf, nc, CAP, dim)
        return [
            jnp.einsum("cjrt,jcrd->ctd", slots[m], shaped[:, m], preferred_element_type=BF).reshape(
                seq, dim
            )
            for m in range(nf)
        ]

    g_rows = take_rows(g_blocks)
    w_out_e = w_out.reshape(experts, halves * FH, dim)
    dinner_raw = jnp.einsum("jrd,jfd->jrf", g_rows, w_out_e, preferred_element_type=F32)
    x_rows = take_rows(x_blocks)
    route = jnp.einsum("jrd,de->jre", x_rows, router, preferred_element_type=F32)
    route = jax.nn.softmax(route, axis=-1)
    chosen = mine[:, None, None] == jnp.arange(E, dtype=jnp.int32)
    gate = jnp.sum(jnp.where(chosen, route, 0.0), axis=-1)[..., None]
    nrow = x_rows.shape[1]
    x_pieces = jnp.broadcast_to(x_rows[:, None], (experts, halves, nrow, dim))
    x_pieces = x_pieces.reshape(pieces, nrow, dim)
    projected = jnp.einsum("prd,pdf->prf", x_pieces, w_in, preferred_element_type=F32)
    gate_part, up_part = projected[..., :FH], projected[..., FH:]
    sig = jax.nn.sigmoid(gate_part)
    inner_float = gate_part * sig * up_part
    inner = inner_float.astype(BF)
    dinner_p = dinner_raw.reshape(experts, nrow, halves, FH).transpose(0, 2, 1, 3)
    dinner_p = dinner_p.reshape(pieces, nrow, FH)
    dgate_rows = jnp.sum(
        jnp.sum(inner.astype(F32) * dinner_p, axis=-1).reshape(experts, halves, nrow), axis=1
    )
    gate_p = jnp.broadcast_to(gate[:, None], (experts, halves, nrow, 1)).reshape(pieces, nrow, 1)
    dinner = gate_p * dinner_p
    dprojected = jnp.concatenate(
        [
            dinner * up_part * sig * (1.0 + gate_part * (1.0 - sig)),
            dinner * gate_part * sig,
        ],
        axis=-1,
    ).astype(BF)
    dslot_p = jnp.einsum("prf,pdf->prd", dprojected, w_in, preferred_element_type=F32)
    dslot = jnp.sum(dslot_p.reshape(experts, halves, nrow, dim), axis=1).astype(BF)
    dmoe_stream = links.scatter_fsdp(put_rows(dslot)).astype(BF)
    dmoe = links.scatter_ctx(dmoe_stream.reshape(nc, tok, dim))

    dgate_blocks = dgate_rows.reshape(experts, nf, nc, CAP)
    dgate_tok = jnp.einsum(
        "mcjrt,jmcr->mcjt", slots.astype(F32), dgate_blocks, precision=HIGHEST
    )
    dgate_sorted = jnp.stack([pick(dgate_tok, links.block_of(j)) for j in range(nf)])
    dgate_back = lax.all_to_all(
        dgate_sorted.reshape(ndev, experts, tok), ALL, split_axis=0, concat_axis=0, tiled=True
    )
    dprob = jnp.sum(dgate_back.reshape(E, ndev * experts // E, tok), axis=1).T

    inner_e = inner.reshape(experts, halves, nrow, FH)
    inner_e = inner_e.transpose(0, 2, 1, 3).reshape(experts, nrow, halves * FH)
    combined = jnp.einsum("jrf,jfd->jrd", inner_e, w_out_e, preferred_element_type=F32)
    out_stream = links.scatter_fsdp(put_rows((gate * combined).astype(BF))).astype(BF)
    out_rows = links.scatter_ctx(out_stream.reshape(nc, tok, dim))
    hidden_own = pick(hidden.reshape(nc, tok, dim), links.c)
    output = (hidden_own + out_rows).astype(BF)

    gated_inner = (gate * inner_e.astype(F32)).astype(BF)
    grad_w_out = jnp.einsum("jrf,jrd->jfd", gated_inner, g_rows, preferred_element_type=F32)
    grad_w_out = grad_w_out.reshape(w_out.shape)
    grad_w_in = jnp.einsum("prd,prf->pdf", x_pieces, dprojected, preferred_element_type=F32)

    moe_own = pick(moe_in.reshape(nc, tok, dim), links.c)
    router_probs = jax.nn.softmax(dot(moe_own, router), axis=-1)
    dlogits = router_probs * (dprob - jnp.sum(router_probs * dprob, axis=-1, keepdims=True))
    grad_router = jnp.einsum("td,te->de", moe_own.astype(F32), dlogits, precision=HIGHEST)
    dmoe = dmoe + jnp.einsum("te,de->td", dlogits, router.astype(F32), precision=HIGHEST)
    inv_own = pick(inv_ffn.reshape(nc, tok, 1), links.c)
    dhidden, grad_gain_ffn = rms_back(hidden_own, inv_own, gain_ffn, dmoe)
    dhidden = g_own.astype(F32) + dhidden

    dhidden_all = links.gather_ctx(dhidden.astype(BF)).reshape(seq, dim)
    w_o_own = pick(w_o.reshape(nc, width, dim), links.c)
    dmixed = dot_t(dhidden_all, w_o_own).astype(BF).reshape(seq, heads, HD)
    dprobs = jnp.einsum("qhd,khd->hqk", dmixed, values, preferred_element_type=F32)
    delta = jnp.sum(probs * dprobs, axis=-1, keepdims=True)
    dscores = (probs * (dprobs - delta)).astype(BF)
    dqueries = jnp.einsum("hqk,khd->qhd", dscores, keys, preferred_element_type=F32) * scale
    dkeys = jnp.einsum("hqk,qhd->khd", dscores, queries, preferred_element_type=F32) * scale
    dvalue = jnp.einsum("hqk,qhd->khd", probs_low, dmixed, preferred_element_type=F32)
    dvalue_low = dvalue.reshape(seq, width).astype(BF)
    turned_query = rotate(dqueries.reshape(seq, width), cosine, -sine)
    turned_key = rotate(dkeys.reshape(seq, width), cosine, -sine)
    uq, uk = turned_query * gq, turned_key * gk
    back = jnp.stack([jnp.sum(uq * query_raw, -1), jnp.sum(uk * key_raw, -1)])
    back = links.sum_ctx(back) / dim
    dquery_low = (inv_query * uq - query_raw * inv_query**3 * back[0][:, None]).astype(BF)
    dkey_low = (inv_key * uk - key_raw * inv_key**3 * back[1][:, None]).astype(BF)
    grad_gain_query = jnp.sum(turned_query * query_raw * inv_query, axis=0)
    grad_gain_key = jnp.sum(turned_key * key_raw * inv_key, axis=0)
    dqkv = jnp.concatenate([dquery_low, dkey_low, dvalue_low], axis=1)
    dnormed = links.scatter_ctx(dot_t(dqkv, w_qkv).astype(BF).reshape(nc, tok, dim))
    x_own_float = x_own.astype(F32)
    dx, grad_gain_attn = rms_back(x_own_float, rms_parts(x_own_float), gain_attn, dnormed)
    input_grad = (dhidden + dx)[None]

    dhidden_cols = pick(dhidden_all.reshape(seq, nc, width).transpose(1, 0, 2), links.c)

    def reduce_columns(grad):
        blocks = grad.astype(BF).reshape(nf, fsdp_rows, grad.shape[1])
        summed = links.scatter_fsdp([pick(blocks, links.block_of(m)) for m in range(nf)])
        return links.exchange_ctx(summed.reshape(nc, own_rows, grad.shape[1]))

    grad_o = reduce_columns(t_dot(mixed_all, dhidden_cols))
    grad_attn_out = grad_o.transpose(1, 0, 2).reshape(own_rows, dim)
    grad_qkv = reduce_columns(t_dot(normed, dqkv))
    grad_qkv = grad_qkv.reshape(nc, own_rows, 3, width).transpose(2, 1, 0, 3)
    grad_qkv = grad_qkv.reshape(3, own_rows, dim)

    def placed(vector):
        return lax.dynamic_update_slice(
            jnp.zeros((dim,), F32), vector, (links.c * width,)
        )

    router_terms = jnp.concatenate(
        [grad_router.reshape(ndev, -1), grad_gain_ffn.reshape(ndev, -1)], axis=1
    )
    gain_terms = jnp.stack([grad_gain_attn, placed(grad_gain_query), placed(grad_gain_key)])
    gain_terms = gain_terms.reshape(3, ndev, own_rows).transpose(1, 0, 2).reshape(ndev, -1)

    def reduce_small(terms):
        count = terms.shape[1]
        rows = -(-count // 1024) * 8
        padded = jnp.pad(terms, ((0, 0), (0, rows * 128 - count))).reshape(ndev, rows, 128)
        moved = lax.all_to_all(padded, ALL, split_axis=0, concat_axis=0, tiled=True)
        return jnp.sum(moved, axis=0).reshape(-1)[:count]

    router_sum = reduce_small(router_terms)
    gain_sum = reduce_small(gain_terms).reshape(3, own_rows)
    return (
        output[None],
        input_grad,
        grad_qkv[0],
        grad_qkv[1],
        grad_qkv[2],
        grad_attn_out,
        router_sum[: own_rows * E].reshape(own_rows, E),
        gain_sum[0],
        gain_sum[1],
        gain_sum[2],
        router_sum[own_rows * E :],
        grad_w_in,
        grad_w_out,
    )


def solution(mesh):
    rows = P(ALL, None)
    vec = P(ALL)
    cube = P(ALL, None, None)
    stream = P("fsdp", "ctx", None)
    return jax.shard_map(
        shards,
        mesh=mesh,
        in_specs=(
            stream,
            P("fsdp", None),
            stream,
            rows,
            rows,
            rows,
            rows,
            rows,
            vec,
            vec,
            vec,
            vec,
            cube,
            cube,
            stream,
        ),
        out_specs=(
            stream,
            stream,
            rows,
            rows,
            rows,
            rows,
            rows,
            vec,
            vec,
            vec,
            vec,
            cube,
            cube,
        ),
        check_vma=False,
    )
```

```python
import functools
import math

import jax
import jax.numpy as jnp
from jax import lax
from jax.experimental import pallas as pl
from jax.experimental.pallas import tpu as pltpu
from jax.sharding import PartitionSpec as P

H = 16
HD = 128
E = 64
TOP = 8
FH = 512
CAP = 24

EPS = 1e-05
MASKED = -1e30
ROPE_BASE = 10000.0
HIGHEST = lax.Precision.HIGHEST
F32 = jnp.float32
BF = jnp.bfloat16
ALL = ("fsdp", "ctx")
LANES = 128
VMEM_LIMIT = 60 * 1024 * 1024


def pick(stacked, index):
    return lax.dynamic_index_in_dim(stacked, index, 0, keepdims=False)


def after(value, *others):
    return held([value], *others)[0]


def held(values, *others):
    if not others:
        return list(values)
    values = list(values)
    anywhere = pl.BlockSpec(memory_space=pl.ANY)
    done = pl.pallas_call(
        lambda *refs: None,
        out_shape=[jax.ShapeDtypeStruct(v.shape, v.dtype) for v in values],
        in_specs=[anywhere] * (len(values) + len(others)),
        out_specs=[anywhere] * len(values),
        input_output_aliases={i: i for i in range(len(values))},
    )(*values, *others)
    return list(done)


def held_pieces(blocks, *gate):
    flat = held([a for b in blocks for a in b], *gate)
    return [[flat.pop(0) for _ in b] for b in blocks]


def add_low(*terms):
    return sum(t.astype(F32) for t in terms).astype(BF)


class Links:
    def __init__(self, nf, nc):
        self.nf, self.nc = nf, nc
        self.native = nf == 8 and nc == 4
        self.cores = 2 if self.native else 1
        self.f = lax.axis_index("fsdp")
        self.c = lax.axis_index("ctx")
        ms = jnp.arange(nf, dtype=jnp.int32)
        self.frel = self.f ^ ms if self.native else ms

    def swap(self, value, mask):
        return lax.ppermute(value, "fsdp", [(i, i ^ mask) for i in range(self.nf)])

    def cswap(self, value, mask):
        return lax.ppermute(value, "ctx", [(i, i ^ mask) for i in range(self.nc)])

    def exchange(self, value):
        return lax.all_to_all(value, "ctx", split_axis=0, concat_axis=0, tiled=True)

    def gather(self, value, *gate):
        return self.exchange(after(jnp.broadcast_to(value, (self.nc,) + value.shape), *gate))

    def slots(self, value):
        if not self.native:
            whole = lax.all_gather(value, "ctx", axis=0)
            return [whole[k] for k in range(self.nc)]
        return [value] + [self.cswap(value, k) for k in range(1, self.nc)]

    def sum_slots(self, parts):
        if not self.native:
            whole = jnp.stack(parts)
            return [lax.psum_scatter(whole, "ctx", scatter_dimension=0, tiled=False)]
        return [parts[0]] + [self.cswap(parts[k], k) for k in range(1, self.nc)]

    def relative(self, value, planes=False):
        if not self.native:
            return value
        dims = value.shape
        for bit, place in ((4, self.f), (2, self.f), (1, self.f), (2, self.c), (1, self.c)):
            lead = 0 if place is self.f else 1
            if lead and planes:
                continue
            n = dims[lead]
            split = dims[:lead] + (n // (2 * bit), 2, bit) + dims[lead + 1 :]
            cut = value.reshape(split)
            parts = jnp.split(cut, 2, axis=lead + 1)
            flipped = jnp.concatenate(parts[::-1], axis=lead + 1)
            value = jnp.where((place & bit) > 0, flipped, cut).reshape(dims)
        return value

    def plane_start(self, value):
        if not self.native:
            return [value]
        return [value, self.swap(value, 2), self.swap(value, 4)]

    def plane_end(self, begun, *gate):
        if not self.native:
            whole = lax.all_gather(begun[0], "fsdp", axis=0)
            return [[whole[m]] for m in range(self.nf)], begun
        value, from_x, from_y = begun
        half = value.shape[0] // 2
        from_x, from_y = held([from_x, from_y], *gate)
        sent = [from_y[:half], from_x[half:]]
        diag_a = self.swap(sent[0], 2)
        diag_b = self.swap(sent[1], 4)
        return [[value], [from_x], [from_y], [diag_a, diag_b]], sent

    def all_blocks(self, pieces):
        blocks = [b[0] if len(b) == 1 else jnp.concatenate(b) for b in pieces]
        if not self.native:
            return blocks
        return [a for b in blocks for a in (b, self.swap(b, 1))]

    def dense_plan(self, rows):
        if not self.native:
            return [(m, 0, rows, 0, m * rows) for m in range(self.nf)], [self.nf * rows]
        h = rows // 2
        order = [(2, 0), (6, 0), (4, h), (6, h), (4, 0), (2, h), (0, 0), (0, h)]
        entries = []
        for core in (0, 1):
            for place, (m, first) in enumerate(order):
                entries.append((m + core, first, h, core, place * h))
        return entries, [8 * h, 8 * h]

    def dense_start(self, arrays, rows, *gate):
        if not self.native:
            return arrays
        mine, other = arrays
        near = after(self.swap(other, 1), *gate)
        h = rows // 2
        spans = [(0, 2), (2, 2), (4, 1), (5, 1), (6, 2)]
        sums = [
            add_low(mine[a * h : (a + n) * h], near[a * h : (a + n) * h]) for a, n in spans
        ]
        return self.reduce_start(sums)

    def plane_plan(self, rows):
        if not self.native:
            return [(m, 0, rows, 0, m * rows) for m in range(self.nf)], [self.nf * rows]
        h = rows // 2
        entries = [(2, 0, h, 0, 0), (6, 0, h, 0, h), (4, h, h, 1, 0), (6, h, h, 1, h)]
        entries += [(4, 0, h, 2, 0), (2, h, h, 3, 0), (0, 0, rows, 4, 0)]
        return entries, [rows, rows, h, h, rows]

    def reduce_start(self, arrays):
        if not self.native:
            return arrays
        to_x, to_y, rest_y, rest_x, own = arrays
        return [self.swap(to_x, 2), self.swap(to_y, 4), rest_y, rest_x, own]

    def reduce_next(self, begun, *gate):
        if not self.native:
            return begun
        got_x, got_y, rest_y, rest_x, own = begun
        if gate:
            got_x, got_y = held([got_x, got_y], *gate)
        h = rest_y.shape[0]
        last_y = add_low(rest_y, got_x[h:])
        last_x = add_low(rest_x, got_y[h:])
        return [got_x, got_y, self.swap(last_y, 4), self.swap(last_x, 2), own, last_y, last_x]

    def reduce_end(self, begun, rows, *gate):
        if not self.native:
            whole = begun[0].reshape((self.nf, rows) + begun[0].shape[1:])
            return lax.psum_scatter(whole, "fsdp", scatter_dimension=0, tiled=False)
        got_x, got_y, last_y, last_x, own = begun[:5]
        if gate:
            last_y, last_x = held([last_y, last_x], *gate)
        h = rows // 2
        return jnp.concatenate(
            [add_low(own[:h], got_x[:h], last_y), add_low(own[h:], got_y[:h], last_x)]
        )


def mm(a, b):
    return lax.dot_general(a, b, (((1,), (0,)), ((), ())), preferred_element_type=F32)


def mm_nt(a, b):
    return lax.dot_general(a, b, (((1,), (1,)), ((), ())), preferred_element_type=F32)


def mm_tn(a, b):
    return lax.dot_general(a, b, (((0,), (0,)), ((), ())), preferred_element_type=F32)


def call(
    kernel, outs, gflop, mbytes, ins=None, grid=(), out_specs=None, scratch=(), aliases=None, spec=None, gate=()
):
    args = dict(
        out_shape=outs,
        input_output_aliases=aliases or {},
        cost_estimate=pl.CostEstimate(
            flops=int(gflop * 5e7), bytes_accessed=int(mbytes * 5e4), transcendentals=0
        ),
        compiler_params=pltpu.CompilerParams(vmem_limit_bytes=VMEM_LIMIT),
    )
    if spec is not None:
        return pl.pallas_call(kernel, grid_spec=spec, **args)
    given, waits = len(ins), len(gate)

    def body(*refs):
        kernel(*refs[:given], *refs[given + waits :])

    args["scratch_shapes"] = list(scratch)
    args["in_specs"] = list(ins) + [pl.BlockSpec(memory_space=pl.ANY)] * waits
    if grid:
        args["grid"] = grid
    if out_specs is not None:
        args["out_specs"] = out_specs
    made = pl.pallas_call(body, **args)
    return lambda *operands: made(*operands, *gate)


SMEM = pl.BlockSpec(memory_space=pltpu.SMEM)
VMEM = pl.BlockSpec(memory_space=pltpu.VMEM)


def shape(dims, dtype):
    return jax.ShapeDtypeStruct(tuple(dims), dtype)


def qkv_kernel(nf, frel, gain, xs, *refs):
    ws = refs[:nf]
    normed, raw, value, sums = refs[nf:]
    width = value.shape[1]
    block = ws[0].shape[0]
    x = xs[...].astype(F32)
    inv = lax.rsqrt(jnp.mean(x * x, axis=-1, keepdims=True) + EPS)
    normed[...] = (x * inv * gain[...]).astype(BF)
    total = None
    for m in range(nf):
        cols = pl.ds(pl.multiple_of(frel[m] * block, block), block)
        term = mm(normed[:, cols], ws[m][:, : 3 * width])
        total = term if total is None else total + term
    q, k = total[:, :width], total[:, width : 2 * width]
    raw[0] = q
    raw[1] = k
    value[...] = total[:, 2 * width :].astype(BF)
    for i, part in enumerate((q, k)):
        column = jnp.sum(part * part, axis=-1, keepdims=True)
        sums[i] = jnp.broadcast_to(column, (column.shape[0], LANES)).T[:8]


def turn(v, cos, sin):
    half = HD // 2
    other = jnp.concatenate([v[:, half:], v[:, :half]], axis=1)
    return v * cos + other * sin


def attend_kernel(scale, raw, value, inv, gain, cos, sin, mask, low, mixed):
    q = turn(raw[0] * inv[0] * gain[0], cos[...], sin[...]).astype(BF)
    k = turn(raw[1] * inv[1] * gain[1], cos[...], sin[...]).astype(BF)
    low[0] = q
    low[1] = k
    scores = jnp.where(mask[...] > 0, mm_nt(q, k) * scale, MASKED)
    top = jnp.max(scores, axis=-1, keepdims=True)
    e = jnp.exp(scores - top)
    probs = e / jnp.sum(e, axis=-1, keepdims=True)
    mixed[...] = mm(probs.astype(BF), value[...]).astype(BF)


def attend_back_kernel(
    scale, raw, low, value, inv, gain, cos, sin, mask, dmixed, u, dv, stats, dgain
):
    q, k, v = low[0], low[1], value[...]
    scores = jnp.where(mask[...] > 0, mm_nt(q, k) * scale, MASKED)
    top = jnp.max(scores, axis=-1, keepdims=True)
    e = jnp.exp(scores - top)
    probs = e / jnp.sum(e, axis=-1, keepdims=True)
    dm = dmixed[...]
    dprobs = mm_nt(dm, v)
    delta = jnp.sum(probs * dprobs, axis=-1, keepdims=True)
    ds = (probs * (dprobs - delta)).astype(BF)
    dv[...] = mm_tn(probs.astype(BF), dm).astype(BF)
    first = pl.program_id(0) == 0
    for i, grad in enumerate((mm(ds, k) * scale, mm_tn(ds, q) * scale)):
        turned = turn(grad, cos[...], -sin[...])
        ui = turned * gain[i]
        u[i] = ui
        line = jnp.sum(turned * raw[i] * inv[i], axis=0, keepdims=True)
        dgain[i] = jnp.broadcast_to(line, (8, line.shape[1]))
        column = jnp.sum(ui * raw[i], axis=-1, keepdims=True)
        flat = jnp.broadcast_to(column, (column.shape[0], LANES)).T[:8]
        stats[i] = jnp.where(first, flat, stats[i] + flat)


def out_kernel(nf, frel, x, gain, mixed, *refs):
    ws = refs[:nf]
    hidden, inv_out, moe, rows = refs[nf:]
    width = mixed.shape[2]
    block = ws[0].shape[0]
    for k in range(mixed.shape[0]):
        rows[:, k * width : (k + 1) * width] = mixed[k]
    total = x[...].astype(F32)
    for m in range(nf):
        cols = pl.ds(pl.multiple_of(frel[m] * block, block), block)
        total = total + mm(rows[:, cols], ws[m][...])
    hidden[...] = total
    inv = lax.rsqrt(jnp.mean(total * total, axis=-1, keepdims=True) + EPS)
    inv_out[...] = jnp.broadcast_to(inv, inv_out.shape)
    moe[...] = (total * inv * gain[...]).astype(BF)


def hidden_back_kernel(nf, nt, frel, hidden, inv_in, moe, g, gain, router, dprob, *refs):
    terms, ws = refs[:nt], refs[nt : nt + nf]
    dhidden, drouter, dgain, low_rows, dmixed, mix_rows = refs[nt + nf :]
    width = dmixed.shape[2]
    block = ws[0].shape[0]
    logits = mm(moe[...], router[...])
    lane = lax.broadcasted_iota(jnp.int32, logits.shape, 1)
    logits = jnp.where(lane < E, logits, MASKED)
    e = jnp.exp(logits - jnp.max(logits, axis=-1, keepdims=True))
    probs = e / jnp.sum(e, axis=-1, keepdims=True)
    dp = dprob[...]
    dlogits = probs * (dp - jnp.sum(probs * dp, axis=-1, keepdims=True))
    high = dlogits.astype(BF)
    rest = (dlogits - high.astype(F32)).astype(BF)
    drouter[...] = mm_tn(moe[...], high) + mm_tn(moe[...], rest)
    dmoe = mm_nt(high, router[...]) + mm_nt(rest, router[...])
    for term in terms:
        dmoe = dmoe + term[...].astype(F32)
    hid = hidden[...]
    inv = inv_in[:, :1]
    u = dmoe * gain[...]
    mean = jnp.mean(u * hid, axis=-1, keepdims=True)
    line = jnp.sum(dmoe * hid * inv, axis=0, keepdims=True)
    dgain[...] = jnp.broadcast_to(line, dgain.shape)
    dh = g[...].astype(F32) + inv * u - hid * (inv * inv * inv) * mean
    dhidden[...] = dh
    low_rows[...] = dh.astype(BF)
    for m in range(nf):
        cols = pl.ds(pl.multiple_of(frel[m] * block, block), block)
        mix_rows[:, cols] = mm_nt(low_rows[...], ws[m][...]).astype(BF)
    for k in range(dmixed.shape[0]):
        dmixed[k] = mix_rows[:, k * width : (k + 1) * width]


def dnormed_kernel(nf, frel, u, raw, inv, mean, dv, x, *refs):
    ws = refs[:nf]
    dqkv, total, line = refs[nf:]
    width = dv.shape[1]
    block = ws[0].shape[0]
    for i in range(2):
        r = inv[i][:, :1]
        b = mean[i][:, :1]
        dqkv[:, i * width : (i + 1) * width] = (r * u[i] - raw[i] * (r * r * r * b)).astype(BF)
    dqkv[:, 2 * width :] = dv[...]
    for m in range(nf):
        cols = pl.ds(pl.multiple_of(frel[m] * block, block), block)
        total[:, cols] = mm_nt(dqkv[...], ws[m][:, : 3 * width]).astype(BF)
    xf = x[...].astype(F32)
    x_inv = lax.rsqrt(jnp.mean(xf * xf, axis=-1, keepdims=True) + EPS)
    terms = jnp.sum(total[...].astype(F32) * xf * x_inv, axis=0, keepdims=True)
    line[...] = jnp.broadcast_to(terms, line.shape)


def place(plan, outs, blocks):
    for m, first, count, which, row in plan:
        outs[which][row : row + count, :] = blocks[m][first : first + count, :]


def place_grad_kernel(nf, plan, frel, left, right, extra, *outs):
    block = left.shape[1] // nf
    for m in range(nf):
        cols = pl.ds(pl.multiple_of(frel[m] * block, block), block)
        term = mm_tn(left[:, cols], right[...]).astype(BF)
        term = jnp.concatenate([term, extra[cols, :]], axis=1)
        place([p for p in plan if p[0] == m], outs, {m: term})


def take_kernel(sizes, experts, slots, *refs):
    cores = slots.shape[1] // (experts * 2 * CAP)
    xs, outs = refs[:-cores], refs[-cores:]
    two = 2 * CAP
    at = 0
    for m, size in enumerate(sizes):
        rows = [r[...] for r in xs[at : at + size]]
        at += size
        got = mm(slots[m], rows[0] if size == 1 else jnp.concatenate(rows, axis=0)).astype(BF)
        for e in range(experts * cores):
            outs[e // experts][e % experts, m * two : (m + 1) * two, :] = got[e * two : (e + 1) * two]


def take_placed_kernel(places, slots, x, out):
    del places
    got = mm(slots[0], x[0]).astype(BF)
    count = got.shape[0] // out.shape[0]
    for e in range(out.shape[0]):
        out[e] = got[e * count : (e + 1) * count]


def put_kernel(blocks, step, plan, slots, *refs):
    cores = step
    rows, outs = refs[:cores], refs[cores:]
    two = 2 * CAP
    for m in range(blocks):
        cut = [
            part[j, m * two : (m + 1) * two, :] for part in rows for j in range(part.shape[0])
        ]
        low = mm(slots[m], jnp.concatenate(cut, axis=0)).astype(BF)
        place([p for p in plan if p[0] == m * step], outs, {m * step: low})


def expert_kernel(halves, cores, first, router, w_in, w_out, *refs):
    xs, gs = refs[:cores], refs[cores : -3 - cores]
    dslots = refs[-3 - cores : -3]
    dproj, inner_out, dgate = refs[-3:]
    xr = jnp.concatenate([r[0] for r in xs], axis=0)
    gr = jnp.concatenate([r[0] for r in gs], axis=0)
    logits = mm(xr, router[...])
    lane = lax.broadcasted_iota(jnp.int32, logits.shape, 1)
    logits = jnp.where(lane < E, logits, MASKED)
    e = jnp.exp(logits - jnp.max(logits, axis=-1, keepdims=True))
    mine = first[0] + pl.program_id(0)
    chosen = jnp.sum(jnp.where(lane == mine, e, 0.0), axis=-1, keepdims=True)
    gate = chosen / jnp.sum(e, axis=-1, keepdims=True)
    back = mm_nt(gr, w_out[0])
    dg = 0.0
    ds = 0.0
    for h in range(halves):
        projected = mm(xr, w_in[h])
        a, up = projected[:, :FH], projected[:, FH:]
        sig = jax.nn.sigmoid(a)
        act = a * sig
        inner = act * up
        b = back[:, h * FH : (h + 1) * FH]
        dg = dg + jnp.sum(inner * b, axis=-1, keepdims=True)
        inner_out[0, :, h * FH : (h + 1) * FH] = (inner * gate).astype(BF)
        db = b * gate
        dproj[h, :, :FH] = (db * up * (sig * (1.0 + a * (1.0 - sig)))).astype(BF)
        dproj[h, :, FH:] = (db * act).astype(BF)
        ds = ds + mm_nt(dproj[h], w_in[h])
    low = ds.astype(BF)
    count = dslots[0].shape[1]
    for i in range(cores):
        dslots[i][0] = low[i * count : (i + 1) * count]
    dgate[0] = jnp.broadcast_to(dg, dgate.shape[1:])


def result_kernel(inner, w_out, *outs):
    low = mm(inner[0], w_out[0]).astype(BF)
    count = outs[0].shape[1]
    for i, out in enumerate(outs):
        out[0] = low[i * count : (i + 1) * count]


def weight_grad_kernel(whole, parts, *refs):
    total = None
    for w, ps in zip(whole, parts):
        at = 0
        for p in ps:
            n = refs[p].shape[1]
            term = (refs[w][0, at : at + n, :], refs[p][0])
            at += n
            term = mm_tn(term[1], term[0]) if w > p else mm_tn(term[0], term[1])
            total = term if total is None else total + term
    refs[-1][0] = total


def rotary_tables(positions):
    half = HD // 2
    frequency = ROPE_BASE ** (-(jnp.arange(half, dtype=F32) * 2.0 / HD))
    angles = positions.astype(F32)[:, None] * frequency[None, :]
    cos, sin = jnp.cos(angles), jnp.sin(angles)
    return jnp.concatenate([cos, cos], axis=1), jnp.concatenate([-sin, sin], axis=1)


def shards(
    tokens,
    doc_starts,
    expert_ids,
    w_query,
    w_key,
    w_value,
    w_attn_out,
    w_router,
    g_attn,
    g_query,
    g_key,
    g_ffn,
    w_in,
    w_out,
    cotangent,
):
    nf, nc = lax.axis_size("fsdp"), lax.axis_size("ctx")
    ndev = nf * nc
    links = Links(nf, nc)
    frel = links.frel
    x_own, g_own = tokens[0], cotangent[0]
    tok, dim = x_own.shape
    seq = tok * nc
    width = dim // nc
    heads = H // nc
    own_rows = w_query.shape[0]
    fsdp_rows = own_rows * nc
    starts = doc_starts[0]

    by_cols = [w.reshape(own_rows, nc, width) for w in (w_query, w_key, w_value)]
    by_cols = jnp.concatenate(by_cols, axis=2).transpose(1, 0, 2)
    per_row = tok * TOP // own_rows
    small_width = -(-(E + 4 + per_row) // LANES) * LANES
    small = [w_router] + [g[:, None] for g in (g_attn, g_query, g_key, g_ffn)]
    small += [expert_ids[0].T.reshape(own_rows, per_row).astype(BF)]
    small += [jnp.zeros((own_rows, small_width - E - 4 - per_row), BF)]
    x_copies = jnp.broadcast_to(x_own, (nc,) + x_own.shape)
    g_copies = jnp.broadcast_to(g_own, (nc,) + g_own.shape)
    to_all = jnp.concatenate([w_attn_out] + small, axis=1)
    to_all = jnp.broadcast_to(to_all, (nc,) + to_all.shape)
    got = links.exchange(jnp.concatenate([by_cols, to_all], axis=2)).reshape(fsdp_rows, -1)
    cols_o = 3 * width + dim
    qkv_rows = jnp.concatenate([got[:, : 3 * width], got[:, cols_o:]], axis=1)
    w_o_rows = got[:, 3 * width : cols_o]
    qkv_begun = links.plane_start(qkv_rows)
    w_qkv = links.all_blocks(links.plane_end(qkv_begun)[0])
    group = 2
    groups = nc // group
    x_all = links.exchange(after(x_copies, got)).reshape(seq, dim)
    w_o_begun = links.plane_start(after(w_o_rows, w_qkv[-1]))
    w_o_pieces, w_o_sent = links.plane_end(w_o_begun)
    small_all = jnp.stack([w[:, 3 * width :] for w in w_qkv])
    small_all = small_all.reshape(nf, nc, own_rows, small_width)
    small_all = links.relative(small_all, planes=True).reshape(dim, small_width)
    router = jnp.where(jnp.arange(LANES) < E, small_all[:, :LANES], 0)
    gains = small_all[:, E : E + 4].T.reshape(4, 1, dim).astype(F32)
    gain_attn, gain_query, gain_key, gain_ffn = gains
    ids_all = small_all[:, E + 4 : E + 4 + per_row].astype(jnp.int32)
    ids_all = ids_all.reshape(nf, nc, TOP, tok)

    normed, raw, value, sums = call(
        functools.partial(qkv_kernel, nf),
        [
            shape((seq, dim), BF),
            shape((2, seq, width), F32),
            shape((seq, width), BF),
            shape((2, 8, seq), F32),
        ],
        3.2,
        13,
        ins=[SMEM] + [VMEM] * (2 + nf),
        gate=w_o_sent,
    )(frel, gain_attn, x_all, *w_qkv)

    w_o = links.all_blocks(w_o_pieces)
    if links.native:
        g_groups = [jnp.concatenate([g_own, links.cswap(after(g_own, sums), 1)])]
    else:
        g_groups = links.slots(g_own)
        g_groups = [jnp.concatenate(g_groups[i * group : (i + 1) * group]) for i in range(groups)]
    g_all = [lax.all_gather(g, "fsdp", axis=0) for g in g_groups]

    def columns(flat):
        return jnp.broadcast_to(flat[:, :, None], (2, seq, LANES))

    sums = jnp.sum(links.gather(sums), axis=0)[:, 0]
    inv = columns(lax.rsqrt(sums / dim + EPS))
    positions = jnp.arange(seq, dtype=jnp.int32)
    cos, sin = rotary_tables(positions)
    head_gain = jnp.stack([gain_query, gain_key]).reshape(2, nc, 1, width)
    head_gain = lax.dynamic_index_in_dim(head_gain, links.c, 1, keepdims=False)
    scale = 1.0 / math.sqrt(HD)
    docs = jnp.sum((starts[None, :] <= positions[:, None]).astype(jnp.int32), axis=1)
    allowed = (positions[None, :] <= positions[:, None]) & (docs[None, :] == docs[:, None])
    mask = allowed.astype(F32)

    def whole(*dims):
        return pl.BlockSpec(dims, lambda h: (0,) * len(dims))

    pair_spec = pl.BlockSpec((2, seq, HD), lambda h: (0, 0, h))
    head_spec = pl.BlockSpec((seq, HD), lambda h: (0, h))
    gain_spec = pl.BlockSpec((2, 1, HD), lambda h: (0, 0, h))
    table_specs = [whole(seq, HD), whole(seq, HD), whole(seq, seq)]
    low, mixed = call(
        functools.partial(attend_kernel, scale),
        [shape((2, seq, width), BF), shape((seq, width), BF)],
        0.6,
        7,
        grid=(heads,),
        ins=[pair_spec, head_spec, whole(2, seq, LANES), gain_spec] + table_specs,
        out_specs=[pair_spec, head_spec],
    )(raw, value, inv, head_gain, cos, sin, mask)
    mixed_rows = links.exchange(mixed.reshape(nc, tok, width))
    pieces = w_in.shape[0]
    halves = min(2, pieces)
    experts = pieces // halves
    device = links.f * nc + links.c
    first_expert = device * pieces // 2
    cores = links.cores
    mine = first_expert + jnp.arange(experts, dtype=jnp.int32)
    theirs = ((links.f ^ 1) * nc + links.c) * pieces // 2 + jnp.arange(experts, dtype=jnp.int32)
    both = jnp.concatenate([mine, theirs]) if cores == 2 else mine
    ids_rel = links.relative(ids_all).transpose(1, 0, 2, 3)
    before = (jnp.arange(tok)[:, None] < jnp.arange(tok)[None, :]).astype(BF)
    ranks = jnp.arange(CAP, dtype=F32)[:, None]

    def slots_of(ids, names):
        named = jnp.any(ids[:, :, None] == names[:, None, None], axis=3)
        rank = jnp.einsum("kmet,ts->kmes", named.astype(BF), before, preferred_element_type=F32)
        return (named[:, :, :, None] & (rank[:, :, :, None] == ranks)).astype(BF)

    blocks = nf // cores
    slots = slots_of(ids_rel[:, ::cores], both)
    slot_sets = [slots[:, :, :experts]]
    if cores == 2:
        slot_sets.append(slots_of(ids_rel[:, 1::2], mine))
    rows_all = experts * cores * group * CAP
    eye = jnp.eye(group, dtype=BF)[:, None, :, None]
    spread = slots.reshape(groups, group, blocks, experts * cores, CAP, tok)
    spread = spread.transpose(0, 2, 3, 1, 4, 5)[:, :, :, :, :, None] * eye
    spread = spread.reshape(groups, blocks, rows_all, group * tok)
    taking = [spread[i] for i in range(groups)]
    placing = []
    for i in range(groups if cores == 1 else 1):
        sets = jnp.stack([s[i * group : (i + 1) * group] for s in slot_sets])
        sets = sets.transpose(0, 2, 3, 1, 4, 5)[:, :, :, :, :, None] * eye
        placing.append(sets.reshape(nf, experts * group * CAP, group * tok))
    putting = [spread[i].transpose(0, 2, 1) for i in range(groups)]
    hidden, inv_ffn, moe_in, mixed_all = call(
        functools.partial(out_kernel, nf),
        [shape((tok, dim), F32), shape((tok, LANES), F32)] + [shape((tok, dim), BF)] * 2,
        1.1,
        12,
        ins=[SMEM] + [VMEM] * (3 + nf),
        gate=taking + putting + placing,
    )(frel, x_own, gain_ffn, mixed_rows, *w_o)

    part = blocks * group * CAP
    nrow = part * cores
    tile = 1024

    def tiles(*dims):
        return pl.BlockSpec(dims[:-1] + (tile,), lambda d: (0,) * (len(dims) - 1) + (d,))

    def fixed(array):
        return pl.BlockSpec(array.shape, lambda d: (0,) * array.ndim)

    def take_rows(i, entries, *gate):
        arrays = [a for entry in entries for a in entry]
        parts = call(
            functools.partial(take_kernel, [len(entry) for entry in entries], experts),
            [shape((experts, part, dim), BF)] * cores,
            1.6,
            8,
            grid=(dim // tile,),
            ins=[fixed(taking[i])] + [tiles(*a.shape) for a in arrays],
            out_specs=[tiles(experts, part, dim)] * cores,
            gate=gate,
        )(taking[i], *arrays)
        if cores == 1:
            return parts
        return [parts[0], links.swap(parts[1], 1)]

    plan, plan_rows = links.plane_plan(group * tok)

    def put_rows(i, parts, *gate):
        if cores == 2:
            parts = [parts[0], links.swap(parts[1], 1)]
        return call(
            functools.partial(put_kernel, blocks, cores, plan),
            [shape((n, dim), BF) for n in plan_rows],
            1.6,
            8,
            grid=(dim // tile,),
            ins=[fixed(putting[i])] + [tiles(experts, part, dim)] * cores,
            out_specs=[tiles(n, dim) for n in plan_rows],
            gate=gate,
        )(putting[i], *parts)

    def grouped(pieces):
        return [jnp.concatenate(pieces[i * group : (i + 1) * group]) for i in range(groups)]

    def take_placed(i, whole):
        order = [m for p in range(cores) for m in range(p, nf, cores)]
        sets = placing[i]
        places = jnp.array(order, jnp.int32)
        places = links.f ^ places if links.native else places
        return call(
            take_placed_kernel,
            shape((experts, nrow, dim), BF),
            0.8,
            12,
            spec=pltpu.PrefetchScalarGridSpec(
                num_scalar_prefetch=1,
                grid=(nf,),
                in_specs=[pl.BlockSpec((1,) + sets.shape[1:], lambda m, at: (m, 0, 0))]
                + [pl.BlockSpec((1, group * tok, dim), lambda m, at: (at[m], 0, 0))],
                out_specs=pl.BlockSpec((experts, group * CAP, dim), lambda m, at: (0, m, 0)),
            ),
        )(places, sets, whole)

    g_rows = [[take_placed(i, g)] for i, g in enumerate(g_all)]

    def pick_far(stacked):
        return [pick(stacked, links.c ^ 2), pick(stacked, links.c ^ 3)]

    if links.native:
        near = links.cswap(moe_in, 1)
        far = links.gather(moe_in, near)
        x_begun = [links.plane_start(jnp.concatenate([moe_in, near]))]
        seen, sent = links.plane_end(x_begun[0], g_rows[0][0])
        far = after(far, *sent)
        g_far = links.exchange(after(g_copies, far))
        x_begun.append(links.plane_start(jnp.concatenate(pick_far(far))))
        x_rows = [take_rows(0, seen, x_begun[1][0])]
    else:
        x_groups = grouped(links.slots(moe_in))
        x_rows = [take_rows(i, links.plane_end(links.plane_start(x))[0]) for i, x in enumerate(x_groups)]
    w_out_e = w_out.reshape(experts, halves * FH, dim)
    inner_width = halves * FH

    def by_expert(*dims):
        return pl.BlockSpec(dims, lambda j: (j,) + (0,) * (len(dims) - 1))

    dtile = 512
    n = groups * cores
    of_group = [list(range(i * cores, (i + 1) * cores)) for i in range(groups)]

    def grad_out_pieces(inners, g_rows, *gate):
        flat = [a for parts in g_rows for a in parts]
        g_parts, at = [], groups
        for parts in g_rows:
            g_parts.append(list(range(at, at + len(parts))))
            at += len(parts)
        return call(
            functools.partial(
                weight_grad_kernel,
                list(range(groups)),
                g_parts,
            ),
            shape(w_out_e.shape, F32),
            6.5,
            26,
            grid=(experts, halves),
            ins=[pl.BlockSpec((1, nrow, FH), lambda j, h: (j, 0, h))] * groups
            + [pl.BlockSpec((1, g.shape[1], dim), lambda j, h: (j, 0, 0)) for g in flat],
            out_specs=pl.BlockSpec((1, FH, dim), lambda j, h: (j, h, 0)),
            gate=gate,
        )(*inners, *flat)

    def grad_in_pieces(j, total, *gate):
        flat = [a for parts in x_rows for a in parts]
        return call(
            functools.partial(weight_grad_kernel, [n + i for i in range(groups)], of_group),
            shape(w_in.shape, F32),
            6.5,
            25,
            grid=(halves, dim // dtile),
            ins=[pl.BlockSpec((1, part, dtile), lambda p, d: (j, 0, d))] * n
            + [pl.BlockSpec((1, nrow, 2 * FH), lambda p, d: (j * halves + p, 0, 0))] * groups
            + [pl.BlockSpec(memory_space=pl.ANY)] * (j > 0),
            out_specs=pl.BlockSpec((1, dtile, 2 * FH), lambda p, d: (j * halves + p, d, 0)),
            aliases={n + groups: 0} if j else {},
            gate=gate,
        )(*flat, *dprojs, *([total] if j else []))

    def expert(i, *gate):
        rows_in = [by_expert(1, part, dim)] * cores
        return call(
            functools.partial(expert_kernel, halves, cores),
            [shape((experts, part, dim), BF)] * cores
            + [
                shape((pieces, nrow, 2 * FH), BF),
                shape((experts, nrow, inner_width), BF),
                shape((experts, nrow, LANES), F32),
            ],
            34,
            30,
            grid=(experts,),
            ins=[
                SMEM,
                pl.BlockSpec((dim, LANES), lambda j: (0, 0)),
                by_expert(halves, dim, 2 * FH),
                by_expert(1, inner_width, dim),
            ]
            + rows_in
            + [by_expert(1, g.shape[1], dim) for g in g_rows[i]],
            out_specs=rows_in
            + [
                by_expert(halves, nrow, 2 * FH),
                by_expert(1, nrow, inner_width),
                by_expert(1, nrow, LANES),
            ],
            gate=gate,
        )(first_expert.reshape(1), router, w_in, w_out_e, *x_rows[i], *g_rows[i])

    def result(inner, *gate):
        return call(
            result_kernel,
            [shape((experts, part, dim), BF)] * cores,
            3.4,
            14,
            grid=(experts,),
            ins=[by_expert(1, nrow, inner_width), by_expert(1, inner_width, dim)],
            out_specs=[by_expert(1, part, dim)] * cores,
            gate=gate,
        )(inner, w_out_e)

    def cut_group(total):
        return [total[b * tok : (b + 1) * tok] for b in range(group)]

    done, begun, more, totals = [], [], [], []
    last = x_rows[0][0]
    for i in range(groups):
        done.append(expert(i, last))
        if links.native and i == 0:
            pieces_x, sent = links.plane_end(x_begun[1], done[0][0])
            g_begun = links.plane_start(jnp.concatenate(pick_far(after(g_far, *sent))))
            arrays = put_rows(0, done[0][:cores], g_begun[0])
            x_rows.append(take_rows(1, pieces_x, arrays[0]))
            pieces_g, sent = links.plane_end(g_begun, x_rows[1][0])
            arrays = held(arrays, *sent)
            g_rows.append(take_rows(1, pieces_g))
            last = g_rows[1][0]
        elif i == 1:
            more.append(links.reduce_next(begun[0], done[1][0]))
            arrays = put_rows(1, done[1][:cores], *more[0][-2:])
            last = arrays[0]
        else:
            arrays = put_rows(i, done[i][:cores], done[i][0])
            last = arrays[0]
        begun.append(links.reduce_start(arrays))
    dgate = jnp.stack([d[cores + 2][:, :, 0] for d in done], axis=1)
    dgate = dgate.reshape(experts, groups, cores, blocks, group, CAP).transpose(2, 1, 4, 3, 0, 5)
    dgate = dgate.reshape(cores, nc, blocks, experts, CAP, 1)
    dgate_tok = jnp.stack(
        [jnp.sum(s.astype(F32) * d, axis=3) for s, d in zip(slot_sets, dgate)], axis=2
    ).reshape(nc, nf, experts, tok)
    dgate_tok = links.relative(dgate_tok.transpose(1, 0, 2, 3))
    dgate_back = lax.all_to_all(
        dgate_tok.reshape(ndev, experts, tok), ALL, split_axis=0, concat_axis=0, tiled=True
    )
    results, out_arrays, out_begun = [], [], []
    for i in range(groups):
        results.append(result(done[i][cores + 1], last))
        last = results[i][0]
    totals.append(links.reduce_end(more[0], group * tok, last))
    out_arrays.append(put_rows(0, results[0], totals[0]))
    last = out_arrays[0][0]
    for i in range(1, groups):
        more.append(links.reduce_next(begun[i], last))
        last = more[i][-1]
        out_begun.append(links.reduce_start(held(out_arrays[i - 1], last)))
        out_arrays.append(put_rows(i, results[i], last))
        last = out_arrays[i][0]
    dprojs = [d[cores] for d in done]
    inners = [d[cores + 1] for d in done]
    for i in range(1, groups):
        totals.append(links.reduce_end(more[i], group * tok, last))
        last = totals[i]
    dmoe_terms = links.sum_slots([t for total in totals for t in cut_group(total)])
    grad_w_out = grad_out_pieces(inners, g_rows, last)
    out_begun.append(links.reduce_start(held(out_arrays[-1], grad_w_out)))
    dmoe_terms = held(dmoe_terms, grad_w_out)
    dgate_back = after(dgate_back, grad_w_out)
    dprob = jnp.sum(dgate_back.reshape(E, ndev * experts // E, tok), axis=1).T
    dprob = jnp.pad(dprob, ((0, 0), (0, LANES - E)))

    back = call(
        functools.partial(hidden_back_kernel, nf, len(dmoe_terms)),
        [shape((tok, dim), F32), shape((dim, LANES), F32), shape((8, dim), F32)]
        + [shape((tok, dim), BF), shape((nc, tok, width), BF)],
        1.3,
        15,
        ins=[SMEM] + [VMEM] * (7 + len(dmoe_terms) + nf),
        scratch=[pltpu.VMEM((tok, dim), BF)],
    )(frel, hidden, inv_ffn, moe_in, g_own, gain_ffn, router, dprob, *dmoe_terms, *w_o)
    dhidden, grad_router, grad_gain_ffn, dlow, dmixed = back
    dmixed = links.exchange(dmixed)
    grad_plan, grad_rows = links.dense_plan(fsdp_rows)

    def dense_terms(left, right, extra, *gate):
        return call(
            functools.partial(place_grad_kernel, nf, grad_plan),
            [shape((r, right.shape[1] + LANES), BF) for r in grad_rows],
            right.shape[0] * right.shape[1] * dim * 2e-9,
            right.shape[1] * dim * 2e-6,
            ins=[SMEM, VMEM, VMEM, VMEM],
            gate=gate,
        )(frel, left, right, extra)

    last = dlow
    out_more = []
    for b in out_begun:
        out_more.append(links.reduce_next(b, last))
        last = out_more[-1][-1]
    grad_w_in = grad_in_pieces(0, None, last)
    last = grad_w_in
    dmixed = after(dmixed, last).reshape(seq, width)

    u, dvalue, stats, dgain = call(
        functools.partial(attend_back_kernel, scale),
        [
            shape((2, seq, width), F32),
            shape((seq, width), BF),
            shape((2, 8, seq), F32),
            shape((2, 8, width), F32),
        ],
        1.4,
        10,
        grid=(heads,),
        ins=[pair_spec, pair_spec, head_spec, whole(2, seq, LANES), gain_spec]
        + table_specs
        + [head_spec],
        out_specs=[
            pair_spec,
            head_spec,
            whole(2, 8, seq),
            pl.BlockSpec((2, 8, HD), lambda h: (0, 0, h)),
        ],
    )(raw, low, value, inv, head_gain, cos, sin, mask, dmixed)
    with_ffn = jnp.where(jnp.arange(LANES) == E, grad_gain_ffn[0][:, None], grad_router)
    grad_o_terms = dense_terms(mixed_all, dlow, with_ffn.astype(BF), stats)
    mean = columns(jnp.sum(links.gather(stats), axis=0)[:, 0] / dim)
    last = grad_o_terms[0]
    out_totals = []
    for m in out_more:
        out_totals.append(links.reduce_end(m, group * tok, last))
        last = out_totals[-1]
    out_terms = links.sum_slots([t for o in out_totals for t in cut_group(o)])
    mean = after(mean, last)
    dqkv, dnormed_terms, dgain_attn = call(
        functools.partial(dnormed_kernel, nf),
        [shape((seq, 3 * width), BF), shape((seq, dim), BF), shape((8, dim), F32)],
        3.3,
        15,
        ins=[SMEM] + [VMEM] * (6 + nf),
    )(frel, u, raw, inv, mean, dvalue, x_all, *w_qkv)
    dnormed_terms = links.exchange(dnormed_terms.reshape(nc, tok, dim))

    def placed(vector):
        return lax.dynamic_update_slice(jnp.zeros((dim,), F32), vector, (links.c * width,))

    grad_o_begun = links.dense_start(grad_o_terms, fsdp_rows, dqkv)
    gain_terms = jnp.stack([dgain_attn[0], placed(dgain[0, 0]), placed(dgain[1, 0])])
    gain_terms = jnp.pad(gain_terms.astype(BF), ((0, LANES - 3), (0, 0))).T
    grad_qkv_terms = dense_terms(normed, dqkv, gain_terms, *grad_o_begun[2:3])
    grad_qkv_begun = links.dense_start(grad_qkv_terms, fsdp_rows, grad_qkv_terms[0])
    last = grad_qkv_begun[-1]
    for j in range(1, experts):
        grad_w_in = grad_in_pieces(j, grad_w_in, last)
        last = grad_w_in
    grad_o_more = links.reduce_next(grad_o_begun, last)
    grad_qkv_more = links.reduce_next(grad_qkv_begun, grad_o_more[-1])
    out_terms = held(out_terms, grad_qkv_more[-1])
    grad_o_total = links.reduce_end(grad_o_more, fsdp_rows, out_terms[-1])
    grad_o = links.exchange(grad_o_total.reshape(nc, own_rows, -1))
    grad_qkv_total = links.reduce_end(grad_qkv_more, fsdp_rows, grad_o_total)
    dnormed_terms = after(dnormed_terms, grad_qkv_total)
    dnormed = jnp.sum(dnormed_terms.astype(F32), axis=0)
    x_float = x_own.astype(F32)
    x_inv = lax.rsqrt(jnp.mean(x_float * x_float, axis=-1, keepdims=True) + EPS)
    ux = dnormed * gain_attn
    x_mean = jnp.mean(ux * x_float, axis=-1, keepdims=True)
    input_grad = (dhidden + x_inv * ux - x_float * x_inv**3 * x_mean)[None]

    output = (hidden + sum(t.astype(F32) for t in out_terms)).astype(BF)
    grad_o = jnp.sum(grad_o.astype(F32), axis=0)
    grad_attn_out, router_sum = grad_o[:, :dim], grad_o[:, dim:]
    grad_qkv = links.exchange(grad_qkv_total.reshape(nc, own_rows, -1)).astype(F32)
    gain_sum = jnp.sum(grad_qkv[:, :, 3 * width :], axis=0).T
    grad_dense = grad_qkv[:, :, : 3 * width].reshape(nc, own_rows, 3, width).transpose(2, 1, 0, 3)
    grad_dense = grad_dense.reshape(3, own_rows, dim)
    return (
        output[None],
        input_grad,
        grad_dense[0],
        grad_dense[1],
        grad_dense[2],
        grad_attn_out,
        router_sum[:, :E],
        gain_sum[0],
        gain_sum[1],
        gain_sum[2],
        router_sum[:, E],
        grad_w_in,
        grad_w_out.reshape(w_out.shape),
    )


def solution(mesh):
    rows = P(ALL, None)
    vec = P(ALL)
    cube = P(ALL, None, None)
    stream = P("fsdp", "ctx", None)
    weights = (rows,) * 5 + (vec,) * 4 + (cube,) * 2
    return jax.shard_map(
        shards,
        mesh=mesh,
        in_specs=(stream, P("fsdp", None), stream) + weights + (stream,),
        out_specs=(stream, stream) + weights,
        check_vma=False,
    )
```

```python
import functools
import math

import jax
import jax.numpy as jnp
from jax import lax
from jax.experimental import pallas as pl
from jax.experimental.pallas import tpu as pltpu
from jax.sharding import PartitionSpec as P

H = 16
HD = 128
E = 64
TOP = 8
FH = 512
CAP = 24

EPS = 1e-05
MASKED = -1e30
ROPE_BASE = 10000.0
HIGHEST = lax.Precision.HIGHEST
F32 = jnp.float32
BF = jnp.bfloat16
ALL = ("fsdp", "ctx")
LANES = 128
VMEM_LIMIT = 60 * 1024 * 1024


def pick(stacked, index):
    return lax.dynamic_index_in_dim(stacked, index, 0, keepdims=False)


def after(value, *others):
    return held([value], *others)[0]


def held(values, *others):
    if not others:
        return list(values)
    values = list(values)
    anywhere = pl.BlockSpec(memory_space=pl.ANY)
    done = pl.pallas_call(
        lambda *refs: None,
        out_shape=[jax.ShapeDtypeStruct(v.shape, v.dtype) for v in values],
        in_specs=[anywhere] * (len(values) + len(others)),
        out_specs=[anywhere] * len(values),
        input_output_aliases={i: i for i in range(len(values))},
    )(*values, *others)
    return list(done)


def held_pieces(blocks, *gate):
    flat = held([a for b in blocks for a in b], *gate)
    return [[flat.pop(0) for _ in b] for b in blocks]


def add_low(*terms):
    return sum(t.astype(F32) for t in terms).astype(BF)


class Links:
    def __init__(self, nf, nc):
        self.nf, self.nc = nf, nc
        self.native = nf == 8 and nc == 4
        self.cores = 2 if self.native else 1
        self.f = lax.axis_index("fsdp")
        self.c = lax.axis_index("ctx")
        ms = jnp.arange(nf, dtype=jnp.int32)
        self.frel = self.f ^ ms if self.native else ms

    def swap(self, value, mask):
        return lax.ppermute(value, "fsdp", [(i, i ^ mask) for i in range(self.nf)])

    def cswap(self, value, mask):
        return lax.ppermute(value, "ctx", [(i, i ^ mask) for i in range(self.nc)])

    def exchange(self, value):
        return lax.all_to_all(value, "ctx", split_axis=0, concat_axis=0, tiled=True)

    def gather(self, value, *gate):
        return self.exchange(after(jnp.broadcast_to(value, (self.nc,) + value.shape), *gate))

    def slots(self, value):
        if not self.native:
            whole = lax.all_gather(value, "ctx", axis=0)
            return [whole[k] for k in range(self.nc)]
        return [value] + [self.cswap(value, k) for k in range(1, self.nc)]

    def sum_slots(self, parts):
        if not self.native:
            whole = jnp.stack(parts)
            return [lax.psum_scatter(whole, "ctx", scatter_dimension=0, tiled=False)]
        return [parts[0]] + [self.cswap(parts[k], k) for k in range(1, self.nc)]

    def sum_at_once(self, parts):
        whole = jnp.stack(parts)
        if not self.native:
            return lax.psum_scatter(whole, "ctx", scatter_dimension=0, tiled=True)
        for bit in (1, 2):
            flipped = jnp.stack([whole[k ^ bit] for k in range(self.nc)])
            whole = jnp.where((self.c & bit) > 0, flipped, whole)
        return self.exchange(whole)

    def relative(self, value, planes=False):
        if not self.native:
            return value
        dims = value.shape
        for bit, place in ((4, self.f), (2, self.f), (1, self.f), (2, self.c), (1, self.c)):
            lead = 0 if place is self.f else 1
            if lead and planes:
                continue
            n = dims[lead]
            split = dims[:lead] + (n // (2 * bit), 2, bit) + dims[lead + 1 :]
            cut = value.reshape(split)
            parts = jnp.split(cut, 2, axis=lead + 1)
            flipped = jnp.concatenate(parts[::-1], axis=lead + 1)
            value = jnp.where((place & bit) > 0, flipped, cut).reshape(dims)
        return value

    def plane_start(self, value):
        if not self.native:
            return [value]
        return [value, self.swap(value, 2), self.swap(value, 4)]

    def plane_end(self, begun, *gate):
        if not self.native:
            whole = lax.all_gather(begun[0], "fsdp", axis=0)
            return [[whole[m]] for m in range(self.nf)], begun
        value, from_x, from_y = begun
        half = value.shape[0] // 2
        from_x, from_y = held([from_x, from_y], *gate)
        sent = [from_y[:half], from_x[half:]]
        diag_a = self.swap(sent[0], 2)
        diag_b = self.swap(sent[1], 4)
        return [[value], [from_x], [from_y], [diag_a, diag_b]], sent

    def all_blocks(self, pieces):
        blocks = [b[0] if len(b) == 1 else jnp.concatenate(b) for b in pieces]
        if not self.native:
            return blocks
        return [a for b in blocks for a in (b, self.swap(b, 1))]

    def dense_plan(self, rows):
        if not self.native:
            return [(m, 0, rows, 0, m * rows) for m in range(self.nf)], [self.nf * rows]
        h = rows // 2
        order = [(2, 0), (6, 0), (4, h), (6, h), (4, 0), (2, h), (0, 0), (0, h)]
        entries = []
        for core in (0, 1):
            for place, (m, first) in enumerate(order):
                entries.append((m + core, first, h, core, place * h))
        return entries, [8 * h, 8 * h]

    def dense_start(self, arrays, rows, *gate):
        if not self.native:
            return arrays
        mine, other = arrays
        near = after(self.swap(other, 1), *gate)
        h = rows // 2
        spans = [(0, 2), (2, 2), (4, 1), (5, 1), (6, 2)]
        sums = [
            add_low(mine[a * h : (a + n) * h], near[a * h : (a + n) * h]) for a, n in spans
        ]
        return self.reduce_start(sums)

    def plane_plan(self, rows):
        if not self.native:
            return [(m, 0, rows, 0, m * rows) for m in range(self.nf)], [self.nf * rows]
        h = rows // 2
        entries = [(2, 0, h, 0, 0), (6, 0, h, 0, h), (4, h, h, 1, 0), (6, h, h, 1, h)]
        entries += [(4, 0, h, 2, 0), (2, h, h, 3, 0), (0, 0, rows, 4, 0)]
        return entries, [rows, rows, h, h, rows]

    def reduce_start(self, arrays):
        if not self.native:
            return arrays
        to_x, to_y, rest_y, rest_x, own = arrays
        return [self.swap(to_x, 2), self.swap(to_y, 4), rest_y, rest_x, own]

    def reduce_next(self, begun, *gate):
        if not self.native:
            return begun
        got_x, got_y, rest_y, rest_x, own = begun
        if gate:
            got_x, got_y = held([got_x, got_y], *gate)
        h = rest_y.shape[0]
        last_y = add_low(rest_y, got_x[h:])
        last_x = add_low(rest_x, got_y[h:])
        return [got_x, got_y, self.swap(last_y, 4), self.swap(last_x, 2), own, last_y, last_x]

    def reduce_end(self, begun, rows, *gate):
        if not self.native:
            whole = begun[0].reshape((self.nf, rows) + begun[0].shape[1:])
            return lax.psum_scatter(whole, "fsdp", scatter_dimension=0, tiled=False)
        got_x, got_y, last_y, last_x, own = begun[:5]
        if gate:
            last_y, last_x = held([last_y, last_x], *gate)
        h = rows // 2
        return jnp.concatenate(
            [add_low(own[:h], got_x[:h], last_y), add_low(own[h:], got_y[:h], last_x)]
        )


def mm(a, b):
    return lax.dot_general(a, b, (((1,), (0,)), ((), ())), preferred_element_type=F32)


def mm_nt(a, b):
    return lax.dot_general(a, b, (((1,), (1,)), ((), ())), preferred_element_type=F32)


def mm_tn(a, b):
    return lax.dot_general(a, b, (((0,), (0,)), ((), ())), preferred_element_type=F32)


def call(
    kernel, outs, gflop, mbytes, ins=None, grid=(), out_specs=None, scratch=(), aliases=None, spec=None, gate=()
):
    args = dict(
        out_shape=outs,
        input_output_aliases=aliases or {},
        cost_estimate=pl.CostEstimate(
            flops=int(gflop * 5e7), bytes_accessed=int(mbytes * 5e4), transcendentals=0
        ),
        compiler_params=pltpu.CompilerParams(vmem_limit_bytes=VMEM_LIMIT),
    )
    if spec is not None:
        return pl.pallas_call(kernel, grid_spec=spec, **args)
    given, waits = len(ins), len(gate)

    def body(*refs):
        kernel(*refs[:given], *refs[given + waits :])

    args["scratch_shapes"] = list(scratch)
    args["in_specs"] = list(ins) + [pl.BlockSpec(memory_space=pl.ANY)] * waits
    if grid:
        args["grid"] = grid
    if out_specs is not None:
        args["out_specs"] = out_specs
    made = pl.pallas_call(body, **args)
    return lambda *operands: made(*operands, *gate)


SMEM = pl.BlockSpec(memory_space=pltpu.SMEM)
VMEM = pl.BlockSpec(memory_space=pltpu.VMEM)


def shape(dims, dtype):
    return jax.ShapeDtypeStruct(tuple(dims), dtype)


def qkv_kernel(nf, frel, gain, xs, *refs):
    ws = refs[:nf]
    normed, raw, value, sums = refs[nf:]
    width = value.shape[1]
    block = ws[0].shape[0]
    x = xs[...].astype(F32)
    inv = lax.rsqrt(jnp.mean(x * x, axis=-1, keepdims=True) + EPS)
    normed[...] = (x * inv * gain[...]).astype(BF)
    total = None
    for m in range(nf):
        cols = pl.ds(pl.multiple_of(frel[m] * block, block), block)
        term = mm(normed[:, cols], ws[m][:, : 3 * width])
        total = term if total is None else total + term
    q, k = total[:, :width], total[:, width : 2 * width]
    raw[0] = q
    raw[1] = k
    value[...] = total[:, 2 * width :].astype(BF)
    for i, part in enumerate((q, k)):
        column = jnp.sum(part * part, axis=-1, keepdims=True)
        sums[i] = jnp.broadcast_to(column, (column.shape[0], LANES)).T[:8]


def turn(v, cos, sin):
    half = HD // 2
    other = jnp.concatenate([v[:, half:], v[:, :half]], axis=1)
    return v * cos + other * sin


def attend_kernel(scale, raw, value, inv, gain, cos, sin, mask, low, mixed):
    q = turn(raw[0] * inv[0] * gain[0], cos[...], sin[...]).astype(BF)
    k = turn(raw[1] * inv[1] * gain[1], cos[...], sin[...]).astype(BF)
    low[0] = q
    low[1] = k
    scores = jnp.where(mask[...] > 0, mm_nt(q, k) * scale, MASKED)
    top = jnp.max(scores, axis=-1, keepdims=True)
    e = jnp.exp(scores - top)
    probs = e / jnp.sum(e, axis=-1, keepdims=True)
    mixed[...] = mm(probs.astype(BF), value[...]).astype(BF)


def attend_back_kernel(
    scale, raw, low, value, inv, gain, cos, sin, mask, dmixed, u, dv, stats, dgain
):
    q, k, v = low[0], low[1], value[...]
    scores = jnp.where(mask[...] > 0, mm_nt(q, k) * scale, MASKED)
    top = jnp.max(scores, axis=-1, keepdims=True)
    e = jnp.exp(scores - top)
    probs = e / jnp.sum(e, axis=-1, keepdims=True)
    dm = dmixed[...]
    dprobs = mm_nt(dm, v)
    delta = jnp.sum(probs * dprobs, axis=-1, keepdims=True)
    ds = (probs * (dprobs - delta)).astype(BF)
    dv[...] = mm_tn(probs.astype(BF), dm).astype(BF)
    first = pl.program_id(0) == 0
    for i, grad in enumerate((mm(ds, k) * scale, mm_tn(ds, q) * scale)):
        turned = turn(grad, cos[...], -sin[...])
        ui = turned * gain[i]
        u[i] = ui
        line = jnp.sum(turned * raw[i] * inv[i], axis=0, keepdims=True)
        dgain[i] = jnp.broadcast_to(line, (8, line.shape[1]))
        column = jnp.sum(ui * raw[i], axis=-1, keepdims=True)
        flat = jnp.broadcast_to(column, (column.shape[0], LANES)).T[:8]
        stats[i] = jnp.where(first, flat, stats[i] + flat)


def out_kernel(nf, frel, x, gain, mixed, *refs):
    ws = refs[:nf]
    hidden, inv_out, moe, rows = refs[nf:]
    width = mixed.shape[2]
    block = ws[0].shape[0]
    for k in range(mixed.shape[0]):
        rows[:, k * width : (k + 1) * width] = mixed[k]
    total = x[...].astype(F32)
    for m in range(nf):
        cols = pl.ds(pl.multiple_of(frel[m] * block, block), block)
        total = total + mm(rows[:, cols], ws[m][...])
    hidden[...] = total
    inv = lax.rsqrt(jnp.mean(total * total, axis=-1, keepdims=True) + EPS)
    inv_out[...] = jnp.broadcast_to(inv, inv_out.shape)
    moe[...] = (total * inv * gain[...]).astype(BF)


def hidden_back_kernel(nf, nt, frel, hidden, inv_in, moe, g, gain, router, dprob, *refs):
    terms, ws = refs[:nt], refs[nt : nt + nf]
    dhidden, drouter, dgain, low_rows, dmixed, mix_rows = refs[nt + nf :]
    width = dmixed.shape[2]
    block = ws[0].shape[0]
    logits = mm(moe[...], router[...])
    lane = lax.broadcasted_iota(jnp.int32, logits.shape, 1)
    logits = jnp.where(lane < E, logits, MASKED)
    e = jnp.exp(logits - jnp.max(logits, axis=-1, keepdims=True))
    probs = e / jnp.sum(e, axis=-1, keepdims=True)
    dp = dprob[...]
    dlogits = probs * (dp - jnp.sum(probs * dp, axis=-1, keepdims=True))
    high = dlogits.astype(BF)
    rest = (dlogits - high.astype(F32)).astype(BF)
    drouter[...] = mm_tn(moe[...], high) + mm_tn(moe[...], rest)
    dmoe = mm_nt(high, router[...]) + mm_nt(rest, router[...])
    for term in terms:
        dmoe = dmoe + term[...].astype(F32)
    hid = hidden[...]
    inv = inv_in[:, :1]
    u = dmoe * gain[...]
    mean = jnp.mean(u * hid, axis=-1, keepdims=True)
    line = jnp.sum(dmoe * hid * inv, axis=0, keepdims=True)
    dgain[...] = jnp.broadcast_to(line, dgain.shape)
    dh = g[...].astype(F32) + inv * u - hid * (inv * inv * inv) * mean
    dhidden[...] = dh
    low_rows[...] = dh.astype(BF)
    for m in range(nf):
        cols = pl.ds(pl.multiple_of(frel[m] * block, block), block)
        mix_rows[:, cols] = mm_nt(low_rows[...], ws[m][...]).astype(BF)
    for k in range(dmixed.shape[0]):
        dmixed[k] = mix_rows[:, k * width : (k + 1) * width]


def dnormed_kernel(nf, frel, u, raw, inv, mean, dv, x, *refs):
    ws = refs[:nf]
    dqkv, total, line = refs[nf:]
    width = dv.shape[1]
    block = ws[0].shape[0]
    for i in range(2):
        r = inv[i][:, :1]
        b = mean[i][:, :1]
        dqkv[:, i * width : (i + 1) * width] = (r * u[i] - raw[i] * (r * r * r * b)).astype(BF)
    dqkv[:, 2 * width :] = dv[...]
    for m in range(nf):
        cols = pl.ds(pl.multiple_of(frel[m] * block, block), block)
        total[:, cols] = mm_nt(dqkv[...], ws[m][:, : 3 * width]).astype(BF)
    xf = x[...].astype(F32)
    x_inv = lax.rsqrt(jnp.mean(xf * xf, axis=-1, keepdims=True) + EPS)
    terms = jnp.sum(total[...].astype(F32) * xf * x_inv, axis=0, keepdims=True)
    line[...] = jnp.broadcast_to(terms, line.shape)


def place(plan, outs, blocks):
    for m, first, count, which, row in plan:
        outs[which][row : row + count, :] = blocks[m][first : first + count, :]


def place_grad_kernel(nf, plan, frel, left, right, extra, *outs):
    block = left.shape[1] // nf
    for m in range(nf):
        cols = pl.ds(pl.multiple_of(frel[m] * block, block), block)
        term = mm_tn(left[:, cols], right[...]).astype(BF)
        term = jnp.concatenate([term, extra[cols, :]], axis=1)
        place([p for p in plan if p[0] == m], outs, {m: term})


def take_kernel(sizes, experts, slots, *refs):
    cores = slots.shape[1] // (experts * 2 * CAP)
    xs, outs = refs[:-cores], refs[-cores:]
    two = 2 * CAP
    at = 0
    for m, size in enumerate(sizes):
        rows = [r[...] for r in xs[at : at + size]]
        at += size
        got = mm(slots[m], rows[0] if size == 1 else jnp.concatenate(rows, axis=0)).astype(BF)
        for e in range(experts * cores):
            outs[e // experts][e % experts, m * two : (m + 1) * two, :] = got[e * two : (e + 1) * two]


def take_placed_kernel(places, slots, x, out):
    del places
    got = mm(slots[0], x[0]).astype(BF)
    count = got.shape[0] // out.shape[0]
    for e in range(out.shape[0]):
        out[e] = got[e * count : (e + 1) * count]


def put_kernel(blocks, step, plan, slots, *refs):
    cores = step
    rows, outs = refs[:cores], refs[cores:]
    two = 2 * CAP
    for m in range(blocks):
        cut = [
            part[j, m * two : (m + 1) * two, :] for part in rows for j in range(part.shape[0])
        ]
        low = mm(slots[m], jnp.concatenate(cut, axis=0)).astype(BF)
        place([p for p in plan if p[0] == m * step], outs, {m * step: low})


def expert_kernel(halves, cores, first, router, w_in, w_out, *refs):
    xs, gs = refs[:cores], refs[cores : -3 - cores]
    dslots = refs[-3 - cores : -3]
    dproj, inner_out, dgate = refs[-3:]
    xr = jnp.concatenate([r[0] for r in xs], axis=0)
    gr = jnp.concatenate([r[0] for r in gs], axis=0)
    logits = mm(xr, router[...])
    lane = lax.broadcasted_iota(jnp.int32, logits.shape, 1)
    logits = jnp.where(lane < E, logits, MASKED)
    e = jnp.exp(logits - jnp.max(logits, axis=-1, keepdims=True))
    mine = first[0] + pl.program_id(0)
    chosen = jnp.sum(jnp.where(lane == mine, e, 0.0), axis=-1, keepdims=True)
    gate = chosen / jnp.sum(e, axis=-1, keepdims=True)
    back = mm_nt(gr, w_out[0])
    dg = 0.0
    ds = 0.0
    for h in range(halves):
        projected = mm(xr, w_in[h])
        a, up = projected[:, :FH], projected[:, FH:]
        sig = jax.nn.sigmoid(a)
        act = a * sig
        inner = act * up
        b = back[:, h * FH : (h + 1) * FH]
        dg = dg + jnp.sum(inner * b, axis=-1, keepdims=True)
        inner_out[0, :, h * FH : (h + 1) * FH] = (inner * gate).astype(BF)
        db = b * gate
        dproj[h, :, :FH] = (db * up * (sig * (1.0 + a * (1.0 - sig)))).astype(BF)
        dproj[h, :, FH:] = (db * act).astype(BF)
        ds = ds + mm_nt(dproj[h], w_in[h])
    low = ds.astype(BF)
    count = dslots[0].shape[1]
    for i in range(cores):
        dslots[i][0] = low[i * count : (i + 1) * count]
    dgate[0] = jnp.broadcast_to(dg, dgate.shape[1:])


def result_kernel(inner, w_out, *outs):
    low = mm(inner[0], w_out[0]).astype(BF)
    count = outs[0].shape[1]
    for i, out in enumerate(outs):
        out[0] = low[i * count : (i + 1) * count]


def weight_grad_kernel(whole, parts, *refs):
    total = None
    for w, ps in zip(whole, parts):
        at = 0
        for p in ps:
            n = refs[p].shape[1]
            term = (refs[w][0, at : at + n, :], refs[p][0])
            at += n
            term = mm_tn(term[1], term[0]) if w > p else mm_tn(term[0], term[1])
            total = term if total is None else total + term
    refs[-1][0] = total


def rotary_tables(positions):
    half = HD // 2
    frequency = ROPE_BASE ** (-(jnp.arange(half, dtype=F32) * 2.0 / HD))
    angles = positions.astype(F32)[:, None] * frequency[None, :]
    cos, sin = jnp.cos(angles), jnp.sin(angles)
    return jnp.concatenate([cos, cos], axis=1), jnp.concatenate([-sin, sin], axis=1)


def shards(
    tokens,
    doc_starts,
    expert_ids,
    w_query,
    w_key,
    w_value,
    w_attn_out,
    w_router,
    g_attn,
    g_query,
    g_key,
    g_ffn,
    w_in,
    w_out,
    cotangent,
):
    nf, nc = lax.axis_size("fsdp"), lax.axis_size("ctx")
    ndev = nf * nc
    links = Links(nf, nc)
    frel = links.frel
    x_own, g_own = tokens[0], cotangent[0]
    tok, dim = x_own.shape
    seq = tok * nc
    width = dim // nc
    heads = H // nc
    own_rows = w_query.shape[0]
    fsdp_rows = own_rows * nc
    starts = doc_starts[0]

    by_cols = [w.reshape(own_rows, nc, width) for w in (w_query, w_key, w_value)]
    by_cols = jnp.concatenate(by_cols, axis=2).transpose(1, 0, 2)
    per_row = tok * TOP // own_rows
    small_width = -(-(E + 4 + per_row) // LANES) * LANES
    small = [w_router] + [g[:, None] for g in (g_attn, g_query, g_key, g_ffn)]
    small += [expert_ids[0].T.reshape(own_rows, per_row).astype(BF)]
    small += [jnp.zeros((own_rows, small_width - E - 4 - per_row), BF)]
    x_copies = jnp.broadcast_to(x_own, (nc,) + x_own.shape)
    g_copies = jnp.broadcast_to(g_own, (nc,) + g_own.shape)
    to_all = jnp.concatenate([w_attn_out] + small, axis=1)
    to_all = jnp.broadcast_to(to_all, (nc,) + to_all.shape)
    got = links.exchange(jnp.concatenate([by_cols, to_all], axis=2)).reshape(fsdp_rows, -1)
    cols_o = 3 * width + dim
    qkv_rows = jnp.concatenate([got[:, : 3 * width], got[:, cols_o:]], axis=1)
    w_o_rows = got[:, 3 * width : cols_o]
    qkv_begun = links.plane_start(qkv_rows)
    x_sent = after(x_copies, got)
    w_qkv = links.all_blocks(links.plane_end(qkv_begun, x_sent)[0])
    group = 2
    groups = nc // group
    x_all = links.exchange(x_sent).reshape(seq, dim)
    w_o_begun = links.plane_start(after(w_o_rows, w_qkv[-1]))
    w_o_pieces, w_o_sent = links.plane_end(w_o_begun)
    small_all = jnp.stack([w[:, 3 * width :] for w in w_qkv])
    small_all = small_all.reshape(nf, nc, own_rows, small_width)
    small_all = links.relative(small_all, planes=True).reshape(dim, small_width)
    router = jnp.where(jnp.arange(LANES) < E, small_all[:, :LANES], 0)
    gains = small_all[:, E : E + 4].T.reshape(4, 1, dim).astype(F32)
    gain_attn, gain_query, gain_key, gain_ffn = gains
    ids_all = small_all[:, E + 4 : E + 4 + per_row].astype(jnp.int32)
    ids_all = ids_all.reshape(nf, nc, TOP, tok)

    positions = jnp.arange(seq, dtype=jnp.int32)
    cos, sin = rotary_tables(positions)
    docs = jnp.sum((starts[None, :] <= positions[:, None]).astype(jnp.int32), axis=1)
    allowed = (positions[None, :] <= positions[:, None]) & (docs[None, :] == docs[:, None])
    mask = allowed.astype(F32)
    normed, raw, value, sums = call(
        functools.partial(qkv_kernel, nf),
        [
            shape((seq, dim), BF),
            shape((2, seq, width), F32),
            shape((seq, width), BF),
            shape((2, 8, seq), F32),
        ],
        3.2,
        13,
        ins=[SMEM] + [VMEM] * (2 + nf),
        gate=w_o_sent + [mask, cos, sin],
    )(frel, gain_attn, x_all, *w_qkv)

    w_o = links.all_blocks(w_o_pieces)
    if links.native:
        g_one = links.cswap(after(g_own, w_qkv[-1]), 1)
        g_groups = [jnp.concatenate([g_own, after(g_one, sums)])]
    else:
        g_groups = links.slots(g_own)
        g_groups = [jnp.concatenate(g_groups[i * group : (i + 1) * group]) for i in range(groups)]
    g_all = [lax.all_gather(g, "fsdp", axis=0) for g in g_groups]

    def columns(flat):
        return jnp.broadcast_to(flat[:, :, None], (2, seq, LANES))

    sums = jnp.sum(links.gather(sums), axis=0)[:, 0]
    inv = columns(lax.rsqrt(sums / dim + EPS))
    head_gain = jnp.stack([gain_query, gain_key]).reshape(2, nc, 1, width)
    head_gain = lax.dynamic_index_in_dim(head_gain, links.c, 1, keepdims=False)
    scale = 1.0 / math.sqrt(HD)

    def whole(*dims):
        return pl.BlockSpec(dims, lambda h: (0,) * len(dims))

    pair_spec = pl.BlockSpec((2, seq, HD), lambda h: (0, 0, h))
    head_spec = pl.BlockSpec((seq, HD), lambda h: (0, h))
    gain_spec = pl.BlockSpec((2, 1, HD), lambda h: (0, 0, h))
    table_specs = [whole(seq, HD), whole(seq, HD), whole(seq, seq)]
    low, mixed = call(
        functools.partial(attend_kernel, scale),
        [shape((2, seq, width), BF), shape((seq, width), BF)],
        0.6,
        7,
        grid=(heads,),
        ins=[pair_spec, head_spec, whole(2, seq, LANES), gain_spec] + table_specs,
        out_specs=[pair_spec, head_spec],
    )(raw, value, inv, head_gain, cos, sin, mask)
    mixed_rows = links.exchange(mixed.reshape(nc, tok, width))
    pieces = w_in.shape[0]
    halves = min(2, pieces)
    experts = pieces // halves
    device = links.f * nc + links.c
    first_expert = device * pieces // 2
    cores = links.cores
    mine = first_expert + jnp.arange(experts, dtype=jnp.int32)
    theirs = ((links.f ^ 1) * nc + links.c) * pieces // 2 + jnp.arange(experts, dtype=jnp.int32)
    both = jnp.concatenate([mine, theirs]) if cores == 2 else mine
    ids_rel = links.relative(after(ids_all, mixed)).transpose(1, 0, 2, 3)
    before = (jnp.arange(tok)[:, None] < jnp.arange(tok)[None, :]).astype(BF)
    ranks = jnp.arange(CAP, dtype=F32)[:, None]

    def slots_of(ids, names):
        named = jnp.any(ids[:, :, None] == names[:, None, None], axis=3)
        rank = jnp.einsum("kmet,ts->kmes", named.astype(BF), before, preferred_element_type=F32)
        return (named[:, :, :, None] & (rank[:, :, :, None] == ranks)).astype(BF)

    blocks = nf // cores
    slots = slots_of(ids_rel[:, ::cores], both)
    slot_sets = [slots[:, :, :experts]]
    if cores == 2:
        slot_sets.append(slots_of(ids_rel[:, 1::2], mine))
    rows_all = experts * cores * group * CAP
    eye = jnp.eye(group, dtype=BF)[:, None, :, None]
    spread = slots.reshape(groups, group, blocks, experts * cores, CAP, tok)
    spread = spread.transpose(0, 2, 3, 1, 4, 5)[:, :, :, :, :, None] * eye
    spread = spread.reshape(groups, blocks, rows_all, group * tok)
    taking = [spread[i] for i in range(groups)]
    placing = []
    for i in range(groups if cores == 1 else 1):
        sets = jnp.stack([s[i * group : (i + 1) * group] for s in slot_sets])
        sets = sets.transpose(0, 2, 3, 1, 4, 5)[:, :, :, :, :, None] * eye
        placing.append(sets.reshape(nf, experts * group * CAP, group * tok))
    putting = [spread[i].transpose(0, 2, 1) for i in range(groups)]
    hidden, inv_ffn, moe_in, mixed_all = call(
        functools.partial(out_kernel, nf),
        [shape((tok, dim), F32), shape((tok, LANES), F32)] + [shape((tok, dim), BF)] * 2,
        1.1,
        12,
        ins=[SMEM] + [VMEM] * (3 + nf),
        gate=taking + putting + placing,
    )(frel, x_own, gain_ffn, mixed_rows, *w_o)

    part = blocks * group * CAP
    nrow = part * cores
    tile = 1024

    def tiles(*dims):
        return pl.BlockSpec(dims[:-1] + (tile,), lambda d: (0,) * (len(dims) - 1) + (d,))

    def fixed(array):
        return pl.BlockSpec(array.shape, lambda d: (0,) * array.ndim)

    def take_rows(i, entries, *gate):
        arrays = [a for entry in entries for a in entry]
        parts = call(
            functools.partial(take_kernel, [len(entry) for entry in entries], experts),
            [shape((experts, part, dim), BF)] * cores,
            1.6,
            8,
            grid=(dim // tile,),
            ins=[fixed(taking[i])] + [tiles(*a.shape) for a in arrays],
            out_specs=[tiles(experts, part, dim)] * cores,
            gate=gate,
        )(taking[i], *arrays)
        if cores == 1:
            return parts
        return [parts[0], links.swap(parts[1], 1)]

    plan, plan_rows = links.plane_plan(group * tok)

    def put_rows(i, parts, *gate):
        if cores == 2:
            parts = [parts[0], links.swap(parts[1], 1)]
        return call(
            functools.partial(put_kernel, blocks, cores, plan),
            [shape((n, dim), BF) for n in plan_rows],
            1.6,
            8,
            grid=(dim // tile,),
            ins=[fixed(putting[i])] + [tiles(experts, part, dim)] * cores,
            out_specs=[tiles(n, dim) for n in plan_rows],
            gate=gate,
        )(putting[i], *parts)

    def grouped(pieces):
        return [jnp.concatenate(pieces[i * group : (i + 1) * group]) for i in range(groups)]

    def take_placed(i, whole):
        order = [m for p in range(cores) for m in range(p, nf, cores)]
        sets = placing[i]
        places = jnp.array(order, jnp.int32)
        places = links.f ^ places if links.native else places
        return call(
            take_placed_kernel,
            shape((experts, nrow, dim), BF),
            0.8,
            12,
            spec=pltpu.PrefetchScalarGridSpec(
                num_scalar_prefetch=1,
                grid=(nf,),
                in_specs=[pl.BlockSpec((1,) + sets.shape[1:], lambda m, at: (m, 0, 0))]
                + [pl.BlockSpec((1, group * tok, dim), lambda m, at: (at[m], 0, 0))],
                out_specs=pl.BlockSpec((experts, group * CAP, dim), lambda m, at: (0, m, 0)),
            ),
        )(places, sets, whole)

    g_rows = [[take_placed(i, g)] for i, g in enumerate(g_all)]

    def pick_far(stacked):
        return [pick(stacked, links.c ^ 2), pick(stacked, links.c ^ 3)]

    if links.native:
        near = links.cswap(moe_in, 1)
        far = links.gather(moe_in, near)
        x_begun = [links.plane_start(jnp.concatenate([moe_in, near]))]
        seen, sent = links.plane_end(x_begun[0], g_rows[0][0])
        far = after(far, *seen[3])
        g_far = links.exchange(after(g_copies, far))
        x_begun.append(links.plane_start(jnp.concatenate(pick_far(far))))
        x_rows = [take_rows(0, seen, x_begun[1][0])]
    else:
        x_groups = grouped(links.slots(moe_in))
        x_rows = [take_rows(i, links.plane_end(links.plane_start(x))[0]) for i, x in enumerate(x_groups)]
    w_out_e = w_out.reshape(experts, halves * FH, dim)
    inner_width = halves * FH

    def by_expert(*dims):
        return pl.BlockSpec(dims, lambda j: (j,) + (0,) * (len(dims) - 1))

    dtile = 512
    n = groups * cores
    of_group = [list(range(i * cores, (i + 1) * cores)) for i in range(groups)]

    def grad_out_pieces(inners, g_rows, *gate):
        flat = [a for parts in g_rows for a in parts]
        g_parts, at = [], groups
        for parts in g_rows:
            g_parts.append(list(range(at, at + len(parts))))
            at += len(parts)
        return call(
            functools.partial(
                weight_grad_kernel,
                list(range(groups)),
                g_parts,
            ),
            shape(w_out_e.shape, F32),
            6.5,
            26,
            grid=(experts, halves),
            ins=[pl.BlockSpec((1, nrow, FH), lambda j, h: (j, 0, h))] * groups
            + [pl.BlockSpec((1, g.shape[1], dim), lambda j, h: (j, 0, 0)) for g in flat],
            out_specs=pl.BlockSpec((1, FH, dim), lambda j, h: (j, h, 0)),
            gate=gate,
        )(*inners, *flat)

    def grad_in_pieces(j, total, *gate):
        flat = [a for parts in x_rows for a in parts]
        return call(
            functools.partial(weight_grad_kernel, [n + i for i in range(groups)], of_group),
            shape(w_in.shape, F32),
            6.5,
            25,
            grid=(halves, dim // dtile),
            ins=[pl.BlockSpec((1, part, dtile), lambda p, d: (j, 0, d))] * n
            + [pl.BlockSpec((1, nrow, 2 * FH), lambda p, d: (j * halves + p, 0, 0))] * groups
            + [pl.BlockSpec(memory_space=pl.ANY)] * (j > 0),
            out_specs=pl.BlockSpec((1, dtile, 2 * FH), lambda p, d: (j * halves + p, d, 0)),
            aliases={n + groups: 0} if j else {},
            gate=gate,
        )(*flat, *dprojs, *([total] if j else []))

    def expert(i, *gate):
        rows_in = [by_expert(1, part, dim)] * cores
        return call(
            functools.partial(expert_kernel, halves, cores),
            [shape((experts, part, dim), BF)] * cores
            + [
                shape((pieces, nrow, 2 * FH), BF),
                shape((experts, nrow, inner_width), BF),
                shape((experts, nrow, LANES), F32),
            ],
            34,
            30,
            grid=(experts,),
            ins=[
                SMEM,
                pl.BlockSpec((dim, LANES), lambda j: (0, 0)),
                by_expert(halves, dim, 2 * FH),
                by_expert(1, inner_width, dim),
            ]
            + rows_in
            + [by_expert(1, g.shape[1], dim) for g in g_rows[i]],
            out_specs=rows_in
            + [
                by_expert(halves, nrow, 2 * FH),
                by_expert(1, nrow, inner_width),
                by_expert(1, nrow, LANES),
            ],
            gate=gate,
        )(first_expert.reshape(1), router, w_in, w_out_e, *x_rows[i], *g_rows[i])

    def result(inner, *gate):
        return call(
            result_kernel,
            [shape((experts, part, dim), BF)] * cores,
            3.4,
            14,
            grid=(experts,),
            ins=[by_expert(1, nrow, inner_width), by_expert(1, inner_width, dim)],
            out_specs=[by_expert(1, part, dim)] * cores,
            gate=gate,
        )(inner, w_out_e)

    def cut_group(total):
        return [total[b * tok : (b + 1) * tok] for b in range(group)]

    done, begun, more, totals = [], [], [], []
    last = x_rows[0][0]
    for i in range(groups):
        done.append(expert(i, last))
        if links.native and i == 0:
            pieces_x, sent = links.plane_end(x_begun[1], done[0][0])
            g_begun = links.plane_start(jnp.concatenate(pick_far(after(g_far, *sent))))
            arrays = put_rows(0, done[0][:cores], g_begun[0])
            x_rows.append(take_rows(1, pieces_x, arrays[0]))
            pieces_g, sent = links.plane_end(g_begun, x_rows[1][0])
            arrays = held(arrays, *sent)
            g_rows.append(take_rows(1, pieces_g))
            last = g_rows[1][0]
        elif i == 1:
            more.append(links.reduce_next(begun[0], done[1][0]))
            arrays = put_rows(1, done[1][:cores], *more[0][-2:])
            last = arrays[0]
        else:
            arrays = put_rows(i, done[i][:cores], done[i][0])
            last = arrays[0]
        begun.append(links.reduce_start(arrays))
    dgate = jnp.stack([d[cores + 2][:, :, 0] for d in done], axis=1)
    dgate = dgate.reshape(experts, groups, cores, blocks, group, CAP).transpose(2, 1, 4, 3, 0, 5)
    dgate = dgate.reshape(cores, nc, blocks, experts, CAP, 1)
    dgate_tok = jnp.stack(
        [jnp.sum(s.astype(F32) * d, axis=3) for s, d in zip(slot_sets, dgate)], axis=2
    ).reshape(nc, nf, experts, tok)
    dgate_tok = links.relative(dgate_tok.transpose(1, 0, 2, 3))
    dgate_back = lax.all_to_all(
        dgate_tok.reshape(ndev, experts, tok), ALL, split_axis=0, concat_axis=0, tiled=True
    )
    results, out_arrays, out_begun = [], [], []
    for i in range(groups):
        results.append(result(done[i][cores + 1], last))
        last = results[i][0]
    totals.append(links.reduce_end(more[0], group * tok, last))
    out_arrays.append(put_rows(0, results[0], totals[0]))
    last = out_arrays[0][0]
    for i in range(1, groups):
        more.append(links.reduce_next(begun[i], last))
        last = more[i][-1]
        out_begun.append(links.reduce_start(held(out_arrays[i - 1], last)))
        out_arrays.append(put_rows(i, results[i], last))
        last = out_arrays[i][0]
    dprojs = [d[cores] for d in done]
    inners = [d[cores + 1] for d in done]
    for i in range(1, groups):
        totals.append(links.reduce_end(more[i], group * tok, last))
        last = totals[i]
    dmoe_terms = links.sum_slots([t for total in totals for t in cut_group(total)])
    dgate_back = after(dgate_back, out_arrays[0][0])
    dprob = jnp.sum(dgate_back.reshape(E, ndev * experts // E, tok), axis=1).T
    dprob = jnp.pad(dprob, ((0, 0), (0, LANES - E)))
    grad_w_out = grad_out_pieces(inners, g_rows, last, dprob)
    out_begun.append(links.reduce_start(held(out_arrays[-1], grad_w_out)))
    dmoe_terms = held(dmoe_terms, grad_w_out)

    back = call(
        functools.partial(hidden_back_kernel, nf, len(dmoe_terms)),
        [shape((tok, dim), F32), shape((dim, LANES), F32), shape((8, dim), F32)]
        + [shape((tok, dim), BF), shape((nc, tok, width), BF)],
        1.3,
        15,
        ins=[SMEM] + [VMEM] * (7 + len(dmoe_terms) + nf),
        scratch=[pltpu.VMEM((tok, dim), BF)],
    )(frel, hidden, inv_ffn, moe_in, g_own, gain_ffn, router, dprob, *dmoe_terms, *w_o)
    dhidden, grad_router, grad_gain_ffn, dlow, dmixed = back
    dmixed = links.exchange(dmixed)
    grad_plan, grad_rows = links.dense_plan(fsdp_rows)

    def dense_terms(left, right, extra, *gate):
        return call(
            functools.partial(place_grad_kernel, nf, grad_plan),
            [shape((r, right.shape[1] + LANES), BF) for r in grad_rows],
            right.shape[0] * right.shape[1] * dim * 2e-9,
            right.shape[1] * dim * 2e-6,
            ins=[SMEM, VMEM, VMEM, VMEM],
            gate=gate,
        )(frel, left, right, extra)

    last = dlow
    out_more = []
    for b in out_begun:
        out_more.append(links.reduce_next(b, last))
        last = out_more[-1][-1]
    grad_w_in = grad_in_pieces(0, None, last)
    last = grad_w_in
    dmixed = after(dmixed, last).reshape(seq, width)

    u, dvalue, stats, dgain = call(
        functools.partial(attend_back_kernel, scale),
        [
            shape((2, seq, width), F32),
            shape((seq, width), BF),
            shape((2, 8, seq), F32),
            shape((2, 8, width), F32),
        ],
        1.4,
        10,
        grid=(heads,),
        ins=[pair_spec, pair_spec, head_spec, whole(2, seq, LANES), gain_spec]
        + table_specs
        + [head_spec],
        out_specs=[
            pair_spec,
            head_spec,
            whole(2, 8, seq),
            pl.BlockSpec((2, 8, HD), lambda h: (0, 0, h)),
        ],
    )(raw, low, value, inv, head_gain, cos, sin, mask, dmixed)
    with_ffn = jnp.where(jnp.arange(LANES) == E, grad_gain_ffn[0][:, None], grad_router)
    grad_o_terms = dense_terms(mixed_all, dlow, with_ffn.astype(BF), stats)
    mean = columns(jnp.sum(links.gather(stats), axis=0)[:, 0] / dim)
    last = grad_o_terms[0]
    out_totals = []
    for m in out_more:
        out_totals.append(links.reduce_end(m, group * tok, last))
        last = out_totals[-1]
    out_terms = links.sum_at_once([t for o in out_totals for t in cut_group(o)])
    mean = after(mean, last)
    dqkv, dnormed_terms, dgain_attn = call(
        functools.partial(dnormed_kernel, nf),
        [shape((seq, 3 * width), BF), shape((seq, dim), BF), shape((8, dim), F32)],
        3.3,
        15,
        ins=[SMEM] + [VMEM] * (6 + nf),
    )(frel, u, raw, inv, mean, dvalue, x_all, *w_qkv)

    def placed(vector):
        return lax.dynamic_update_slice(jnp.zeros((dim,), F32), vector, (links.c * width,))

    grad_o_begun = links.dense_start(grad_o_terms, fsdp_rows, dqkv)
    gain_terms = jnp.stack([dgain_attn[0], placed(dgain[0, 0]), placed(dgain[1, 0])])
    gain_terms = jnp.pad(gain_terms.astype(BF), ((0, LANES - 3), (0, 0))).T
    last = dqkv
    for j in range(1, experts):
        grad_w_in = grad_in_pieces(j, grad_w_in, dqkv, *grad_o_begun[2:3])
        last = grad_w_in
    grad_qkv_terms = dense_terms(normed, dqkv, gain_terms, last, out_terms)
    last = grad_qkv_terms[0]
    dnormed_terms = after(dnormed_terms.reshape(nc, tok, dim), out_terms)
    grad_qkv_begun = links.dense_start(grad_qkv_terms, fsdp_rows, last, dnormed_terms)
    dnormed_terms = links.exchange(dnormed_terms)
    last = grad_qkv_begun[-1]
    grad_o_more = links.reduce_next(grad_o_begun, last)
    grad_qkv_more = links.reduce_next(grad_qkv_begun, grad_o_more[-1])
    grad_o_total = links.reduce_end(grad_o_more, fsdp_rows, grad_qkv_more[-1])
    grad_o = links.exchange(grad_o_total.reshape(nc, own_rows, -1))
    grad_qkv_total = links.reduce_end(grad_qkv_more, fsdp_rows, grad_o_total)
    dnormed_terms = after(dnormed_terms, grad_qkv_total)
    dnormed = jnp.sum(dnormed_terms.astype(F32), axis=0)
    x_float = x_own.astype(F32)
    x_inv = lax.rsqrt(jnp.mean(x_float * x_float, axis=-1, keepdims=True) + EPS)
    ux = dnormed * gain_attn
    x_mean = jnp.mean(ux * x_float, axis=-1, keepdims=True)
    input_grad = (dhidden + x_inv * ux - x_float * x_inv**3 * x_mean)[None]

    output = (hidden + jnp.sum(out_terms.astype(F32), axis=0)).astype(BF)
    grad_o = jnp.sum(grad_o.astype(F32), axis=0)
    grad_attn_out, router_sum = grad_o[:, :dim], grad_o[:, dim:]
    grad_qkv = links.exchange(grad_qkv_total.reshape(nc, own_rows, -1)).astype(F32)
    gain_sum = jnp.sum(grad_qkv[:, :, 3 * width :], axis=0).T
    grad_dense = grad_qkv[:, :, : 3 * width].reshape(nc, own_rows, 3, width).transpose(2, 1, 0, 3)
    grad_dense = grad_dense.reshape(3, own_rows, dim)
    return (
        output[None],
        input_grad,
        grad_dense[0],
        grad_dense[1],
        grad_dense[2],
        grad_attn_out,
        router_sum[:, :E],
        gain_sum[0],
        gain_sum[1],
        gain_sum[2],
        router_sum[:, E],
        grad_w_in,
        grad_w_out.reshape(w_out.shape),
    )


def solution(mesh):
    rows = P(ALL, None)
    vec = P(ALL)
    cube = P(ALL, None, None)
    stream = P("fsdp", "ctx", None)
    weights = (rows,) * 5 + (vec,) * 4 + (cube,) * 2
    return jax.shard_map(
        shards,
        mesh=mesh,
        in_specs=(stream, P("fsdp", None), stream) + weights + (stream,),
        out_specs=(stream, stream) + weights,
        check_vma=False,
    )
```

```python
import functools
import math

import jax
import jax.numpy as jnp
from jax import lax
from jax.experimental import pallas as pl
from jax.experimental.pallas import tpu as pltpu
from jax.sharding import PartitionSpec as P

H = 16
HD = 128
E = 64
TOP = 8
FH = 512
CAP = 24

EPS = 1e-05
MASKED = -1e30
ROPE_BASE = 10000.0
HIGHEST = lax.Precision.HIGHEST
F32 = jnp.float32
BF = jnp.bfloat16
ALL = ("fsdp", "ctx")
LANES = 128
VMEM_LIMIT = 60 * 1024 * 1024


def pick(stacked, index):
    return lax.dynamic_index_in_dim(stacked, index, 0, keepdims=False)


def after(value, *others):
    return held([value], *others)[0]


def held(values, *others):
    if not others:
        return list(values)
    values = list(values)
    anywhere = pl.BlockSpec(memory_space=pl.ANY)
    done = pl.pallas_call(
        lambda *refs: None,
        out_shape=[jax.ShapeDtypeStruct(v.shape, v.dtype) for v in values],
        in_specs=[anywhere] * (len(values) + len(others)),
        out_specs=[anywhere] * len(values),
        input_output_aliases={i: i for i in range(len(values))},
    )(*values, *others)
    return list(done)


def held_pieces(blocks, *gate):
    flat = held([a for b in blocks for a in b], *gate)
    return [[flat.pop(0) for _ in b] for b in blocks]


def add_low(*terms):
    return sum(t.astype(F32) for t in terms).astype(BF)


class Links:
    def __init__(self, nf, nc):
        self.nf, self.nc = nf, nc
        self.native = nf == 8 and nc == 4
        self.cores = 2 if self.native else 1
        self.f = lax.axis_index("fsdp")
        self.c = lax.axis_index("ctx")
        ms = jnp.arange(nf, dtype=jnp.int32)
        self.frel = self.f ^ ms if self.native else ms

    def swap(self, value, mask):
        return lax.ppermute(value, "fsdp", [(i, i ^ mask) for i in range(self.nf)])

    def cswap(self, value, mask):
        return lax.ppermute(value, "ctx", [(i, i ^ mask) for i in range(self.nc)])

    def exchange(self, value):
        return lax.all_to_all(value, "ctx", split_axis=0, concat_axis=0, tiled=True)

    def gather(self, value, *gate):
        return self.exchange(after(jnp.broadcast_to(value, (self.nc,) + value.shape), *gate))

    def slots(self, value):
        if not self.native:
            whole = lax.all_gather(value, "ctx", axis=0)
            return [whole[k] for k in range(self.nc)]
        return [value] + [self.cswap(value, k) for k in range(1, self.nc)]

    def sum_slots(self, parts):
        if not self.native:
            whole = jnp.stack(parts)
            return [lax.psum_scatter(whole, "ctx", scatter_dimension=0, tiled=False)]
        return [parts[0]] + [self.cswap(parts[k], k) for k in range(1, self.nc)]

    def sum_at_once(self, parts):
        whole = jnp.stack(parts)
        if not self.native:
            return lax.psum_scatter(whole, "ctx", scatter_dimension=0, tiled=True)
        for bit in (1, 2):
            flipped = jnp.stack([whole[k ^ bit] for k in range(self.nc)])
            whole = jnp.where((self.c & bit) > 0, flipped, whole)
        return self.exchange(whole)

    def relative(self, value, planes=False):
        if not self.native:
            return value
        dims = value.shape
        for bit, place in ((4, self.f), (2, self.f), (1, self.f), (2, self.c), (1, self.c)):
            lead = 0 if place is self.f else 1
            if lead and planes:
                continue
            n = dims[lead]
            split = dims[:lead] + (n // (2 * bit), 2, bit) + dims[lead + 1 :]
            cut = value.reshape(split)
            parts = jnp.split(cut, 2, axis=lead + 1)
            flipped = jnp.concatenate(parts[::-1], axis=lead + 1)
            value = jnp.where((place & bit) > 0, flipped, cut).reshape(dims)
        return value

    def plane_start(self, value):
        if not self.native:
            return [value]
        return [value, self.swap(value, 2), self.swap(value, 4)]

    def plane_end(self, begun, *gate):
        if not self.native:
            whole = lax.all_gather(begun[0], "fsdp", axis=0)
            return [[whole[m]] for m in range(self.nf)], begun
        value, from_x, from_y = begun
        half = value.shape[0] // 2
        from_x, from_y = held([from_x, from_y], *gate)
        sent = [from_y[:half], from_x[half:]]
        diag_a = self.swap(sent[0], 2)
        diag_b = self.swap(sent[1], 4)
        return [[value], [from_x], [from_y], [diag_a, diag_b]], sent

    def all_blocks(self, pieces):
        blocks = [b[0] if len(b) == 1 else jnp.concatenate(b) for b in pieces]
        if not self.native:
            return blocks
        return [a for b in blocks for a in (b, self.swap(b, 1))]

    def dense_plan(self, rows):
        if not self.native:
            return [(m, 0, rows, 0, m * rows) for m in range(self.nf)], [self.nf * rows]
        h = rows // 2
        order = [(2, 0), (6, 0), (4, h), (6, h), (4, 0), (2, h), (0, 0), (0, h)]
        entries = []
        for core in (0, 1):
            for place, (m, first) in enumerate(order):
                entries.append((m + core, first, h, core, place * h))
        return entries, [8 * h, 8 * h]

    def dense_start(self, arrays, rows, *gate):
        if not self.native:
            return arrays
        mine, other = arrays
        near = after(self.swap(other, 1), *gate)
        h = rows // 2
        spans = [(0, 2), (2, 2), (4, 1), (5, 1), (6, 2)]
        sums = [
            add_low(mine[a * h : (a + n) * h], near[a * h : (a + n) * h]) for a, n in spans
        ]
        return self.reduce_start(sums)

    def plane_plan(self, rows):
        if not self.native:
            return [(m, 0, rows, 0, m * rows) for m in range(self.nf)], [self.nf * rows]
        h = rows // 2
        entries = [(2, 0, h, 0, 0), (6, 0, h, 0, h), (4, h, h, 1, 0), (6, h, h, 1, h)]
        entries += [(4, 0, h, 2, 0), (2, h, h, 3, 0), (0, 0, rows, 4, 0)]
        return entries, [rows, rows, h, h, rows]

    def reduce_start(self, arrays):
        if not self.native:
            return arrays
        to_x, to_y, rest_y, rest_x, own = arrays
        return [self.swap(to_x, 2), self.swap(to_y, 4), rest_y, rest_x, own]

    def reduce_next(self, begun, *gate):
        if not self.native:
            return begun
        got_x, got_y, rest_y, rest_x, own = begun
        if gate:
            got_x, got_y = held([got_x, got_y], *gate)
        h = rest_y.shape[0]
        last_y = add_low(rest_y, got_x[h:])
        last_x = add_low(rest_x, got_y[h:])
        return [got_x, got_y, self.swap(last_y, 4), self.swap(last_x, 2), own, last_y, last_x]

    def reduce_end(self, begun, rows, *gate):
        if not self.native:
            whole = begun[0].reshape((self.nf, rows) + begun[0].shape[1:])
            return lax.psum_scatter(whole, "fsdp", scatter_dimension=0, tiled=False)
        got_x, got_y, last_y, last_x, own = begun[:5]
        if gate:
            last_y, last_x = held([last_y, last_x], *gate)
        h = rows // 2
        return jnp.concatenate(
            [add_low(own[:h], got_x[:h], last_y), add_low(own[h:], got_y[:h], last_x)]
        )


def mm(a, b):
    return lax.dot_general(a, b, (((1,), (0,)), ((), ())), preferred_element_type=F32)


def mm_nt(a, b):
    return lax.dot_general(a, b, (((1,), (1,)), ((), ())), preferred_element_type=F32)


def mm_tn(a, b):
    return lax.dot_general(a, b, (((0,), (0,)), ((), ())), preferred_element_type=F32)


def call(
    kernel, outs, gflop, mbytes, ins=None, grid=(), out_specs=None, scratch=(), aliases=None, spec=None, gate=()
):
    args = dict(
        out_shape=outs,
        input_output_aliases=aliases or {},
        cost_estimate=pl.CostEstimate(
            flops=int(gflop * 5e7), bytes_accessed=int(mbytes * 5e4), transcendentals=0
        ),
        compiler_params=pltpu.CompilerParams(vmem_limit_bytes=VMEM_LIMIT),
    )
    if spec is not None:
        return pl.pallas_call(kernel, grid_spec=spec, **args)
    given, waits = len(ins), len(gate)

    def body(*refs):
        kernel(*refs[:given], *refs[given + waits :])

    args["scratch_shapes"] = list(scratch)
    args["in_specs"] = list(ins) + [pl.BlockSpec(memory_space=pl.ANY)] * waits
    if grid:
        args["grid"] = grid
    if out_specs is not None:
        args["out_specs"] = out_specs
    made = pl.pallas_call(body, **args)
    return lambda *operands: made(*operands, *gate)


SMEM = pl.BlockSpec(memory_space=pltpu.SMEM)
VMEM = pl.BlockSpec(memory_space=pltpu.VMEM)


def shape(dims, dtype):
    return jax.ShapeDtypeStruct(tuple(dims), dtype)


def qkv_kernel(nf, frel, gain, xs, *refs):
    ws = refs[:nf]
    normed, raw, value, sums = refs[nf:]
    width = value.shape[1]
    block = ws[0].shape[0]
    x = xs[...].astype(F32)
    inv = lax.rsqrt(jnp.mean(x * x, axis=-1, keepdims=True) + EPS)
    normed[...] = (x * inv * gain[...]).astype(BF)
    total = None
    for m in range(nf):
        cols = pl.ds(pl.multiple_of(frel[m] * block, block), block)
        term = mm(normed[:, cols], ws[m][:, : 3 * width])
        total = term if total is None else total + term
    q, k = total[:, :width], total[:, width : 2 * width]
    raw[0] = q
    raw[1] = k
    value[...] = total[:, 2 * width :].astype(BF)
    for i, part in enumerate((q, k)):
        column = jnp.sum(part * part, axis=-1, keepdims=True)
        sums[i] = jnp.broadcast_to(column, (column.shape[0], LANES)).T[:8]


def turn(v, cos, sin):
    half = HD // 2
    other = jnp.concatenate([v[:, half:], v[:, :half]], axis=1)
    return v * cos + other * sin


def attend_kernel(scale, raw, value, inv, gain, cos, sin, mask, low, mixed):
    q = turn(raw[0] * inv[0] * gain[0], cos[...], sin[...]).astype(BF)
    k = turn(raw[1] * inv[1] * gain[1], cos[...], sin[...]).astype(BF)
    low[0] = q
    low[1] = k
    scores = jnp.where(mask[...] > 0, mm_nt(q, k) * scale, MASKED)
    top = jnp.max(scores, axis=-1, keepdims=True)
    e = jnp.exp(scores - top)
    probs = e / jnp.sum(e, axis=-1, keepdims=True)
    mixed[...] = mm(probs.astype(BF), value[...]).astype(BF)


def attend_back_kernel(
    scale, raw, low, value, inv, gain, cos, sin, mask, dmixed, u, dv, stats, dgain
):
    q, k, v = low[0], low[1], value[...]
    scores = jnp.where(mask[...] > 0, mm_nt(q, k) * scale, MASKED)
    top = jnp.max(scores, axis=-1, keepdims=True)
    e = jnp.exp(scores - top)
    probs = e / jnp.sum(e, axis=-1, keepdims=True)
    dm = dmixed[...]
    dprobs = mm_nt(dm, v)
    delta = jnp.sum(probs * dprobs, axis=-1, keepdims=True)
    ds = (probs * (dprobs - delta)).astype(BF)
    dv[...] = mm_tn(probs.astype(BF), dm).astype(BF)
    first = pl.program_id(0) == 0
    for i, grad in enumerate((mm(ds, k) * scale, mm_tn(ds, q) * scale)):
        turned = turn(grad, cos[...], -sin[...])
        ui = turned * gain[i]
        u[i] = ui
        line = jnp.sum(turned * raw[i] * inv[i], axis=0, keepdims=True)
        dgain[i] = jnp.broadcast_to(line, (8, line.shape[1]))
        column = jnp.sum(ui * raw[i], axis=-1, keepdims=True)
        flat = jnp.broadcast_to(column, (column.shape[0], LANES)).T[:8]
        stats[i] = jnp.where(first, flat, stats[i] + flat)


def out_kernel(nf, frel, x, gain, mixed, *refs):
    ws = refs[:nf]
    hidden, inv_out, moe, rows = refs[nf:]
    width = mixed.shape[2]
    block = ws[0].shape[0]
    for k in range(mixed.shape[0]):
        rows[:, k * width : (k + 1) * width] = mixed[k]
    total = x[...].astype(F32)
    for m in range(nf):
        cols = pl.ds(pl.multiple_of(frel[m] * block, block), block)
        total = total + mm(rows[:, cols], ws[m][...])
    hidden[...] = total
    inv = lax.rsqrt(jnp.mean(total * total, axis=-1, keepdims=True) + EPS)
    inv_out[...] = jnp.broadcast_to(inv, inv_out.shape)
    moe[...] = (total * inv * gain[...]).astype(BF)


def hidden_back_kernel(nf, nt, frel, hidden, inv_in, moe, g, gain, router, dprob, *refs):
    terms, ws = refs[:nt], refs[nt : nt + nf]
    dhidden, drouter, dgain, low_rows, dmixed, mix_rows = refs[nt + nf :]
    width = dmixed.shape[2]
    block = ws[0].shape[0]
    logits = mm(moe[...], router[...])
    lane = lax.broadcasted_iota(jnp.int32, logits.shape, 1)
    logits = jnp.where(lane < E, logits, MASKED)
    e = jnp.exp(logits - jnp.max(logits, axis=-1, keepdims=True))
    probs = e / jnp.sum(e, axis=-1, keepdims=True)
    dp = dprob[...]
    dlogits = probs * (dp - jnp.sum(probs * dp, axis=-1, keepdims=True))
    high = dlogits.astype(BF)
    rest = (dlogits - high.astype(F32)).astype(BF)
    drouter[...] = mm_tn(moe[...], high) + mm_tn(moe[...], rest)
    dmoe = mm_nt(high, router[...]) + mm_nt(rest, router[...])
    for term in terms:
        dmoe = dmoe + term[...].astype(F32)
    hid = hidden[...]
    inv = inv_in[:, :1]
    u = dmoe * gain[...]
    mean = jnp.mean(u * hid, axis=-1, keepdims=True)
    line = jnp.sum(dmoe * hid * inv, axis=0, keepdims=True)
    dgain[...] = jnp.broadcast_to(line, dgain.shape)
    dh = g[...].astype(F32) + inv * u - hid * (inv * inv * inv) * mean
    dhidden[...] = dh
    low_rows[...] = dh.astype(BF)
    for m in range(nf):
        cols = pl.ds(pl.multiple_of(frel[m] * block, block), block)
        mix_rows[:, cols] = mm_nt(low_rows[...], ws[m][...]).astype(BF)
    for k in range(dmixed.shape[0]):
        dmixed[k] = mix_rows[:, k * width : (k + 1) * width]


def dnormed_kernel(nf, frel, u, raw, inv, mean, dv, x, *refs):
    ws = refs[:nf]
    dqkv, total, line = refs[nf:]
    width = dv.shape[1]
    block = ws[0].shape[0]
    for i in range(2):
        r = inv[i][:, :1]
        b = mean[i][:, :1]
        dqkv[:, i * width : (i + 1) * width] = (r * u[i] - raw[i] * (r * r * r * b)).astype(BF)
    dqkv[:, 2 * width :] = dv[...]
    for m in range(nf):
        cols = pl.ds(pl.multiple_of(frel[m] * block, block), block)
        total[:, cols] = mm_nt(dqkv[...], ws[m][:, : 3 * width]).astype(BF)
    xf = x[...].astype(F32)
    x_inv = lax.rsqrt(jnp.mean(xf * xf, axis=-1, keepdims=True) + EPS)
    terms = jnp.sum(total[...].astype(F32) * xf * x_inv, axis=0, keepdims=True)
    line[...] = jnp.broadcast_to(terms, line.shape)


def place(plan, outs, blocks):
    for m, first, count, which, row in plan:
        outs[which][row : row + count, :] = blocks[m][first : first + count, :]


def place_grad_kernel(nf, plan, frel, left, right, extra, *outs):
    block = left.shape[1] // nf
    for m in range(nf):
        cols = pl.ds(pl.multiple_of(frel[m] * block, block), block)
        term = mm_tn(left[:, cols], right[...]).astype(BF)
        term = jnp.concatenate([term, extra[cols, :]], axis=1)
        place([p for p in plan if p[0] == m], outs, {m: term})


def take_kernel(sizes, experts, slots, *refs):
    cores = slots.shape[1] // (experts * 2 * CAP)
    xs, outs = refs[:-cores], refs[-cores:]
    two = 2 * CAP
    at = 0
    for m, size in enumerate(sizes):
        rows = [r[...] for r in xs[at : at + size]]
        at += size
        got = mm(slots[m], rows[0] if size == 1 else jnp.concatenate(rows, axis=0)).astype(BF)
        for e in range(experts * cores):
            outs[e // experts][e % experts, m * two : (m + 1) * two, :] = got[e * two : (e + 1) * two]


def take_placed_kernel(places, slots, x, out):
    del places
    got = mm(slots[0], x[0]).astype(BF)
    count = got.shape[0] // out.shape[0]
    for e in range(out.shape[0]):
        out[e] = got[e * count : (e + 1) * count]


def put_kernel(blocks, step, plan, slots, *refs):
    cores = step
    rows, outs = refs[:cores], refs[cores:]
    two = 2 * CAP
    for m in range(blocks):
        cut = [
            part[j, m * two : (m + 1) * two, :] for part in rows for j in range(part.shape[0])
        ]
        low = mm(slots[m], jnp.concatenate(cut, axis=0)).astype(BF)
        place([p for p in plan if p[0] == m * step], outs, {m * step: low})


def expert_kernel(halves, cores, first, router, w_in, w_out, *refs):
    xs, gs = refs[:cores], refs[cores : -3 - cores]
    dslots = refs[-3 - cores : -3]
    dproj, inner_out, dgate = refs[-3:]
    xr = jnp.concatenate([r[0] for r in xs], axis=0)
    gr = jnp.concatenate([r[0] for r in gs], axis=0)
    logits = mm(xr, router[...])
    lane = lax.broadcasted_iota(jnp.int32, logits.shape, 1)
    logits = jnp.where(lane < E, logits, MASKED)
    e = jnp.exp(logits - jnp.max(logits, axis=-1, keepdims=True))
    mine = first[0] + pl.program_id(0)
    chosen = jnp.sum(jnp.where(lane == mine, e, 0.0), axis=-1, keepdims=True)
    gate = chosen / jnp.sum(e, axis=-1, keepdims=True)
    back = mm_nt(gr, w_out[0])
    dg = 0.0
    ds = 0.0
    for h in range(halves):
        projected = mm(xr, w_in[h])
        a, up = projected[:, :FH], projected[:, FH:]
        sig = jax.nn.sigmoid(a)
        act = a * sig
        inner = act * up
        b = back[:, h * FH : (h + 1) * FH]
        dg = dg + jnp.sum(inner * b, axis=-1, keepdims=True)
        inner_out[0, :, h * FH : (h + 1) * FH] = (inner * gate).astype(BF)
        db = b * gate
        dproj[h, :, :FH] = (db * up * (sig * (1.0 + a * (1.0 - sig)))).astype(BF)
        dproj[h, :, FH:] = (db * act).astype(BF)
        ds = ds + mm_nt(dproj[h], w_in[h])
    low = ds.astype(BF)
    count = dslots[0].shape[1]
    for i in range(cores):
        dslots[i][0] = low[i * count : (i + 1) * count]
    dgate[0] = jnp.broadcast_to(dg, dgate.shape[1:])


def result_kernel(inner, w_out, *outs):
    low = mm(inner[0], w_out[0]).astype(BF)
    count = outs[0].shape[1]
    for i, out in enumerate(outs):
        out[0] = low[i * count : (i + 1) * count]


def weight_grad_kernel(whole, parts, *refs):
    total = None
    for w, ps in zip(whole, parts):
        at = 0
        for p in ps:
            n = refs[p].shape[1]
            term = (refs[w][0, at : at + n, :], refs[p][0])
            at += n
            term = mm_tn(term[1], term[0]) if w > p else mm_tn(term[0], term[1])
            total = term if total is None else total + term
    refs[-1][0] = total


def rotary_tables(positions):
    half = HD // 2
    frequency = ROPE_BASE ** (-(jnp.arange(half, dtype=F32) * 2.0 / HD))
    angles = positions.astype(F32)[:, None] * frequency[None, :]
    cos, sin = jnp.cos(angles), jnp.sin(angles)
    return jnp.concatenate([cos, cos], axis=1), jnp.concatenate([-sin, sin], axis=1)


def shards(
    tokens,
    doc_starts,
    expert_ids,
    w_query,
    w_key,
    w_value,
    w_attn_out,
    w_router,
    g_attn,
    g_query,
    g_key,
    g_ffn,
    w_in,
    w_out,
    cotangent,
):
    nf, nc = lax.axis_size("fsdp"), lax.axis_size("ctx")
    ndev = nf * nc
    links = Links(nf, nc)
    frel = links.frel
    x_own, g_own = tokens[0], cotangent[0]
    tok, dim = x_own.shape
    seq = tok * nc
    width = dim // nc
    heads = H // nc
    own_rows = w_query.shape[0]
    fsdp_rows = own_rows * nc
    starts = doc_starts[0]

    by_cols = [w.reshape(own_rows, nc, width) for w in (w_query, w_key, w_value)]
    by_cols = jnp.concatenate(by_cols, axis=2).transpose(1, 0, 2)
    per_row = tok * TOP // own_rows
    small_width = -(-(E + 4 + per_row) // LANES) * LANES
    small = [w_router] + [g[:, None] for g in (g_attn, g_query, g_key, g_ffn)]
    small += [expert_ids[0].T.reshape(own_rows, per_row).astype(BF)]
    small += [jnp.zeros((own_rows, small_width - E - 4 - per_row), BF)]
    x_copies = jnp.broadcast_to(x_own, (nc,) + x_own.shape)
    g_copies = jnp.broadcast_to(g_own, (nc,) + g_own.shape)
    to_all = jnp.concatenate([w_attn_out] + small, axis=1)
    to_all = jnp.broadcast_to(to_all, (nc,) + to_all.shape)
    got = links.exchange(jnp.concatenate([by_cols, to_all], axis=2)).reshape(fsdp_rows, -1)
    cols_o = 3 * width + dim
    qkv_rows = jnp.concatenate([got[:, : 3 * width], got[:, cols_o:]], axis=1)
    w_o_rows = got[:, 3 * width : cols_o]
    qkv_begun = links.plane_start(qkv_rows)
    x_sent = after(x_copies, got)
    w_qkv = links.all_blocks(links.plane_end(qkv_begun, x_sent)[0])
    group = 2
    groups = nc // group
    x_all = links.exchange(x_sent).reshape(seq, dim)
    w_o_begun = links.plane_start(after(w_o_rows, w_qkv[-1]))
    w_o_pieces, w_o_sent = links.plane_end(w_o_begun)
    small_all = jnp.stack([w[:, 3 * width :] for w in w_qkv])
    small_all = small_all.reshape(nf, nc, own_rows, small_width)
    small_all = links.relative(small_all, planes=True).reshape(dim, small_width)
    router = jnp.where(jnp.arange(LANES) < E, small_all[:, :LANES], 0)
    gains = small_all[:, E : E + 4].T.reshape(4, 1, dim).astype(F32)
    gain_attn, gain_query, gain_key, gain_ffn = gains
    ids_all = small_all[:, E + 4 : E + 4 + per_row].astype(jnp.int32)
    ids_all = ids_all.reshape(nf, nc, TOP, tok)

    positions = jnp.arange(seq, dtype=jnp.int32)
    cos, sin = rotary_tables(positions)
    docs = jnp.sum((starts[None, :] <= positions[:, None]).astype(jnp.int32), axis=1)
    allowed = (positions[None, :] <= positions[:, None]) & (docs[None, :] == docs[:, None])
    mask = allowed.astype(F32)
    normed, raw, value, sums = call(
        functools.partial(qkv_kernel, nf),
        [
            shape((seq, dim), BF),
            shape((2, seq, width), F32),
            shape((seq, width), BF),
            shape((2, 8, seq), F32),
        ],
        3.2,
        13,
        ins=[SMEM] + [VMEM] * (2 + nf),
        gate=w_o_sent + [mask, cos, sin],
    )(frel, gain_attn, x_all, *w_qkv)

    w_o = links.all_blocks(w_o_pieces)
    if links.native:
        g_one = links.cswap(after(g_own, w_qkv[-1]), 1)
        g_groups = [jnp.concatenate([g_own, after(g_one, sums)])]
    else:
        g_groups = links.slots(g_own)
        g_groups = [jnp.concatenate(g_groups[i * group : (i + 1) * group]) for i in range(groups)]
    g_all = [lax.all_gather(g, "fsdp", axis=0) for g in g_groups]

    def columns(flat):
        return jnp.broadcast_to(flat[:, :, None], (2, seq, LANES))

    sums = jnp.sum(links.gather(sums), axis=0)[:, 0]
    inv = columns(lax.rsqrt(sums / dim + EPS))
    head_gain = jnp.stack([gain_query, gain_key]).reshape(2, nc, 1, width)
    head_gain = lax.dynamic_index_in_dim(head_gain, links.c, 1, keepdims=False)
    scale = 1.0 / math.sqrt(HD)

    def whole(*dims):
        return pl.BlockSpec(dims, lambda h: (0,) * len(dims))

    pair_spec = pl.BlockSpec((2, seq, HD), lambda h: (0, 0, h))
    head_spec = pl.BlockSpec((seq, HD), lambda h: (0, h))
    gain_spec = pl.BlockSpec((2, 1, HD), lambda h: (0, 0, h))
    table_specs = [whole(seq, HD), whole(seq, HD), whole(seq, seq)]
    low, mixed = call(
        functools.partial(attend_kernel, scale),
        [shape((2, seq, width), BF), shape((seq, width), BF)],
        0.6,
        7,
        grid=(heads,),
        ins=[pair_spec, head_spec, whole(2, seq, LANES), gain_spec] + table_specs,
        out_specs=[pair_spec, head_spec],
    )(raw, value, inv, head_gain, cos, sin, mask)
    mixed_rows = links.exchange(mixed.reshape(nc, tok, width))
    pieces = w_in.shape[0]
    halves = min(2, pieces)
    experts = pieces // halves
    device = links.f * nc + links.c
    first_expert = device * pieces // 2
    cores = links.cores
    mine = first_expert + jnp.arange(experts, dtype=jnp.int32)
    theirs = ((links.f ^ 1) * nc + links.c) * pieces // 2 + jnp.arange(experts, dtype=jnp.int32)
    both = jnp.concatenate([mine, theirs]) if cores == 2 else mine
    ids_rel = links.relative(after(ids_all, mixed)).transpose(1, 0, 2, 3)
    before = (jnp.arange(tok)[:, None] < jnp.arange(tok)[None, :]).astype(BF)
    ranks = jnp.arange(CAP, dtype=F32)[:, None]

    def slots_of(ids, names):
        named = jnp.any(ids[:, :, None] == names[:, None, None], axis=3)
        rank = jnp.einsum("kmet,ts->kmes", named.astype(BF), before, preferred_element_type=F32)
        return (named[:, :, :, None] & (rank[:, :, :, None] == ranks)).astype(BF)

    blocks = nf // cores
    slots = slots_of(ids_rel[:, ::cores], both)
    slot_sets = [slots[:, :, :experts]]
    if cores == 2:
        slot_sets.append(slots_of(ids_rel[:, 1::2], mine))
    rows_all = experts * cores * group * CAP
    eye = jnp.eye(group, dtype=BF)[:, None, :, None]
    spread = slots.reshape(groups, group, blocks, experts * cores, CAP, tok)
    spread = spread.transpose(0, 2, 3, 1, 4, 5)[:, :, :, :, :, None] * eye
    spread = spread.reshape(groups, blocks, rows_all, group * tok)
    taking = [spread[i] for i in range(groups)]
    placing = []
    for i in range(groups if cores == 1 else 1):
        sets = jnp.stack([s[i * group : (i + 1) * group] for s in slot_sets])
        sets = sets.transpose(0, 2, 3, 1, 4, 5)[:, :, :, :, :, None] * eye
        placing.append(sets.reshape(nf, experts * group * CAP, group * tok))
    putting = [spread[i].transpose(0, 2, 1) for i in range(groups)]
    hidden, inv_ffn, moe_in, mixed_all = call(
        functools.partial(out_kernel, nf),
        [shape((tok, dim), F32), shape((tok, LANES), F32)] + [shape((tok, dim), BF)] * 2,
        1.1,
        12,
        ins=[SMEM] + [VMEM] * (3 + nf),
        gate=taking + putting + placing,
    )(frel, x_own, gain_ffn, mixed_rows, *w_o)

    part = blocks * group * CAP
    nrow = part * cores
    tile = 1024

    def tiles(*dims):
        return pl.BlockSpec(dims[:-1] + (tile,), lambda d: (0,) * (len(dims) - 1) + (d,))

    def fixed(array):
        return pl.BlockSpec(array.shape, lambda d: (0,) * array.ndim)

    def take_rows(i, entries, *gate):
        arrays = [a for entry in entries for a in entry]
        parts = call(
            functools.partial(take_kernel, [len(entry) for entry in entries], experts),
            [shape((experts, part, dim), BF)] * cores,
            1.6,
            8,
            grid=(dim // tile,),
            ins=[fixed(taking[i])] + [tiles(*a.shape) for a in arrays],
            out_specs=[tiles(experts, part, dim)] * cores,
            gate=gate,
        )(taking[i], *arrays)
        if cores == 1:
            return parts
        return [parts[0], links.swap(parts[1], 1)]

    plan, plan_rows = links.plane_plan(group * tok)

    def put_rows(i, parts, *gate):
        if cores == 2:
            parts = [parts[0], links.swap(parts[1], 1)]
        return call(
            functools.partial(put_kernel, blocks, cores, plan),
            [shape((n, dim), BF) for n in plan_rows],
            1.6,
            8,
            grid=(dim // tile,),
            ins=[fixed(putting[i])] + [tiles(experts, part, dim)] * cores,
            out_specs=[tiles(n, dim) for n in plan_rows],
            gate=gate,
        )(putting[i], *parts)

    def grouped(pieces):
        return [jnp.concatenate(pieces[i * group : (i + 1) * group]) for i in range(groups)]

    def take_placed(i, whole):
        order = [m for p in range(cores) for m in range(p, nf, cores)]
        sets = placing[i]
        places = jnp.array(order, jnp.int32)
        places = links.f ^ places if links.native else places
        return call(
            take_placed_kernel,
            shape((experts, nrow, dim), BF),
            0.8,
            12,
            spec=pltpu.PrefetchScalarGridSpec(
                num_scalar_prefetch=1,
                grid=(nf,),
                in_specs=[pl.BlockSpec((1,) + sets.shape[1:], lambda m, at: (m, 0, 0))]
                + [pl.BlockSpec((1, group * tok, dim), lambda m, at: (at[m], 0, 0))],
                out_specs=pl.BlockSpec((experts, group * CAP, dim), lambda m, at: (0, m, 0)),
            ),
        )(places, sets, whole)

    g_rows = [[take_placed(i, g)] for i, g in enumerate(g_all)]

    def pick_far(stacked):
        return [pick(stacked, links.c ^ 2), pick(stacked, links.c ^ 3)]

    if links.native:
        near = links.cswap(moe_in, 1)
        far = links.gather(moe_in, near)
        x_begun = [links.plane_start(jnp.concatenate([moe_in, near]))]
        seen, sent = links.plane_end(x_begun[0], g_rows[0][0])
        far = after(far, *seen[3])
        g_far = links.exchange(after(g_copies, far))
        x_begun.append(links.plane_start(jnp.concatenate(pick_far(far))))
        x_rows = [take_rows(0, seen, x_begun[1][0])]
    else:
        x_groups = grouped(links.slots(moe_in))
        x_rows = [take_rows(i, links.plane_end(links.plane_start(x))[0]) for i, x in enumerate(x_groups)]
    w_out_e = w_out.reshape(experts, halves * FH, dim)
    inner_width = halves * FH

    def by_expert(*dims):
        return pl.BlockSpec(dims, lambda j: (j,) + (0,) * (len(dims) - 1))

    dtile = 512
    n = groups * cores
    of_group = [list(range(i * cores, (i + 1) * cores)) for i in range(groups)]

    def grad_out_pieces(inners, g_rows, *gate):
        flat = [a for parts in g_rows for a in parts]
        g_parts, at = [], groups
        for parts in g_rows:
            g_parts.append(list(range(at, at + len(parts))))
            at += len(parts)
        return call(
            functools.partial(
                weight_grad_kernel,
                list(range(groups)),
                g_parts,
            ),
            shape(w_out_e.shape, F32),
            6.5,
            26,
            grid=(experts, halves),
            ins=[pl.BlockSpec((1, nrow, FH), lambda j, h: (j, 0, h))] * groups
            + [pl.BlockSpec((1, g.shape[1], dim), lambda j, h: (j, 0, 0)) for g in flat],
            out_specs=pl.BlockSpec((1, FH, dim), lambda j, h: (j, h, 0)),
            gate=gate,
        )(*inners, *flat)

    def grad_in_pieces(j, total, *gate):
        flat = [a for parts in x_rows for a in parts]
        return call(
            functools.partial(weight_grad_kernel, [n + i for i in range(groups)], of_group),
            shape(w_in.shape, F32),
            6.5,
            25,
            grid=(halves, dim // dtile),
            ins=[pl.BlockSpec((1, part, dtile), lambda p, d: (j, 0, d))] * n
            + [pl.BlockSpec((1, nrow, 2 * FH), lambda p, d: (j * halves + p, 0, 0))] * groups
            + [pl.BlockSpec(memory_space=pl.ANY)] * (j > 0),
            out_specs=pl.BlockSpec((1, dtile, 2 * FH), lambda p, d: (j * halves + p, d, 0)),
            aliases={n + groups: 0} if j else {},
            gate=gate,
        )(*flat, *dprojs, *([total] if j else []))

    def expert(i, *gate):
        rows_in = [by_expert(1, part, dim)] * cores
        return call(
            functools.partial(expert_kernel, halves, cores),
            [shape((experts, part, dim), BF)] * cores
            + [
                shape((pieces, nrow, 2 * FH), BF),
                shape((experts, nrow, inner_width), BF),
                shape((experts, nrow, LANES), F32),
            ],
            34,
            30,
            grid=(experts,),
            ins=[
                SMEM,
                pl.BlockSpec((dim, LANES), lambda j: (0, 0)),
                by_expert(halves, dim, 2 * FH),
                by_expert(1, inner_width, dim),
            ]
            + rows_in
            + [by_expert(1, g.shape[1], dim) for g in g_rows[i]],
            out_specs=rows_in
            + [
                by_expert(halves, nrow, 2 * FH),
                by_expert(1, nrow, inner_width),
                by_expert(1, nrow, LANES),
            ],
            gate=gate,
        )(first_expert.reshape(1), router, w_in, w_out_e, *x_rows[i], *g_rows[i])

    def result(inner, *gate):
        return call(
            result_kernel,
            [shape((experts, part, dim), BF)] * cores,
            3.4,
            14,
            grid=(experts,),
            ins=[by_expert(1, nrow, inner_width), by_expert(1, inner_width, dim)],
            out_specs=[by_expert(1, part, dim)] * cores,
            gate=gate,
        )(inner, w_out_e)

    def cut_group(total):
        return [total[b * tok : (b + 1) * tok] for b in range(group)]

    done, begun, more, totals = [], [], [], []
    last = x_rows[0][0]
    for i in range(groups):
        done.append(expert(i, last))
        if links.native and i == 0:
            pieces_x, sent = links.plane_end(x_begun[1], done[0][0])
            g_begun = links.plane_start(jnp.concatenate(pick_far(after(g_far, *sent))))
            arrays = put_rows(0, done[0][:cores], g_begun[0])
            x_rows.append(take_rows(1, pieces_x, arrays[0]))
            pieces_g, sent = links.plane_end(g_begun, x_rows[1][0])
            arrays = held(arrays, *sent)
            g_rows.append(take_rows(1, pieces_g))
            last = g_rows[1][0]
        elif i == 1:
            more.append(links.reduce_next(begun[0], done[1][0]))
            arrays = put_rows(1, done[1][:cores], *more[0][-2:])
            last = arrays[0]
        else:
            arrays = put_rows(i, done[i][:cores], done[i][0])
            last = arrays[0]
        begun.append(links.reduce_start(arrays))
    dgate = jnp.stack([d[cores + 2][:, :, 0] for d in done], axis=1)
    dgate = dgate.reshape(experts, groups, cores, blocks, group, CAP).transpose(2, 1, 4, 3, 0, 5)
    dgate = dgate.reshape(cores, nc, blocks, experts, CAP, 1)
    dgate_tok = jnp.stack(
        [jnp.sum(s.astype(F32) * d, axis=3) for s, d in zip(slot_sets, dgate)], axis=2
    ).reshape(nc, nf, experts, tok)
    dgate_tok = links.relative(dgate_tok.transpose(1, 0, 2, 3))
    dgate_back = lax.all_to_all(
        dgate_tok.reshape(ndev, experts, tok), ALL, split_axis=0, concat_axis=0, tiled=True
    )
    results, out_arrays, out_begun = [], [], []
    for i in range(groups):
        results.append(result(done[i][cores + 1], last))
        last = results[i][0]
    totals.append(links.reduce_end(more[0], group * tok, last))
    dgate_back = after(dgate_back, results[0][0])
    dprob = jnp.sum(dgate_back.reshape(E, ndev * experts // E, tok), axis=1).T
    dprob = jnp.pad(dprob, ((0, 0), (0, LANES - E)))
    out_arrays.append(put_rows(0, results[0], totals[0], dprob))
    last = out_arrays[0][0]
    for i in range(1, groups):
        more.append(links.reduce_next(begun[i], last))
        last = more[i][-1]
        out_begun.append(links.reduce_start(held(out_arrays[i - 1], last)))
        out_arrays.append(put_rows(i, results[i], last))
        last = out_arrays[i][0]
    dprojs = [d[cores] for d in done]
    inners = [d[cores + 1] for d in done]
    for i in range(1, groups):
        totals.append(links.reduce_end(more[i], group * tok, last))
        last = totals[i]
    dmoe_terms = links.sum_slots([t for total in totals for t in cut_group(total)])
    grad_w_out = grad_out_pieces(inners, g_rows, last)
    out_begun.append(links.reduce_start(held(out_arrays[-1], grad_w_out)))
    dmoe_terms = held(dmoe_terms, grad_w_out)

    back = call(
        functools.partial(hidden_back_kernel, nf, len(dmoe_terms)),
        [shape((tok, dim), F32), shape((dim, LANES), F32), shape((8, dim), F32)]
        + [shape((tok, dim), BF), shape((nc, tok, width), BF)],
        1.3,
        15,
        ins=[SMEM] + [VMEM] * (7 + len(dmoe_terms) + nf),
        scratch=[pltpu.VMEM((tok, dim), BF)],
    )(frel, hidden, inv_ffn, moe_in, g_own, gain_ffn, router, dprob, *dmoe_terms, *w_o)
    dhidden, grad_router, grad_gain_ffn, dlow, dmixed = back
    dmixed = links.exchange(dmixed)
    grad_plan, grad_rows = links.dense_plan(fsdp_rows)

    def dense_terms(left, right, extra, *gate):
        return call(
            functools.partial(place_grad_kernel, nf, grad_plan),
            [shape((r, right.shape[1] + LANES), BF) for r in grad_rows],
            right.shape[0] * right.shape[1] * dim * 2e-9,
            right.shape[1] * dim * 2e-6,
            ins=[SMEM, VMEM, VMEM, VMEM],
            gate=gate,
        )(frel, left, right, extra)

    last = dlow
    out_more = []
    for b in out_begun:
        out_more.append(links.reduce_next(b, last))
        last = out_more[-1][-1]
    grad_w_in = grad_in_pieces(0, None, last)
    last = grad_w_in
    dmixed = after(dmixed, last).reshape(seq, width)

    u, dvalue, stats, dgain = call(
        functools.partial(attend_back_kernel, scale),
        [
            shape((2, seq, width), F32),
            shape((seq, width), BF),
            shape((2, 8, seq), F32),
            shape((2, 8, width), F32),
        ],
        1.4,
        10,
        grid=(heads,),
        ins=[pair_spec, pair_spec, head_spec, whole(2, seq, LANES), gain_spec]
        + table_specs
        + [head_spec],
        out_specs=[
            pair_spec,
            head_spec,
            whole(2, 8, seq),
            pl.BlockSpec((2, 8, HD), lambda h: (0, 0, h)),
        ],
    )(raw, low, value, inv, head_gain, cos, sin, mask, dmixed)
    with_ffn = jnp.where(jnp.arange(LANES) == E, grad_gain_ffn[0][:, None], grad_router)
    grad_o_terms = dense_terms(mixed_all, dlow, with_ffn.astype(BF), stats)
    mean = columns(jnp.sum(links.gather(stats), axis=0)[:, 0] / dim)
    last = grad_o_terms[0]
    out_totals = []
    for m in out_more:
        out_totals.append(links.reduce_end(m, group * tok, last))
        last = out_totals[-1]
    out_terms = links.sum_at_once([t for o in out_totals for t in cut_group(o)])
    mean = after(mean, last)
    dqkv, dnormed_terms, dgain_attn = call(
        functools.partial(dnormed_kernel, nf),
        [shape((seq, 3 * width), BF), shape((seq, dim), BF), shape((8, dim), F32)],
        3.3,
        15,
        ins=[SMEM] + [VMEM] * (6 + nf),
    )(frel, u, raw, inv, mean, dvalue, x_all, *w_qkv)

    def placed(vector):
        return lax.dynamic_update_slice(jnp.zeros((dim,), F32), vector, (links.c * width,))

    grad_o_begun = links.dense_start(grad_o_terms, fsdp_rows, dqkv)
    gain_terms = jnp.stack([dgain_attn[0], placed(dgain[0, 0]), placed(dgain[1, 0])])
    gain_terms = jnp.pad(gain_terms.astype(BF), ((0, LANES - 3), (0, 0))).T
    last = dqkv
    for j in range(1, experts):
        grad_w_in = grad_in_pieces(j, grad_w_in, dqkv, *grad_o_begun[2:3])
        last = grad_w_in
    grad_o_more = links.reduce_next(grad_o_begun, last)
    grad_qkv_terms = dense_terms(normed, dqkv, gain_terms, grad_o_more[-1], out_terms)
    dnormed_terms = after(dnormed_terms.reshape(nc, tok, dim), out_terms)
    grad_qkv_begun = links.dense_start(grad_qkv_terms, fsdp_rows, dnormed_terms)
    dnormed_terms = links.exchange(dnormed_terms)
    grad_o_total = links.reduce_end(grad_o_more, fsdp_rows, grad_qkv_begun[-1])
    grad_qkv_more = links.reduce_next(grad_qkv_begun, grad_o_total)
    grad_o = links.exchange(grad_o_total.reshape(nc, own_rows, -1))
    grad_qkv_total = links.reduce_end(grad_qkv_more, fsdp_rows, grad_o_total)
    dnormed_terms = after(dnormed_terms, grad_qkv_total)
    dnormed = jnp.sum(dnormed_terms.astype(F32), axis=0)
    x_float = x_own.astype(F32)
    x_inv = lax.rsqrt(jnp.mean(x_float * x_float, axis=-1, keepdims=True) + EPS)
    ux = dnormed * gain_attn
    x_mean = jnp.mean(ux * x_float, axis=-1, keepdims=True)
    input_grad = (dhidden + x_inv * ux - x_float * x_inv**3 * x_mean)[None]

    output = (hidden + jnp.sum(out_terms.astype(F32), axis=0)).astype(BF)
    grad_o = jnp.sum(grad_o.astype(F32), axis=0)
    grad_attn_out, router_sum = grad_o[:, :dim], grad_o[:, dim:]
    grad_qkv = links.exchange(grad_qkv_total.reshape(nc, own_rows, -1)).astype(F32)
    gain_sum = jnp.sum(grad_qkv[:, :, 3 * width :], axis=0).T
    grad_dense = grad_qkv[:, :, : 3 * width].reshape(nc, own_rows, 3, width).transpose(2, 1, 0, 3)
    grad_dense = grad_dense.reshape(3, own_rows, dim)
    return (
        output[None],
        input_grad,
        grad_dense[0],
        grad_dense[1],
        grad_dense[2],
        grad_attn_out,
        router_sum[:, :E],
        gain_sum[0],
        gain_sum[1],
        gain_sum[2],
        router_sum[:, E],
        grad_w_in,
        grad_w_out.reshape(w_out.shape),
    )


def solution(mesh):
    rows = P(ALL, None)
    vec = P(ALL)
    cube = P(ALL, None, None)
    stream = P("fsdp", "ctx", None)
    weights = (rows,) * 5 + (vec,) * 4 + (cube,) * 2
    return jax.shard_map(
        shards,
        mesh=mesh,
        in_specs=(stream, P("fsdp", None), stream) + weights + (stream,),
        out_specs=(stream, stream) + weights,
        check_vma=False,
    )
```

```python
import functools
import math

import jax
import jax.numpy as jnp
from jax import lax
from jax.experimental import pallas as pl
from jax.experimental.pallas import tpu as pltpu
from jax.sharding import PartitionSpec as P

H = 16
HD = 128
E = 64
TOP = 8
FH = 512
CAP = 24

EPS = 1e-05
MASKED = -1e30
ROPE_BASE = 10000.0
HIGHEST = lax.Precision.HIGHEST
F32 = jnp.float32
BF = jnp.bfloat16
ALL = ("fsdp", "ctx")
LANES = 128
VMEM_LIMIT = 60 * 1024 * 1024


def pick(stacked, index):
    return lax.dynamic_index_in_dim(stacked, index, 0, keepdims=False)


def after(value, *others):
    return held([value], *others)[0]


def held(values, *others):
    if not others:
        return list(values)
    values = list(values)
    anywhere = pl.BlockSpec(memory_space=pl.ANY)
    done = pl.pallas_call(
        lambda *refs: None,
        out_shape=[jax.ShapeDtypeStruct(v.shape, v.dtype) for v in values],
        in_specs=[anywhere] * (len(values) + len(others)),
        out_specs=[anywhere] * len(values),
        input_output_aliases={i: i for i in range(len(values))},
    )(*values, *others)
    return list(done)


def held_pieces(blocks, *gate):
    flat = held([a for b in blocks for a in b], *gate)
    return [[flat.pop(0) for _ in b] for b in blocks]


def add_low(*terms):
    return sum(t.astype(F32) for t in terms).astype(BF)


class Links:
    def __init__(self, nf, nc):
        self.nf, self.nc = nf, nc
        self.native = nf == 8 and nc == 4
        self.cores = 2 if self.native else 1
        self.f = lax.axis_index("fsdp")
        self.c = lax.axis_index("ctx")
        ms = jnp.arange(nf, dtype=jnp.int32)
        self.frel = self.f ^ ms if self.native else ms

    def swap(self, value, mask):
        return lax.ppermute(value, "fsdp", [(i, i ^ mask) for i in range(self.nf)])

    def cswap(self, value, mask):
        return lax.ppermute(value, "ctx", [(i, i ^ mask) for i in range(self.nc)])

    def exchange(self, value):
        return lax.all_to_all(value, "ctx", split_axis=0, concat_axis=0, tiled=True)

    def gather(self, value, *gate):
        return self.exchange(after(jnp.broadcast_to(value, (self.nc,) + value.shape), *gate))

    def slots(self, value):
        if not self.native:
            whole = lax.all_gather(value, "ctx", axis=0)
            return [whole[k] for k in range(self.nc)]
        return [value] + [self.cswap(value, k) for k in range(1, self.nc)]

    def sum_slots(self, parts):
        if not self.native:
            whole = jnp.stack(parts)
            return [lax.psum_scatter(whole, "ctx", scatter_dimension=0, tiled=False)]
        return [parts[0]] + [self.cswap(parts[k], k) for k in range(1, self.nc)]

    def sum_at_once(self, parts):
        whole = jnp.stack(parts)
        if not self.native:
            return lax.psum_scatter(whole, "ctx", scatter_dimension=0, tiled=True)
        for bit in (1, 2):
            flipped = jnp.stack([whole[k ^ bit] for k in range(self.nc)])
            whole = jnp.where((self.c & bit) > 0, flipped, whole)
        return self.exchange(whole)

    def relative(self, value, planes=False):
        if not self.native:
            return value
        dims = value.shape
        for bit, place in ((4, self.f), (2, self.f), (1, self.f), (2, self.c), (1, self.c)):
            lead = 0 if place is self.f else 1
            if lead and planes:
                continue
            n = dims[lead]
            split = dims[:lead] + (n // (2 * bit), 2, bit) + dims[lead + 1 :]
            cut = value.reshape(split)
            parts = jnp.split(cut, 2, axis=lead + 1)
            flipped = jnp.concatenate(parts[::-1], axis=lead + 1)
            value = jnp.where((place & bit) > 0, flipped, cut).reshape(dims)
        return value

    def plane_start(self, value):
        if not self.native:
            return [value]
        return [value, self.swap(value, 2), self.swap(value, 4)]

    def plane_end(self, begun, *gate):
        if not self.native:
            whole = lax.all_gather(begun[0], "fsdp", axis=0)
            return [[whole[m]] for m in range(self.nf)], begun
        value, from_x, from_y = begun
        half = value.shape[0] // 2
        from_x, from_y = held([from_x, from_y], *gate)
        sent = [from_y[:half], from_x[half:]]
        diag_a = self.swap(sent[0], 2)
        diag_b = self.swap(sent[1], 4)
        return [[value], [from_x], [from_y], [diag_a, diag_b]], sent

    def all_blocks(self, pieces):
        blocks = [b[0] if len(b) == 1 else jnp.concatenate(b) for b in pieces]
        if not self.native:
            return blocks
        return [a for b in blocks for a in (b, self.swap(b, 1))]

    def dense_plan(self, rows):
        if not self.native:
            return [(m, 0, rows, 0, m * rows) for m in range(self.nf)], [self.nf * rows]
        h = rows // 2
        order = [(2, 0), (6, 0), (4, h), (6, h), (4, 0), (2, h), (0, 0), (0, h)]
        entries = []
        for core in (0, 1):
            for place, (m, first) in enumerate(order):
                entries.append((m + core, first, h, core, place * h))
        return entries, [8 * h, 8 * h]

    def dense_start(self, arrays, rows, *gate):
        if not self.native:
            return arrays
        mine, other = arrays
        near = after(self.swap(other, 1), *gate)
        h = rows // 2
        spans = [(0, 2), (2, 2), (4, 1), (5, 1), (6, 2)]
        sums = [
            add_low(mine[a * h : (a + n) * h], near[a * h : (a + n) * h]) for a, n in spans
        ]
        return self.reduce_start(sums)

    def plane_plan(self, rows):
        if not self.native:
            return [(m, 0, rows, 0, m * rows) for m in range(self.nf)], [self.nf * rows]
        h = rows // 2
        entries = [(2, 0, h, 0, 0), (6, 0, h, 0, h), (4, h, h, 1, 0), (6, h, h, 1, h)]
        entries += [(4, 0, h, 2, 0), (2, h, h, 3, 0), (0, 0, rows, 4, 0)]
        return entries, [rows, rows, h, h, rows]

    def reduce_start(self, arrays):
        if not self.native:
            return arrays
        to_x, to_y, rest_y, rest_x, own = arrays
        return [self.swap(to_x, 2), self.swap(to_y, 4), rest_y, rest_x, own]

    def reduce_next(self, begun, *gate):
        if not self.native:
            return begun
        got_x, got_y, rest_y, rest_x, own = begun
        if gate:
            got_x, got_y = held([got_x, got_y], *gate)
        h = rest_y.shape[0]
        last_y = add_low(rest_y, got_x[h:])
        last_x = add_low(rest_x, got_y[h:])
        return [got_x, got_y, self.swap(last_y, 4), self.swap(last_x, 2), own, last_y, last_x]

    def reduce_end(self, begun, rows, *gate):
        if not self.native:
            whole = begun[0].reshape((self.nf, rows) + begun[0].shape[1:])
            return lax.psum_scatter(whole, "fsdp", scatter_dimension=0, tiled=False)
        got_x, got_y, last_y, last_x, own = begun[:5]
        if gate:
            last_y, last_x = held([last_y, last_x], *gate)
        h = rows // 2
        return jnp.concatenate(
            [add_low(own[:h], got_x[:h], last_y), add_low(own[h:], got_y[:h], last_x)]
        )


def mm(a, b):
    return lax.dot_general(a, b, (((1,), (0,)), ((), ())), preferred_element_type=F32)


def mm_nt(a, b):
    return lax.dot_general(a, b, (((1,), (1,)), ((), ())), preferred_element_type=F32)


def mm_tn(a, b):
    return lax.dot_general(a, b, (((0,), (0,)), ((), ())), preferred_element_type=F32)


def call(
    kernel, outs, gflop, mbytes, ins=None, grid=(), out_specs=None, scratch=(), aliases=None, spec=None, gate=()
):
    args = dict(
        out_shape=outs,
        input_output_aliases=aliases or {},
        cost_estimate=pl.CostEstimate(
            flops=int(gflop * 5e7), bytes_accessed=int(mbytes * 5e4), transcendentals=0
        ),
        compiler_params=pltpu.CompilerParams(vmem_limit_bytes=VMEM_LIMIT),
    )
    if spec is not None:
        return pl.pallas_call(kernel, grid_spec=spec, **args)
    given, waits = len(ins), len(gate)

    def body(*refs):
        kernel(*refs[:given], *refs[given + waits :])

    args["scratch_shapes"] = list(scratch)
    args["in_specs"] = list(ins) + [pl.BlockSpec(memory_space=pl.ANY)] * waits
    if grid:
        args["grid"] = grid
    if out_specs is not None:
        args["out_specs"] = out_specs
    made = pl.pallas_call(body, **args)
    return lambda *operands: made(*operands, *gate)


SMEM = pl.BlockSpec(memory_space=pltpu.SMEM)
VMEM = pl.BlockSpec(memory_space=pltpu.VMEM)


def shape(dims, dtype):
    return jax.ShapeDtypeStruct(tuple(dims), dtype)


def qkv_kernel(nf, frel, gain, xs, *refs):
    ws = refs[:nf]
    normed, raw, value, sums = refs[nf:]
    width = value.shape[1]
    block = ws[0].shape[0]
    x = xs[...].astype(F32)
    inv = lax.rsqrt(jnp.mean(x * x, axis=-1, keepdims=True) + EPS)
    normed[...] = (x * inv * gain[...]).astype(BF)
    total = None
    for m in range(nf):
        cols = pl.ds(pl.multiple_of(frel[m] * block, block), block)
        term = mm(normed[:, cols], ws[m][:, : 3 * width])
        total = term if total is None else total + term
    q, k = total[:, :width], total[:, width : 2 * width]
    raw[0] = q
    raw[1] = k
    value[...] = total[:, 2 * width :].astype(BF)
    for i, part in enumerate((q, k)):
        column = jnp.sum(part * part, axis=-1, keepdims=True)
        sums[i] = jnp.broadcast_to(column, (column.shape[0], LANES)).T[:8]


def turn(v, cos, sin):
    half = HD // 2
    other = jnp.concatenate([v[:, half:], v[:, :half]], axis=1)
    return v * cos + other * sin


def attend_kernel(scale, raw, value, inv, gain, cos, sin, mask, low, mixed):
    q = turn(raw[0] * inv[0] * gain[0], cos[...], sin[...]).astype(BF)
    k = turn(raw[1] * inv[1] * gain[1], cos[...], sin[...]).astype(BF)
    low[0] = q
    low[1] = k
    scores = jnp.where(mask[...] > 0, mm_nt(q, k) * scale, MASKED)
    top = jnp.max(scores, axis=-1, keepdims=True)
    e = jnp.exp(scores - top)
    probs = e / jnp.sum(e, axis=-1, keepdims=True)
    mixed[...] = mm(probs.astype(BF), value[...]).astype(BF)


def attend_back_kernel(
    scale, raw, low, value, inv, gain, cos, sin, mask, dmixed, u, dv, stats, dgain
):
    q, k, v = low[0], low[1], value[...]
    scores = jnp.where(mask[...] > 0, mm_nt(q, k) * scale, MASKED)
    top = jnp.max(scores, axis=-1, keepdims=True)
    e = jnp.exp(scores - top)
    probs = e / jnp.sum(e, axis=-1, keepdims=True)
    dm = dmixed[...]
    dprobs = mm_nt(dm, v)
    delta = jnp.sum(probs * dprobs, axis=-1, keepdims=True)
    ds = (probs * (dprobs - delta)).astype(BF)
    dv[...] = mm_tn(probs.astype(BF), dm).astype(BF)
    first = pl.program_id(0) == 0
    for i, grad in enumerate((mm(ds, k) * scale, mm_tn(ds, q) * scale)):
        turned = turn(grad, cos[...], -sin[...])
        ui = turned * gain[i]
        u[i] = ui
        line = jnp.sum(turned * raw[i] * inv[i], axis=0, keepdims=True)
        dgain[i] = jnp.broadcast_to(line, (8, line.shape[1]))
        column = jnp.sum(ui * raw[i], axis=-1, keepdims=True)
        flat = jnp.broadcast_to(column, (column.shape[0], LANES)).T[:8]
        stats[i] = jnp.where(first, flat, stats[i] + flat)


def out_kernel(nf, frel, x, gain, mixed, *refs):
    ws = refs[:nf]
    hidden, inv_out, moe, rows = refs[nf:]
    width = mixed.shape[2]
    block = ws[0].shape[0]
    for k in range(mixed.shape[0]):
        rows[:, k * width : (k + 1) * width] = mixed[k]
    total = x[...].astype(F32)
    for m in range(nf):
        cols = pl.ds(pl.multiple_of(frel[m] * block, block), block)
        total = total + mm(rows[:, cols], ws[m][...])
    hidden[...] = total
    inv = lax.rsqrt(jnp.mean(total * total, axis=-1, keepdims=True) + EPS)
    inv_out[...] = jnp.broadcast_to(inv, inv_out.shape)
    moe[...] = (total * inv * gain[...]).astype(BF)


def hidden_back_kernel(nf, nt, frel, hidden, inv_in, moe, g, gain, router, dprob, *refs):
    terms, ws = refs[:nt], refs[nt : nt + nf]
    dhidden, drouter, dgain, low_rows, dmixed, mix_rows = refs[nt + nf :]
    width = dmixed.shape[2]
    block = ws[0].shape[0]
    logits = mm(moe[...], router[...])
    lane = lax.broadcasted_iota(jnp.int32, logits.shape, 1)
    logits = jnp.where(lane < E, logits, MASKED)
    e = jnp.exp(logits - jnp.max(logits, axis=-1, keepdims=True))
    probs = e / jnp.sum(e, axis=-1, keepdims=True)
    dp = dprob[...]
    dlogits = probs * (dp - jnp.sum(probs * dp, axis=-1, keepdims=True))
    high = dlogits.astype(BF)
    rest = (dlogits - high.astype(F32)).astype(BF)
    drouter[...] = mm_tn(moe[...], high) + mm_tn(moe[...], rest)
    dmoe = mm_nt(high, router[...]) + mm_nt(rest, router[...])
    for term in terms:
        dmoe = dmoe + term[...].astype(F32)
    hid = hidden[...]
    inv = inv_in[:, :1]
    u = dmoe * gain[...]
    mean = jnp.mean(u * hid, axis=-1, keepdims=True)
    line = jnp.sum(dmoe * hid * inv, axis=0, keepdims=True)
    dgain[...] = jnp.broadcast_to(line, dgain.shape)
    dh = g[...].astype(F32) + inv * u - hid * (inv * inv * inv) * mean
    dhidden[...] = dh
    low_rows[...] = dh.astype(BF)
    for m in range(nf):
        cols = pl.ds(pl.multiple_of(frel[m] * block, block), block)
        mix_rows[:, cols] = mm_nt(low_rows[...], ws[m][...]).astype(BF)
    for k in range(dmixed.shape[0]):
        dmixed[k] = mix_rows[:, k * width : (k + 1) * width]


def dnormed_kernel(nf, frel, u, raw, inv, mean, dv, x, *refs):
    ws = refs[:nf]
    dqkv, total, line = refs[nf:]
    width = dv.shape[1]
    block = ws[0].shape[0]
    for i in range(2):
        r = inv[i][:, :1]
        b = mean[i][:, :1]
        dqkv[:, i * width : (i + 1) * width] = (r * u[i] - raw[i] * (r * r * r * b)).astype(BF)
    dqkv[:, 2 * width :] = dv[...]
    for m in range(nf):
        cols = pl.ds(pl.multiple_of(frel[m] * block, block), block)
        total[:, cols] = mm_nt(dqkv[...], ws[m][:, : 3 * width]).astype(BF)
    xf = x[...].astype(F32)
    x_inv = lax.rsqrt(jnp.mean(xf * xf, axis=-1, keepdims=True) + EPS)
    terms = jnp.sum(total[...].astype(F32) * xf * x_inv, axis=0, keepdims=True)
    line[...] = jnp.broadcast_to(terms, line.shape)


def place(plan, outs, blocks):
    for m, first, count, which, row in plan:
        outs[which][row : row + count, :] = blocks[m][first : first + count, :]


def place_grad_kernel(nf, plan, frel, left, right, extra, *outs):
    block = left.shape[1] // nf
    for m in range(nf):
        cols = pl.ds(pl.multiple_of(frel[m] * block, block), block)
        term = mm_tn(left[:, cols], right[...]).astype(BF)
        term = jnp.concatenate([term, extra[cols, :]], axis=1)
        place([p for p in plan if p[0] == m], outs, {m: term})


def take_kernel(sizes, experts, slots, *refs):
    cores = slots.shape[1] // (experts * 2 * CAP)
    xs, outs = refs[:-cores], refs[-cores:]
    two = 2 * CAP
    at = 0
    for m, size in enumerate(sizes):
        rows = [r[...] for r in xs[at : at + size]]
        at += size
        got = mm(slots[m], rows[0] if size == 1 else jnp.concatenate(rows, axis=0)).astype(BF)
        for e in range(experts * cores):
            outs[e // experts][e % experts, m * two : (m + 1) * two, :] = got[e * two : (e + 1) * two]


def take_placed_kernel(places, slots, x, out):
    del places
    got = mm(slots[0], x[0]).astype(BF)
    count = got.shape[0] // out.shape[0]
    for e in range(out.shape[0]):
        out[e] = got[e * count : (e + 1) * count]


def put_kernel(blocks, step, plan, slots, *refs):
    cores = step
    rows, outs = refs[:cores], refs[cores:]
    two = 2 * CAP
    for m in range(blocks):
        cut = [
            part[j, m * two : (m + 1) * two, :] for part in rows for j in range(part.shape[0])
        ]
        low = mm(slots[m], jnp.concatenate(cut, axis=0)).astype(BF)
        place([p for p in plan if p[0] == m * step], outs, {m * step: low})


def expert_kernel(halves, cores, first, router, w_in, w_out, *refs):
    xs, gs = refs[:cores], refs[cores : -3 - cores]
    dslots = refs[-3 - cores : -3]
    dproj, inner_out, dgate = refs[-3:]
    xr = jnp.concatenate([r[0] for r in xs], axis=0)
    gr = jnp.concatenate([r[0] for r in gs], axis=0)
    logits = mm(xr, router[...])
    lane = lax.broadcasted_iota(jnp.int32, logits.shape, 1)
    logits = jnp.where(lane < E, logits, MASKED)
    e = jnp.exp(logits - jnp.max(logits, axis=-1, keepdims=True))
    mine = first[0] + pl.program_id(0)
    chosen = jnp.sum(jnp.where(lane == mine, e, 0.0), axis=-1, keepdims=True)
    gate = chosen / jnp.sum(e, axis=-1, keepdims=True)
    back = mm_nt(gr, w_out[0])
    dg = 0.0
    ds = 0.0
    for h in range(halves):
        projected = mm(xr, w_in[h])
        a, up = projected[:, :FH], projected[:, FH:]
        sig = jax.nn.sigmoid(a)
        act = a * sig
        inner = act * up
        b = back[:, h * FH : (h + 1) * FH]
        dg = dg + jnp.sum(inner * b, axis=-1, keepdims=True)
        inner_out[0, :, h * FH : (h + 1) * FH] = (inner * gate).astype(BF)
        db = b * gate
        dproj[h, :, :FH] = (db * up * (sig * (1.0 + a * (1.0 - sig)))).astype(BF)
        dproj[h, :, FH:] = (db * act).astype(BF)
        ds = ds + mm_nt(dproj[h], w_in[h])
    low = ds.astype(BF)
    count = dslots[0].shape[1]
    for i in range(cores):
        dslots[i][0] = low[i * count : (i + 1) * count]
    dgate[0] = jnp.broadcast_to(dg, dgate.shape[1:])


def result_kernel(inner, w_out, *outs):
    low = mm(inner[0], w_out[0]).astype(BF)
    count = outs[0].shape[1]
    for i, out in enumerate(outs):
        out[0] = low[i * count : (i + 1) * count]


def weight_grad_kernel(whole, parts, *refs):
    total = None
    for w, ps in zip(whole, parts):
        at = 0
        for p in ps:
            n = refs[p].shape[1]
            term = (refs[w][0, at : at + n, :], refs[p][0])
            at += n
            term = mm_tn(term[1], term[0]) if w > p else mm_tn(term[0], term[1])
            total = term if total is None else total + term
    refs[-1][0] = total


def rotary_tables(positions):
    half = HD // 2
    frequency = ROPE_BASE ** (-(jnp.arange(half, dtype=F32) * 2.0 / HD))
    angles = positions.astype(F32)[:, None] * frequency[None, :]
    cos, sin = jnp.cos(angles), jnp.sin(angles)
    return jnp.concatenate([cos, cos], axis=1), jnp.concatenate([-sin, sin], axis=1)


def shards(
    tokens,
    doc_starts,
    expert_ids,
    w_query,
    w_key,
    w_value,
    w_attn_out,
    w_router,
    g_attn,
    g_query,
    g_key,
    g_ffn,
    w_in,
    w_out,
    cotangent,
):
    nf, nc = lax.axis_size("fsdp"), lax.axis_size("ctx")
    ndev = nf * nc
    links = Links(nf, nc)
    frel = links.frel
    x_own, g_own = tokens[0], cotangent[0]
    tok, dim = x_own.shape
    seq = tok * nc
    width = dim // nc
    heads = H // nc
    own_rows = w_query.shape[0]
    fsdp_rows = own_rows * nc
    starts = doc_starts[0]

    by_cols = [w.reshape(own_rows, nc, width) for w in (w_query, w_key, w_value)]
    by_cols = jnp.concatenate(by_cols, axis=2).transpose(1, 0, 2)
    per_row = tok * TOP // own_rows
    small_width = -(-(E + 4 + per_row) // LANES) * LANES
    small = [w_router] + [g[:, None] for g in (g_attn, g_query, g_key, g_ffn)]
    small += [expert_ids[0].T.reshape(own_rows, per_row).astype(BF)]
    small += [jnp.zeros((own_rows, small_width - E - 4 - per_row), BF)]
    x_copies = jnp.broadcast_to(x_own, (nc,) + x_own.shape)
    g_copies = jnp.broadcast_to(g_own, (nc,) + g_own.shape)
    to_all = jnp.concatenate([w_attn_out] + small, axis=1)
    to_all = jnp.broadcast_to(to_all, (nc,) + to_all.shape)
    got = links.exchange(jnp.concatenate([by_cols, to_all], axis=2)).reshape(fsdp_rows, -1)
    cols_o = 3 * width + dim
    qkv_rows = jnp.concatenate([got[:, : 3 * width], got[:, cols_o:]], axis=1)
    w_o_rows = got[:, 3 * width : cols_o]
    qkv_begun = links.plane_start(qkv_rows)
    x_sent = after(x_copies, got)
    w_qkv = links.all_blocks(links.plane_end(qkv_begun, x_sent)[0])
    group = 2
    groups = nc // group
    x_all = links.exchange(x_sent).reshape(seq, dim)
    w_o_begun = links.plane_start(after(w_o_rows, w_qkv[-1]))
    w_o_pieces, w_o_sent = links.plane_end(w_o_begun)
    small_all = jnp.stack([w[:, 3 * width :] for w in w_qkv])
    small_all = small_all.reshape(nf, nc, own_rows, small_width)
    small_all = links.relative(small_all, planes=True).reshape(dim, small_width)
    router = jnp.where(jnp.arange(LANES) < E, small_all[:, :LANES], 0)
    gains = small_all[:, E : E + 4].T.reshape(4, 1, dim).astype(F32)
    gain_attn, gain_query, gain_key, gain_ffn = gains
    ids_all = small_all[:, E + 4 : E + 4 + per_row].astype(jnp.int32)
    ids_all = ids_all.reshape(nf, nc, TOP, tok)

    positions = jnp.arange(seq, dtype=jnp.int32)
    cos, sin = rotary_tables(positions)
    docs = jnp.sum((starts[None, :] <= positions[:, None]).astype(jnp.int32), axis=1)
    allowed = (positions[None, :] <= positions[:, None]) & (docs[None, :] == docs[:, None])
    mask = allowed.astype(F32)
    normed, raw, value, sums = call(
        functools.partial(qkv_kernel, nf),
        [
            shape((seq, dim), BF),
            shape((2, seq, width), F32),
            shape((seq, width), BF),
            shape((2, 8, seq), F32),
        ],
        3.2,
        13,
        ins=[SMEM] + [VMEM] * (2 + nf),
        gate=w_o_sent + [mask, cos, sin],
    )(frel, gain_attn, x_all, *w_qkv)

    w_o = links.all_blocks(w_o_pieces)
    if links.native:
        g_one = links.cswap(after(g_own, w_qkv[-1]), 1)
        g_groups = [jnp.concatenate([g_own, after(g_one, sums)])]
    else:
        g_groups = links.slots(g_own)
        g_groups = [jnp.concatenate(g_groups[i * group : (i + 1) * group]) for i in range(groups)]
    g_all = [lax.all_gather(g, "fsdp", axis=0) for g in g_groups]

    def columns(flat):
        return jnp.broadcast_to(flat[:, :, None], (2, seq, LANES))

    sums = jnp.sum(links.gather(sums), axis=0)[:, 0]
    inv = columns(lax.rsqrt(sums / dim + EPS))
    head_gain = jnp.stack([gain_query, gain_key]).reshape(2, nc, 1, width)
    head_gain = lax.dynamic_index_in_dim(head_gain, links.c, 1, keepdims=False)
    scale = 1.0 / math.sqrt(HD)

    def whole(*dims):
        return pl.BlockSpec(dims, lambda h: (0,) * len(dims))

    pair_spec = pl.BlockSpec((2, seq, HD), lambda h: (0, 0, h))
    head_spec = pl.BlockSpec((seq, HD), lambda h: (0, h))
    gain_spec = pl.BlockSpec((2, 1, HD), lambda h: (0, 0, h))
    table_specs = [whole(seq, HD), whole(seq, HD), whole(seq, seq)]
    low, mixed = call(
        functools.partial(attend_kernel, scale),
        [shape((2, seq, width), BF), shape((seq, width), BF)],
        0.6,
        7,
        grid=(heads,),
        ins=[pair_spec, head_spec, whole(2, seq, LANES), gain_spec] + table_specs,
        out_specs=[pair_spec, head_spec],
    )(raw, value, inv, head_gain, cos, sin, mask)
    mixed_rows = links.exchange(mixed.reshape(nc, tok, width))
    pieces = w_in.shape[0]
    halves = min(2, pieces)
    experts = pieces // halves
    device = links.f * nc + links.c
    first_expert = device * pieces // 2
    cores = links.cores
    mine = first_expert + jnp.arange(experts, dtype=jnp.int32)
    theirs = ((links.f ^ 1) * nc + links.c) * pieces // 2 + jnp.arange(experts, dtype=jnp.int32)
    both = jnp.concatenate([mine, theirs]) if cores == 2 else mine
    ids_rel = links.relative(after(ids_all, mixed)).transpose(1, 0, 2, 3)
    before = (jnp.arange(tok)[:, None] < jnp.arange(tok)[None, :]).astype(BF)
    ranks = jnp.arange(CAP, dtype=F32)[:, None]

    def slots_of(ids, names):
        named = jnp.any(ids[:, :, None] == names[:, None, None], axis=3)
        rank = jnp.einsum("kmet,ts->kmes", named.astype(BF), before, preferred_element_type=F32)
        return (named[:, :, :, None] & (rank[:, :, :, None] == ranks)).astype(BF)

    blocks = nf // cores
    slots = slots_of(ids_rel[:, ::cores], both)
    slot_sets = [slots[:, :, :experts]]
    if cores == 2:
        slot_sets.append(slots_of(ids_rel[:, 1::2], mine))
    rows_all = experts * cores * group * CAP
    eye = jnp.eye(group, dtype=BF)[:, None, :, None]
    spread = slots.reshape(groups, group, blocks, experts * cores, CAP, tok)
    spread = spread.transpose(0, 2, 3, 1, 4, 5)[:, :, :, :, :, None] * eye
    spread = spread.reshape(groups, blocks, rows_all, group * tok)
    taking = [spread[i] for i in range(groups)]
    placing = []
    for i in range(groups if cores == 1 else 1):
        sets = jnp.stack([s[i * group : (i + 1) * group] for s in slot_sets])
        sets = sets.transpose(0, 2, 3, 1, 4, 5)[:, :, :, :, :, None] * eye
        placing.append(sets.reshape(nf, experts * group * CAP, group * tok))
    putting = [spread[i].transpose(0, 2, 1) for i in range(groups)]
    hidden, inv_ffn, moe_in, mixed_all = call(
        functools.partial(out_kernel, nf),
        [shape((tok, dim), F32), shape((tok, LANES), F32)] + [shape((tok, dim), BF)] * 2,
        1.1,
        12,
        ins=[SMEM] + [VMEM] * (3 + nf),
        gate=taking + putting + placing,
    )(frel, x_own, gain_ffn, mixed_rows, *w_o)

    part = blocks * group * CAP
    nrow = part * cores
    tile = 1024

    def tiles(*dims):
        return pl.BlockSpec(dims[:-1] + (tile,), lambda d: (0,) * (len(dims) - 1) + (d,))

    def fixed(array):
        return pl.BlockSpec(array.shape, lambda d: (0,) * array.ndim)

    def take_rows(i, entries, *gate):
        arrays = [a for entry in entries for a in entry]
        parts = call(
            functools.partial(take_kernel, [len(entry) for entry in entries], experts),
            [shape((experts, part, dim), BF)] * cores,
            1.6,
            8,
            grid=(dim // tile,),
            ins=[fixed(taking[i])] + [tiles(*a.shape) for a in arrays],
            out_specs=[tiles(experts, part, dim)] * cores,
            gate=gate,
        )(taking[i], *arrays)
        if cores == 1:
            return parts
        return [parts[0], links.swap(parts[1], 1)]

    plan, plan_rows = links.plane_plan(group * tok)

    def put_rows(i, parts, *gate):
        if cores == 2:
            parts = [parts[0], links.swap(parts[1], 1)]
        return call(
            functools.partial(put_kernel, blocks, cores, plan),
            [shape((n, dim), BF) for n in plan_rows],
            1.6,
            8,
            grid=(dim // tile,),
            ins=[fixed(putting[i])] + [tiles(experts, part, dim)] * cores,
            out_specs=[tiles(n, dim) for n in plan_rows],
            gate=gate,
        )(putting[i], *parts)

    def grouped(pieces):
        return [jnp.concatenate(pieces[i * group : (i + 1) * group]) for i in range(groups)]

    def take_placed(i, whole):
        order = [m for p in range(cores) for m in range(p, nf, cores)]
        sets = placing[i]
        places = jnp.array(order, jnp.int32)
        places = links.f ^ places if links.native else places
        return call(
            take_placed_kernel,
            shape((experts, nrow, dim), BF),
            0.8,
            12,
            spec=pltpu.PrefetchScalarGridSpec(
                num_scalar_prefetch=1,
                grid=(nf,),
                in_specs=[pl.BlockSpec((1,) + sets.shape[1:], lambda m, at: (m, 0, 0))]
                + [pl.BlockSpec((1, group * tok, dim), lambda m, at: (at[m], 0, 0))],
                out_specs=pl.BlockSpec((experts, group * CAP, dim), lambda m, at: (0, m, 0)),
            ),
        )(places, sets, whole)

    g_rows = [[take_placed(i, g)] for i, g in enumerate(g_all)]

    def pick_far(stacked):
        return [pick(stacked, links.c ^ 2), pick(stacked, links.c ^ 3)]

    if links.native:
        near = links.cswap(moe_in, 1)
        far = links.gather(moe_in, near)
        x_begun = [links.plane_start(jnp.concatenate([moe_in, near]))]
        seen, sent = links.plane_end(x_begun[0], g_rows[0][0])
        far = after(far, *seen[3])
        g_far = links.exchange(after(g_copies, far))
        x_begun.append(links.plane_start(jnp.concatenate(pick_far(far))))
        x_rows = [take_rows(0, seen, x_begun[1][0])]
    else:
        x_groups = grouped(links.slots(moe_in))
        x_rows = [take_rows(i, links.plane_end(links.plane_start(x))[0]) for i, x in enumerate(x_groups)]
    w_out_e = w_out.reshape(experts, halves * FH, dim)
    inner_width = halves * FH

    def by_expert(*dims):
        return pl.BlockSpec(dims, lambda j: (j,) + (0,) * (len(dims) - 1))

    dtile = 512
    n = groups * cores
    of_group = [list(range(i * cores, (i + 1) * cores)) for i in range(groups)]

    def grad_out_pieces(inners, g_rows, *gate):
        flat = [a for parts in g_rows for a in parts]
        g_parts, at = [], groups
        for parts in g_rows:
            g_parts.append(list(range(at, at + len(parts))))
            at += len(parts)
        return call(
            functools.partial(
                weight_grad_kernel,
                list(range(groups)),
                g_parts,
            ),
            shape(w_out_e.shape, F32),
            6.5,
            26,
            grid=(experts, halves),
            ins=[pl.BlockSpec((1, nrow, FH), lambda j, h: (j, 0, h))] * groups
            + [pl.BlockSpec((1, g.shape[1], dim), lambda j, h: (j, 0, 0)) for g in flat],
            out_specs=pl.BlockSpec((1, FH, dim), lambda j, h: (j, h, 0)),
            gate=gate,
        )(*inners, *flat)

    def grad_in_pieces(j, total, *gate):
        flat = [a for parts in x_rows for a in parts]
        return call(
            functools.partial(weight_grad_kernel, [n + i for i in range(groups)], of_group),
            shape(w_in.shape, F32),
            6.5,
            25,
            grid=(halves, dim // dtile),
            ins=[pl.BlockSpec((1, part, dtile), lambda p, d: (j, 0, d))] * n
            + [pl.BlockSpec((1, nrow, 2 * FH), lambda p, d: (j * halves + p, 0, 0))] * groups
            + [pl.BlockSpec(memory_space=pl.ANY)] * (j > 0),
            out_specs=pl.BlockSpec((1, dtile, 2 * FH), lambda p, d: (j * halves + p, d, 0)),
            aliases={n + groups: 0} if j else {},
            gate=gate,
        )(*flat, *dprojs, *([total] if j else []))

    def expert(i, *gate):
        rows_in = [by_expert(1, part, dim)] * cores
        return call(
            functools.partial(expert_kernel, halves, cores),
            [shape((experts, part, dim), BF)] * cores
            + [
                shape((pieces, nrow, 2 * FH), BF),
                shape((experts, nrow, inner_width), BF),
                shape((experts, nrow, LANES), F32),
            ],
            34,
            30,
            grid=(experts,),
            ins=[
                SMEM,
                pl.BlockSpec((dim, LANES), lambda j: (0, 0)),
                by_expert(halves, dim, 2 * FH),
                by_expert(1, inner_width, dim),
            ]
            + rows_in
            + [by_expert(1, g.shape[1], dim) for g in g_rows[i]],
            out_specs=rows_in
            + [
                by_expert(halves, nrow, 2 * FH),
                by_expert(1, nrow, inner_width),
                by_expert(1, nrow, LANES),
            ],
            gate=gate,
        )(first_expert.reshape(1), router, w_in, w_out_e, *x_rows[i], *g_rows[i])

    def result(inner, *gate):
        return call(
            result_kernel,
            [shape((experts, part, dim), BF)] * cores,
            3.4,
            14,
            grid=(experts,),
            ins=[by_expert(1, nrow, inner_width), by_expert(1, inner_width, dim)],
            out_specs=[by_expert(1, part, dim)] * cores,
            gate=gate,
        )(inner, w_out_e)

    def cut_group(total):
        return [total[b * tok : (b + 1) * tok] for b in range(group)]

    done, begun, more, totals = [], [], [], []
    last = x_rows[0][0]
    for i in range(groups):
        done.append(expert(i, last))
        if links.native and i == 0:
            pieces_x, sent = links.plane_end(x_begun[1], done[0][0])
            g_begun = links.plane_start(jnp.concatenate(pick_far(after(g_far, *sent))))
            arrays = put_rows(0, done[0][:cores], g_begun[0])
            x_rows.append(take_rows(1, pieces_x, arrays[0]))
            pieces_g, sent = links.plane_end(g_begun, x_rows[1][0])
            arrays = held(arrays, *sent)
            g_rows.append(take_rows(1, pieces_g))
            last = g_rows[1][0]
        elif i == 1:
            more.append(links.reduce_next(begun[0], done[1][0]))
            arrays = put_rows(1, done[1][:cores], *more[0][-2:])
            last = arrays[0]
        else:
            arrays = put_rows(i, done[i][:cores], done[i][0])
            last = arrays[0]
        begun.append(links.reduce_start(arrays))
    dgate = jnp.stack([d[cores + 2][:, :, 0] for d in done], axis=1)
    dgate = dgate.reshape(experts, groups, cores, blocks, group, CAP).transpose(2, 1, 4, 3, 0, 5)
    dgate = dgate.reshape(cores, nc, blocks, experts, CAP, 1)
    dgate_tok = jnp.stack(
        [jnp.sum(s.astype(F32) * d, axis=3) for s, d in zip(slot_sets, dgate)], axis=2
    ).reshape(nc, nf, experts, tok)
    dgate_tok = links.relative(dgate_tok.transpose(1, 0, 2, 3))
    dgate_back = lax.all_to_all(
        dgate_tok.reshape(ndev, experts, tok), ALL, split_axis=0, concat_axis=0, tiled=True
    )
    results, out_arrays, out_begun = [], [], []
    for i in range(groups):
        results.append(result(done[i][cores + 1], last))
        last = results[i][0]
    totals.append(links.reduce_end(more[0], group * tok, last))
    dgate_back = after(dgate_back, results[0][0])
    dprob = jnp.sum(dgate_back.reshape(E, ndev * experts // E, tok), axis=1).T
    dprob = jnp.pad(dprob, ((0, 0), (0, LANES - E)))
    out_arrays.append(put_rows(0, results[0], totals[0], dprob))
    last = out_arrays[0][0]
    for i in range(1, groups):
        more.append(links.reduce_next(begun[i], last))
        last = more[i][-1]
        out_begun.append(links.reduce_start(held(out_arrays[i - 1], last)))
        out_arrays.append(put_rows(i, results[i], last))
        last = out_arrays[i][0]
    dprojs = [d[cores] for d in done]
    inners = [d[cores + 1] for d in done]
    for i in range(1, groups):
        totals.append(links.reduce_end(more[i], group * tok, last))
        last = totals[i]
    dmoe_terms = links.sum_slots([t for total in totals for t in cut_group(total)])
    grad_w_out = grad_out_pieces(inners, g_rows, last)
    out_begun.append(links.reduce_start(held(out_arrays[-1], grad_w_out)))
    dmoe_terms = held(dmoe_terms, grad_w_out)

    back = call(
        functools.partial(hidden_back_kernel, nf, len(dmoe_terms)),
        [shape((tok, dim), F32), shape((dim, LANES), F32), shape((8, dim), F32)]
        + [shape((tok, dim), BF), shape((nc, tok, width), BF)],
        1.3,
        15,
        ins=[SMEM] + [VMEM] * (7 + len(dmoe_terms) + nf),
        scratch=[pltpu.VMEM((tok, dim), BF)],
    )(frel, hidden, inv_ffn, moe_in, g_own, gain_ffn, router, dprob, *dmoe_terms, *w_o)
    dhidden, grad_router, grad_gain_ffn, dlow, dmixed = back
    dmixed = links.exchange(dmixed)
    grad_plan, grad_rows = links.dense_plan(fsdp_rows)

    def dense_terms(left, right, extra, *gate):
        return call(
            functools.partial(place_grad_kernel, nf, grad_plan),
            [shape((r, right.shape[1] + LANES), BF) for r in grad_rows],
            right.shape[0] * right.shape[1] * dim * 2e-9,
            right.shape[1] * dim * 2e-6,
            ins=[SMEM, VMEM, VMEM, VMEM],
            gate=gate,
        )(frel, left, right, extra)

    last = dlow
    out_more = []
    for b in out_begun:
        out_more.append(links.reduce_next(b, last))
        last = out_more[-1][-1]
    grad_w_in = grad_in_pieces(0, None, last)
    last = grad_w_in
    dmixed = after(dmixed, last).reshape(seq, width)

    u, dvalue, stats, dgain = call(
        functools.partial(attend_back_kernel, scale),
        [
            shape((2, seq, width), F32),
            shape((seq, width), BF),
            shape((2, 8, seq), F32),
            shape((2, 8, width), F32),
        ],
        1.4,
        10,
        grid=(heads,),
        ins=[pair_spec, pair_spec, head_spec, whole(2, seq, LANES), gain_spec]
        + table_specs
        + [head_spec],
        out_specs=[
            pair_spec,
            head_spec,
            whole(2, 8, seq),
            pl.BlockSpec((2, 8, HD), lambda h: (0, 0, h)),
        ],
    )(raw, low, value, inv, head_gain, cos, sin, mask, dmixed)
    with_ffn = jnp.where(jnp.arange(LANES) == E, grad_gain_ffn[0][:, None], grad_router)
    grad_o_terms = dense_terms(mixed_all, dlow, with_ffn.astype(BF), stats)
    mean = columns(jnp.sum(links.gather(stats), axis=0)[:, 0] / dim)
    last = grad_o_terms[0]
    out_totals = []
    for m in out_more:
        out_totals.append(links.reduce_end(m, group * tok, last))
        last = out_totals[-1]
    out_terms = links.sum_at_once([t for o in out_totals for t in cut_group(o)])
    mean = after(mean, last)
    dqkv, dnormed_terms, dgain_attn = call(
        functools.partial(dnormed_kernel, nf),
        [shape((seq, 3 * width), BF), shape((seq, dim), BF), shape((8, dim), F32)],
        3.3,
        15,
        ins=[SMEM] + [VMEM] * (6 + nf),
    )(frel, u, raw, inv, mean, dvalue, x_all, *w_qkv)

    def placed(vector):
        return lax.dynamic_update_slice(jnp.zeros((dim,), F32), vector, (links.c * width,))

    grad_o_begun = links.dense_start(grad_o_terms, fsdp_rows, dqkv)
    gain_terms = jnp.stack([dgain_attn[0], placed(dgain[0, 0]), placed(dgain[1, 0])])
    gain_terms = jnp.pad(gain_terms.astype(BF), ((0, LANES - 3), (0, 0))).T
    last = dqkv
    for j in range(1, experts):
        grad_w_in = grad_in_pieces(j, grad_w_in, dqkv, *grad_o_begun[2:3])
        last = grad_w_in
    grad_o_more = links.reduce_next(grad_o_begun, last)
    dnormed_terms = after(dnormed_terms.reshape(nc, tok, dim), out_terms, grad_o_more[-1])
    grad_qkv_terms = dense_terms(normed, dqkv, gain_terms, dnormed_terms)
    grad_qkv_begun = links.dense_start(grad_qkv_terms, fsdp_rows, grad_qkv_terms[0])
    dnormed_terms = links.exchange(dnormed_terms)
    grad_o_total = links.reduce_end(grad_o_more, fsdp_rows, grad_qkv_begun[-1])
    grad_qkv_more = links.reduce_next(grad_qkv_begun, grad_o_total)
    grad_o = links.exchange(grad_o_total.reshape(nc, own_rows, -1))
    grad_qkv_total = links.reduce_end(grad_qkv_more, fsdp_rows, grad_o_total)
    dnormed_terms = after(dnormed_terms, grad_qkv_total)
    dnormed = jnp.sum(dnormed_terms.astype(F32), axis=0)
    x_float = x_own.astype(F32)
    x_inv = lax.rsqrt(jnp.mean(x_float * x_float, axis=-1, keepdims=True) + EPS)
    ux = dnormed * gain_attn
    x_mean = jnp.mean(ux * x_float, axis=-1, keepdims=True)
    input_grad = (dhidden + x_inv * ux - x_float * x_inv**3 * x_mean)[None]

    output = (hidden + jnp.sum(out_terms.astype(F32), axis=0)).astype(BF)
    grad_o = jnp.sum(grad_o.astype(F32), axis=0)
    grad_attn_out, router_sum = grad_o[:, :dim], grad_o[:, dim:]
    grad_qkv = links.exchange(grad_qkv_total.reshape(nc, own_rows, -1)).astype(F32)
    gain_sum = jnp.sum(grad_qkv[:, :, 3 * width :], axis=0).T
    grad_dense = grad_qkv[:, :, : 3 * width].reshape(nc, own_rows, 3, width).transpose(2, 1, 0, 3)
    grad_dense = grad_dense.reshape(3, own_rows, dim)
    return (
        output[None],
        input_grad,
        grad_dense[0],
        grad_dense[1],
        grad_dense[2],
        grad_attn_out,
        router_sum[:, :E],
        gain_sum[0],
        gain_sum[1],
        gain_sum[2],
        router_sum[:, E],
        grad_w_in,
        grad_w_out.reshape(w_out.shape),
    )


def solution(mesh):
    rows = P(ALL, None)
    vec = P(ALL)
    cube = P(ALL, None, None)
    stream = P("fsdp", "ctx", None)
    weights = (rows,) * 5 + (vec,) * 4 + (cube,) * 2
    return jax.shard_map(
        shards,
        mesh=mesh,
        in_specs=(stream, P("fsdp", None), stream) + weights + (stream,),
        out_specs=(stream, stream) + weights,
        check_vma=False,
    )
```
